256 devices in a mesh: rot: 16 (over x, y_hi, core), az: 16 (over y_lo, z).
Axes of the slice: x: 4, y: 4 (y_hi: 2, y_lo: 2; y = y_hi * 2 + y_lo), z: 8, core: 2. Of those that a mesh axis runs over, the one named last changes fastest.
Arguments:
- inputs: bfloat16 [16, 4, 512, 128], P('rot', None, 'az'), may hold values from -6 to 6
- pre_one: bfloat16 [16, 4, 512, 128], P('rot', None, 'az'), may hold values from -8 to 8
- pre_two: bfloat16 [16, 4, 512, 128], P('rot', None, 'az'), may hold values from -8 to 8
- cotangent: bfloat16 [16, 4, 512, 128], P('rot', None, 'az'), may hold values from -6 to 6
- filt_one: bfloat16 [16, 3, 3, 128, 128], P('rot'), may hold values from -0.046875 to 0.046875
- filt_two: bfloat16 [16, 3, 3, 128, 128], P('rot'), may hold values from -0.046875 to 0.046875
Outputs:
- input_grad: bfloat16 [16, 4, 512, 128], P('rot', None, 'az')
- filt_grad_one: float32 [16, 3, 3, 128, 128], P('rot')
- filt_grad_two: float32 [16, 3, 3, 128, 128], P('rot')
The draws below stay inside these ranges and needn't reach their ends.
All inputs are finite; a program needn't handle non-finite values.
Results may differ from the reference program's by a relative error of at most 0.018.
Values may be sent and summed in bfloat16 or wider, within the bound.
No kernel may reach another device: no remote copies, remote signals or barrier semaphores. Data moves between devices by JAX's collectives and lax.ppermute only.
A program may use at most 64 MiB of HBM per device.

```python
import jax
import jax.numpy as jnp
from jax import lax

R = 16
C = 128
H = 4
AZ = 512


def block_scale(own_key, extent, shards, smallest, top_value):
    def one(dim, blocks):
        heights = jax.random.uniform(jax.random.fold_in(jax.random.fold_in(own_key, 6), dim), (blocks,), jnp.float32, smallest / len(shards), top_value / len(shards))
        return jnp.repeat(jnp.exp(heights), extent[dim] // blocks).reshape((-1,) + (1,) * (len(extent) - dim - 1))

    level = one(*shards[0])
    for cut in shards[1:]:
        level = level * one(*cut)
    return level


def gaussian(key, extent, scale, reach, cuts=(), kind=jnp.bfloat16):
    drawn = jax.random.normal(key, extent, jnp.float32) * scale
    if len(cuts) > 0:
        drawn = block_scale(key, extent, cuts, -0.22, 0.18) * drawn
    return jnp.clip(drawn, min=-reach, max=reach).astype(kind)


def setup_inputs(seed: int = 0) -> dict:
    key_of = jax.random.split(jax.random.key(seed), 7)
    inputs = gaussian(key_of[0], (R, H, AZ, C), 1.0, 6.0, ((0, 16), (2, 16)))
    pre_one = gaussian(key_of[1], (R, H, AZ, C), 1.5, 8.0, ((0, 16), (2, 16)))
    pre_two = gaussian(key_of[2], (R, H, AZ, C), 1.5, 8.0, ((0, 16), (2, 16)))
    cotangent = gaussian(key_of[3], (R, H, AZ, C), 1.0, 6.0, ((0, 16), (2, 16)))
    filt_one = gaussian(key_of[4], (R, 3, 3, C, C), (9 * R * C) ** -0.5, 0.046875, ((0, 16),))
    filt_two = gaussian(key_of[5], (R, 3, 3, C, C), (9 * R * C) ** -0.5, 0.046875, ((0, 16),))
    return dict(inputs=inputs, pre_one=pre_one, pre_two=pre_two, cotangent=cotangent, filt_one=filt_one, filt_two=filt_two)


def wrap_pad(field):
    widened = jnp.concatenate([field[:, :, -1:], field, field[:, :, :1]], axis=2)
    return jnp.pad(widened, ((0, 0), (1, 1), (0, 0), (0, 0)))

def slope(pre):
    widened = pre.astype(jnp.float32)
    logistic = jax.nn.sigmoid(widened)
    return logistic * (1.0 + widened * (1.0 - logistic))

def data_grad(gradient, filters):
    padded = wrap_pad(gradient.astype(jnp.float32))
    weights = filters.astype(jnp.float32)
    orient = jnp.arange(R, dtype=jnp.int32)

    def single(target):
        chosen = padded[(target - orient) % R]
        summed = jnp.zeros((H, AZ, C), jnp.float32)
        for row_tap in range(3):
            for col_tap in range(3):
                window = chosen[:, 2 - row_tap:2 - row_tap + H, 2 - col_tap:2 - col_tap + AZ, :]
                summed = summed + jnp.einsum('ryxc,ric->yxi', window, weights[:, row_tap, col_tap], precision=lax.Precision.HIGHEST)
        return summed
    return lax.map(single, orient)

def weight_grad(features, gradient):
    padded = wrap_pad(features.astype(jnp.float32))
    widened = gradient.astype(jnp.float32)
    orient = jnp.arange(R, dtype=jnp.int32)

    def single(relative):
        shifted = padded[(orient + relative) % R]
        pieces = []
        for row_tap in range(3):
            for col_tap in range(3):
                window = shifted[:, row_tap:row_tap + H, col_tap:col_tap + AZ, :]
                pieces.append(jnp.einsum('gyxi,gyxo->io', window, widened, precision=lax.Precision.HIGHEST))
        return jnp.stack(pieces).reshape(3, 3, C, C)
    return lax.map(single, orient)

def reference(inputs, pre_one, pre_two, cotangent, filt_one, filt_two):
    scale = (R * H * AZ) ** (-0.5)
    act_one = jax.nn.silu(pre_one.astype(jnp.float32)).astype(jnp.bfloat16)
    grad_two = (cotangent.astype(jnp.float32) * slope(pre_two)).astype(jnp.bfloat16)
    filt_grad_two = weight_grad(act_one, grad_two) * scale
    delta_one = data_grad(grad_two, filt_two)
    grad_one = (delta_one * slope(pre_one)).astype(jnp.bfloat16)
    input_grad = data_grad(grad_one, filt_one).astype(jnp.bfloat16)
    filt_grad_one = weight_grad(inputs, grad_one) * scale
    return (input_grad, filt_grad_one, filt_grad_two)
```

```python
import functools

import jax
import jax.numpy as jnp
from jax import lax
from jax.experimental import pallas as pl
from jax.experimental.pallas import tpu as pltpu
from jax.sharding import Mesh
from jax.sharding import PartitionSpec as P

CHIPS = ("rot_x", "rot_y")
CORE = "rot_c"
ROT = (*CHIPS, CORE)
AZ = "az"

ROWS = 4
CHAN = 128
WIDE = ROWS * CHAN
SWAP = [(0, 1), (1, 0)]
VMEM = pl.BlockSpec(memory_space=pltpu.VMEM)
SMEM = pl.BlockSpec(memory_space=pltpu.SMEM)


def slope(pre):
    logistic = 1.0 / (1.0 + jnp.exp(-pre))
    return logistic * (1.0 + pre * (1.0 - logistic))


def params():
    return pltpu.CompilerParams(vmem_limit_bytes=40 * 1024 * 1024)


def call(kernel, out_shape, scratch, flops, *operands):
    n_bytes = sum(a.size * a.dtype.itemsize for a in operands)
    in_specs = [SMEM if a.dtype == jnp.int32 else VMEM for a in operands]
    out_specs = jax.tree.map(lambda _: VMEM, out_shape)
    return pl.pallas_call(
        kernel,
        out_shape=out_shape,
        in_specs=in_specs,
        out_specs=out_specs,
        scratch_shapes=scratch,
        compiler_params=params(),
        cost_estimate=pl.CostEstimate(flops=flops, bytes_accessed=2 * n_bytes, transcendentals=0),
    )(*operands)


def interleave(blocks_ref, rows_ref, orients, width, shift):
    per_block = blocks_ref.shape[2] // WIDE
    for g in range(orients):
        s = (g - shift) % orients
        lanes = slice((s % per_block) * WIDE, (s % per_block + 1) * WIDE)
        rows_ref[:, g, :] = blocks_ref[s // per_block, :width, lanes].astype(jnp.float32)


def band_weights(filt_ref, band_ref, slot):
    zero = jnp.zeros((CHAN, CHAN), jnp.bfloat16)
    for j in range(3):
        for out_row in range(ROWS):
            for in_row in range(ROWS):
                i = out_row - in_row + 1
                piece = filt_ref[i, j] if 0 <= i < 3 else zero
                band_ref[
                    slot,
                    j,
                    out_row * CHAN : (out_row + 1) * CHAN,
                    in_row * CHAN : (in_row + 1) * CHAN,
                ] = piece


def conv_kernel(
    orients, width, place_ref, blocks_ref, mine_ref, other_ref, out_ref, rows_0, rows_1, band, sums
):
    chip, core = place_ref[0], place_ref[1]
    in_width = rows_0.shape[0]
    band_weights(mine_ref, band, core)
    band_weights(other_ref, band, 1 - core)
    interleave(blocks_ref, rows_0, orients, in_width, 0)
    interleave(blocks_ref, rows_1, orients, in_width, 1)
    total = None
    for slot, rows in ((0, rows_0), (1, rows_1)):
        flat = rows[...].reshape(in_width * orients, WIDE).astype(jnp.bfloat16)
        for j in range(3):
            window = flat[(2 - j) * orients : (2 - j + width) * orients]
            term = lax.dot_general(
                window,
                band[slot, j],
                (((1,), (1,)), ((), ())),
                preferred_element_type=jnp.float32,
            )
            total = term if total is None else total + term
    sums[...] = jnp.zeros_like(sums)
    sums[:width] = total.reshape(width, orients, WIDE)
    chips = orients // 2
    for pair in range(chips):
        to = lax.rem(pair + chip, chips)
        for half in range(2):
            out_ref[to, :, half * WIDE : (half + 1) * WIDE] = sums[:, 2 * pair + half, :].astype(
                jnp.bfloat16
            )


def conv(place, blocks, mine, other, width, out_width):
    orients = 16
    in_width = blocks.shape[1]
    return call(
        functools.partial(conv_kernel, orients, width),
        jax.ShapeDtypeStruct((orients // 2, out_width, 2 * WIDE), jnp.bfloat16),
        [
            pltpu.VMEM((in_width, orients, WIDE), jnp.float32),
            pltpu.VMEM((in_width, orients, WIDE), jnp.float32),
            pltpu.VMEM((2, 3, WIDE, WIDE), jnp.bfloat16),
            pltpu.VMEM((out_width, orients, WIDE), jnp.float32),
        ],
        2 * 6 * width * orients * WIDE * WIDE,
        place,
        blocks,
        mine,
        other,
    )


def filter_kernel(
    orients, width, first, place_ref, feat_ref, grad_ref, mine_ref, other_ref, feat_rows, grad_rows
):
    chip, core = place_ref[0], place_ref[1]
    in_width = grad_rows.shape[0]
    interleave(grad_ref, grad_rows, orients, in_width, 0)
    grads = grad_rows[...].reshape(in_width * orients, WIDE).astype(jnp.bfloat16)
    for out_ref, slot in ((other_ref, 1 - core), (mine_ref, core)):
        for g in range(orients):
            feat_rows[:, g, :] = feat_ref[lax.rem(g + 2 * chip + slot, orients)].astype(jnp.float32)
        feats = feat_rows[...].reshape(width * orients, WIDE).astype(jnp.bfloat16)
        for j in range(3):
            window = grads[(first - j) * orients : (first - j + width) * orients]
            product = lax.dot_general(
                feats,
                window,
                (((0,), (0,)), ((), ())),
                preferred_element_type=jnp.float32,
            )
            for i in range(3):
                total = None
                for row in range(ROWS):
                    grad_row = row - i + 1
                    if not 0 <= grad_row < ROWS:
                        continue
                    piece = product[
                        row * CHAN : (row + 1) * CHAN, grad_row * CHAN : (grad_row + 1) * CHAN
                    ]
                    total = piece if total is None else total + piece
                out_ref[i, j] = total.astype(jnp.bfloat16)


def filter_terms(place, feats, grads, first):
    orients = feats.shape[0]
    width = feats.shape[1]
    in_width = grads.shape[1]
    bank = jax.ShapeDtypeStruct((3, 3, CHAN, CHAN), jnp.bfloat16)
    mine, other = call(
        functools.partial(filter_kernel, orients, width, first),
        (bank, bank),
        [
            pltpu.VMEM((width, orients, WIDE), jnp.float32),
            pltpu.VMEM((in_width, orients, WIDE), jnp.float32),
        ],
        2 * 6 * width * orients * WIDE * WIDE,
        place,
        feats,
        grads,
    )
    theirs = lax.ppermute(other, CORE, SWAP)
    both = mine.astype(jnp.float32) + theirs.astype(jnp.float32)
    return both.astype(jnp.bfloat16)


def point_kernel(parts_ref, pre_ref, out_ref):
    total = parts_ref[0].astype(jnp.float32)
    for n in range(1, parts_ref.shape[0]):
        total = total + parts_ref[n].astype(jnp.float32)
    grad = (total * slope(pre_ref[...].astype(jnp.float32))).astype(jnp.bfloat16)
    for n in range(out_ref.shape[0]):
        out_ref[n] = grad


def to_everyone(array, axes):
    count = lax.axis_size(axes)
    return jnp.broadcast_to(array[None], (count, *array.shape))


def exchange(parts, axes):
    return lax.all_to_all(parts, axes, 0, 0, tiled=True)


def reduce_kernel(parts_ref, out_ref):
    total = parts_ref[0].astype(jnp.float32)
    for n in range(1, parts_ref.shape[0]):
        total = total + parts_ref[n].astype(jnp.float32)
    total = total.astype(jnp.bfloat16)
    for n in range(out_ref.shape[0]):
        out_ref[n] = total


def summed_over_az(bank, scale):
    count = lax.axis_size(AZ)
    lines = bank.reshape(count, -1, CHAN)
    arrived = exchange(lines, AZ)
    copies = call(
        reduce_kernel, jax.ShapeDtypeStruct(lines.shape, jnp.bfloat16), [], lines.size, arrived
    )
    whole = exchange(copies, AZ).reshape(bank.shape)
    return whole.astype(jnp.float32)[None] * scale


def shards(inputs, pre_one, pre_two, cotangent, filt_one, filt_two):
    columns = inputs.shape[2]
    half = columns // 2
    chip = lax.axis_index(CHIPS)
    core = lax.axis_index(CORE)
    place = jnp.stack([chip, core]).astype(jnp.int32)
    az_count = lax.axis_size(AZ)
    cell_count = lax.axis_size(ROT) * inputs.shape[1] * columns * az_count
    scale = cell_count ** (-0.5)

    def lines(field):
        return jnp.moveaxis(field[0], 0, 1).reshape(columns, WIDE)

    grad_two = lines((cotangent.astype(jnp.float32) * slope(pre_two.astype(jnp.float32))).astype(jnp.bfloat16))
    pre = lines(pre_one)
    forward = [(i, (i + 1) % az_count) for i in range(az_count)]
    backward = [(target, source) for source, target in forward]
    low = lax.ppermute(jnp.concatenate([grad_two[-2:], pre[-1:]]), AZ, forward)
    high = lax.ppermute(jnp.concatenate([grad_two[:2], pre[:1]]), AZ, backward)
    grad_rim = jnp.concatenate([low[:2], grad_two, high[:2]])
    halves = jnp.stack([jnp.pad(grad_rim[n * half : n * half + half + 4], ((0, 4), (0, 0))) for n in range(2)])
    chips = lax.axis_size(CHIPS)
    sent = jnp.broadcast_to(halves[None], (chips, *halves.shape)).reshape(2 * chips, *halves.shape[1:])
    all_grad_two = exchange(sent, ROT)

    other_two = lax.ppermute(filt_two[0], CORE, SWAP)
    other_one = lax.ppermute(filt_one[0], CORE, SWAP)
    act = lines(jax.nn.silu(pre_one.astype(jnp.float32)).astype(jnp.bfloat16))
    feats = jnp.concatenate([act, lines(inputs)], axis=1).reshape(2, half, 2 * WIDE)
    sent = jnp.broadcast_to(feats[None], (chips, *feats.shape)).reshape(2 * chips, *feats.shape[1:])
    all_feats = exchange(sent, ROT)
    all_act, all_inputs = all_feats[:, :, :WIDE], all_feats[:, :, WIDE:]
    pre_rim = jnp.concatenate([low[2:], pre, high[2:]])
    pre_halves = jnp.stack([pre_rim[: half + 2], pre_rim[half:]])
    pre_mine = lax.dynamic_index_in_dim(pre_halves, core, 0, keepdims=False)
    pre_other = lax.ppermute(lax.dynamic_index_in_dim(pre_halves, 1 - core, 0, keepdims=False), CORE, SWAP)
    pre_pair = jnp.where(
        core == 0,
        jnp.concatenate([pre_mine, pre_other], axis=1),
        jnp.concatenate([pre_other, pre_mine], axis=1),
    )
    pre_pair = jnp.pad(pre_pair, ((0, 6), (0, 0)))

    parts = exchange(conv(place, all_grad_two, filt_two[0], other_two, half + 2, half + 8), CHIPS)
    copies = call(
        point_kernel, jax.ShapeDtypeStruct(parts.shape, jnp.bfloat16), [], parts.size, parts, pre_pair
    )
    bank_two = filter_terms(place, all_act, all_grad_two, 3)
    all_grad_one = exchange(copies, CHIPS)
    bank_one = filter_terms(place, all_inputs, all_grad_one, 2)
    filt_grad_two = summed_over_az(bank_two, scale)
    filt_grad_one = summed_over_az(bank_one, scale)

    parts = exchange(conv(place, all_grad_one, filt_one[0], other_one, half, half), CHIPS)
    total = jnp.sum(parts.astype(jnp.float32), axis=0).astype(jnp.bfloat16)
    pair = total.reshape(half, 2, WIDE)
    mine = lax.dynamic_index_in_dim(pair, core, 1, keepdims=False)
    theirs = lax.ppermute(lax.dynamic_index_in_dim(pair, 1 - core, 1, keepdims=False), CORE, SWAP)
    whole = jnp.where(core == 0, jnp.concatenate([mine, theirs]), jnp.concatenate([theirs, mine]))
    input_grad = jnp.moveaxis(whole.reshape(columns, ROWS, CHAN), 1, 0)[None]
    return input_grad, filt_grad_one, filt_grad_two


def solution(mesh):
    finer = Mesh(mesh.devices.reshape(4, 2, 2, mesh.shape["az"]), (*ROT, AZ))
    field = P(ROT, None, AZ, None)
    bank = P(ROT, None, None, None, None)
    return jax.shard_map(
        shards,
        mesh=finer,
        in_specs=(field, field, field, field, bank, bank),
        out_specs=(field, bank, bank),
        check_vma=False,
    )
```

```python
import functools

import jax
import jax.numpy as jnp
from jax import lax
from jax.experimental import pallas as pl
from jax.experimental.pallas import tpu as pltpu
from jax.sharding import Mesh
from jax.sharding import PartitionSpec as P

CHIPS = ("rot_x", "rot_y")
CORE = "rot_c"
ROT = (*CHIPS, CORE)
AZ = "az"

ROWS = 4
CHAN = 128
WIDE = ROWS * CHAN
SWAP = [(0, 1), (1, 0)]
VMEM = pl.BlockSpec(memory_space=pltpu.VMEM)
SMEM = pl.BlockSpec(memory_space=pltpu.SMEM)


def slope(pre):
    logistic = 1.0 / (1.0 + jnp.exp(-pre))
    return logistic * (1.0 + pre * (1.0 - logistic))


def params():
    return pltpu.CompilerParams(vmem_limit_bytes=40 * 1024 * 1024)


def call(kernel, out_shape, scratch, flops, *operands):
    n_bytes = sum(a.size * a.dtype.itemsize for a in operands)
    in_specs = [SMEM if a.dtype == jnp.int32 else VMEM for a in operands]
    out_specs = jax.tree.map(lambda _: VMEM, out_shape)
    return pl.pallas_call(
        kernel,
        out_shape=out_shape,
        in_specs=in_specs,
        out_specs=out_specs,
        scratch_shapes=scratch,
        compiler_params=params(),
        cost_estimate=pl.CostEstimate(flops=flops, bytes_accessed=2 * n_bytes, transcendentals=0),
    )(*operands)


def interleave(blocks_ref, rows_ref, orients, width, shift):
    per_block = blocks_ref.shape[2] // WIDE
    for g in range(orients):
        s = (g - shift) % orients
        lanes = slice((s % per_block) * WIDE, (s % per_block + 1) * WIDE)
        rows_ref[:, g, :] = blocks_ref[s // per_block, :width, lanes].astype(jnp.float32)


def band_weights(filt_ref, band_ref, slot):
    zero = jnp.zeros((CHAN, CHAN), jnp.bfloat16)
    for j in range(3):
        for out_row in range(ROWS):
            for in_row in range(ROWS):
                i = out_row - in_row + 1
                piece = filt_ref[i, j] if 0 <= i < 3 else zero
                band_ref[
                    slot,
                    j,
                    out_row * CHAN : (out_row + 1) * CHAN,
                    in_row * CHAN : (in_row + 1) * CHAN,
                ] = piece


def rotation_sums(orients, width, core, blocks_ref, mine_ref, other_ref, rows_0, rows_1, band):
    in_width = rows_0.shape[0]
    band_weights(mine_ref, band, core)
    band_weights(other_ref, band, 1 - core)
    interleave(blocks_ref, rows_0, orients, in_width, 0)
    interleave(blocks_ref, rows_1, orients, in_width, 1)
    total = None
    for slot, rows in ((0, rows_0), (1, rows_1)):
        flat = rows[...].reshape(in_width * orients, WIDE).astype(jnp.bfloat16)
        for j in range(3):
            window = flat[(2 - j) * orients : (2 - j + width) * orients]
            term = lax.dot_general(
                window,
                band[slot, j],
                (((1,), (1,)), ((), ())),
                preferred_element_type=jnp.float32,
            )
            total = term if total is None else total + term
    return total.reshape(width, orients, WIDE)


def conv_two_kernel(
    orients,
    width,
    place_ref,
    blocks_ref,
    mine_ref,
    other_ref,
    feats_ref,
    partner_ref,
    out_ref,
    rows_0,
    rows_1,
    band,
    sums,
):
    chip, core = place_ref[0], place_ref[1]
    total = rotation_sums(
        orients, width, core, blocks_ref, mine_ref, other_ref, rows_0, rows_1, band
    )
    sums[...] = jnp.zeros_like(sums)
    sums[:width] = total
    chips = orients // 2
    ahead = feats_ref.shape[0]
    feats, partner = feats_ref[...], partner_ref[...]
    first = jnp.where(core == 0, feats, partner)
    second = jnp.where(core == 0, partner, feats)
    for pair in range(chips):
        to = lax.rem(pair + chip, chips)
        for half in range(2):
            out_ref[to, ahead:, half * WIDE : (half + 1) * WIDE] = sums[
                :, 2 * pair + half, :
            ].astype(jnp.bfloat16)
        out_ref[pair, :ahead, :WIDE] = first
        out_ref[pair, :ahead, WIDE:] = second


def conv_one_kernel(
    orients, width, place_ref, blocks_ref, mine_ref, other_ref, out_ref, rows_0, rows_1, band, sums
):
    chip, core = place_ref[0], place_ref[1]
    sums[...] = rotation_sums(
        orients, width, core, blocks_ref, mine_ref, other_ref, rows_0, rows_1, band
    )
    chips = orients // 2
    across = out_ref.shape[1]
    for pair in range(chips):
        to = lax.rem(pair + chip, chips)
        other = lax.rem(to + chip, 2)
        step = lax.rem(to // 2 - chip // 2 + across, across)
        for half in range(2):
            out_ref[other, step, :, half * WIDE : (half + 1) * WIDE] = sums[
                :, 2 * pair + half, :
            ].astype(jnp.bfloat16)


def conv(kernel, place, blocks, width, padded, out_shape, *operands):
    orients = 16
    in_width = blocks.shape[1]
    return call(
        functools.partial(kernel, orients, width),
        jax.ShapeDtypeStruct(out_shape, jnp.bfloat16),
        [
            pltpu.VMEM((in_width, orients, WIDE), jnp.float32),
            pltpu.VMEM((in_width, orients, WIDE), jnp.float32),
            pltpu.VMEM((2, 3, WIDE, WIDE), jnp.bfloat16),
            pltpu.VMEM((padded, orients, WIDE), jnp.float32),
        ],
        2 * 6 * width * orients * WIDE * WIDE,
        place,
        blocks,
        *operands,
    )


def filter_kernel(
    orients, width, feat_first, first, place_ref, feat_ref, grad_ref, mine_ref, other_ref, feat_rows, grad_rows
):
    chip, core = place_ref[0], place_ref[1]
    in_width = grad_rows.shape[0]
    interleave(grad_ref, grad_rows, orients, in_width, 0)
    grads = grad_rows[...].reshape(in_width * orients, WIDE).astype(jnp.bfloat16)
    for out_ref, slot in ((other_ref, 1 - core), (mine_ref, core)):
        for g in range(orients):
            near = lax.rem((g + 1) // 2 + chip, orients // 2)
            here = lax.rem(g // 2 + chip, orients // 2)
            low, high = feat_first, feat_first + width
            shift_0 = feat_ref[here, low:high, (g % 2) * WIDE : (g % 2 + 1) * WIDE]
            shift_1 = feat_ref[near, low:high, ((g + 1) % 2) * WIDE : ((g + 1) % 2 + 1) * WIDE]
            feat_rows[:, g, :] = jnp.where(slot == 0, shift_0, shift_1).astype(jnp.float32)
        feats = feat_rows[...].reshape(width * orients, WIDE).astype(jnp.bfloat16)
        for j in range(3):
            window = grads[(first - j) * orients : (first - j + width) * orients]
            product = lax.dot_general(
                feats,
                window,
                (((0,), (0,)), ((), ())),
                preferred_element_type=jnp.float32,
            )
            for i in range(3):
                total = None
                for row in range(ROWS):
                    grad_row = row - i + 1
                    if not 0 <= grad_row < ROWS:
                        continue
                    piece = product[
                        row * CHAN : (row + 1) * CHAN, grad_row * CHAN : (grad_row + 1) * CHAN
                    ]
                    total = piece if total is None else total + piece
                out_ref[i, j] = total.astype(jnp.bfloat16)


def filter_terms(place, feats, feat_first, width, grads, first):
    orients = 2 * feats.shape[0]
    in_width = grads.shape[1]
    bank = jax.ShapeDtypeStruct((3, 3, CHAN, CHAN), jnp.bfloat16)
    mine, other = call(
        functools.partial(filter_kernel, orients, width, feat_first, first),
        (bank, bank),
        [
            pltpu.VMEM((width, orients, WIDE), jnp.float32),
            pltpu.VMEM((in_width, orients, WIDE), jnp.float32),
        ],
        2 * 6 * width * orients * WIDE * WIDE,
        place,
        feats,
        grads,
    )
    return mine, lax.ppermute(other, CORE, SWAP)


def point_kernel(place_ref, parts_ref, pre_ref, partner_ref, out_ref):
    core = place_ref[1]
    ahead = parts_ref.shape[1] - out_ref.shape[1]
    total = parts_ref[0, ahead:].astype(jnp.float32)
    for n in range(1, parts_ref.shape[0]):
        total = total + parts_ref[n, ahead:].astype(jnp.float32)
    mine = slope(pre_ref[...].astype(jnp.float32))
    partner = slope(partner_ref[...].astype(jnp.float32))
    first = total[:, :WIDE] * jnp.where(core == 0, mine, partner)
    second = total[:, WIDE:] * jnp.where(core == 0, partner, mine)
    first, second = first.astype(jnp.bfloat16), second.astype(jnp.bfloat16)
    for n in range(out_ref.shape[0]):
        out_ref[n, :, :WIDE] = first
        out_ref[n, :, WIDE:] = second


def exchange(parts, axes):
    return lax.all_to_all(parts, axes, 0, 0, tiled=True)


def join_kernel(mine_1, theirs_1, mine_2, theirs_2, out_ref):
    size = mine_1.shape[1]
    for first, mine, theirs in ((0, mine_1, theirs_1), (size, mine_2, theirs_2)):
        both = mine[...].astype(jnp.float32) + theirs[...].astype(jnp.float32)
        out_ref[:, first : first + size] = both.astype(jnp.bfloat16)


def reduce_kernel(parts_ref, out_ref):
    total = parts_ref[0].astype(jnp.float32)
    for n in range(1, parts_ref.shape[0]):
        total = total + parts_ref[n].astype(jnp.float32)
    total = total.astype(jnp.bfloat16)
    for n in range(out_ref.shape[0]):
        out_ref[n] = total


def summed_over_az(pairs, scale):
    count = lax.axis_size(AZ)
    banks = [bank.reshape(count, -1, CHAN) for pair in pairs for bank in pair]
    size = banks[0].shape[1]
    shape = jax.ShapeDtypeStruct((count, 2 * size, CHAN), jnp.bfloat16)
    joined = call(join_kernel, shape, [], count * size * CHAN, *banks)
    copies = call(reduce_kernel, shape, [], count * size * CHAN, exchange(joined, AZ))
    whole = exchange(copies, AZ)
    one, two = whole[:, :size], whole[:, size:]
    return tuple(
        (part.astype(jnp.float32) * scale).reshape(1, 3, 3, CHAN, CHAN) for part in (one, two)
    )


def lanes_kernel(
    place_ref, inputs_ref, pre_one_ref, pre_two_ref, cotangent_ref, grad_ref, pre_ref, feats_ref, partner_ref, up_ref, down_ref
):
    core = place_ref[1]
    columns = grad_ref.shape[0]
    half = columns // 2
    for row in range(ROWS):
        lanes = slice(row * CHAN, (row + 1) * CHAN)
        pre = pre_one_ref[0, row]
        wide = pre.astype(jnp.float32)
        grad = cotangent_ref[0, row].astype(jnp.float32) * slope(
            pre_two_ref[0, row].astype(jnp.float32)
        )
        grad_ref[:, lanes] = grad.astype(jnp.bfloat16)
        pre_ref[:, lanes] = pre
        act = (wide / (1.0 + jnp.exp(-wide))).astype(jnp.bfloat16)
        given = inputs_ref[0, row]
        for first, field in ((0, act), (half, given)):
            low, high = field[:half], field[half:]
            feats_ref[first : first + half, lanes] = jnp.where(core == 0, low, high)
            partner_ref[first : first + half, lanes] = jnp.where(core == 0, high, low)
        grad = grad.astype(jnp.bfloat16).astype(jnp.float32)
        pad = jnp.zeros((5, CHAN), jnp.float32)
        up_ref[:, lanes] = jnp.concatenate([grad[-2:], wide[-1:], pad]).astype(jnp.bfloat16)
        down_ref[:, lanes] = jnp.concatenate([grad[:2], wide[:1], pad]).astype(jnp.bfloat16)


def rims_kernel(
    place_ref, grad_ref, pre_ref, low_ref, high_ref, sent_ref, mine_ref, partner_ref, grad_rim, pre_rim
):
    core = place_ref[1]
    columns = grad_ref.shape[0]
    half = columns // 2
    rows = sent_ref.shape[1]
    low, high = low_ref[...].astype(jnp.float32), high_ref[...].astype(jnp.float32)
    grad_rim[...] = jnp.zeros_like(grad_rim)
    grad_rim[:2] = low[:2]
    grad_rim[2 : 2 + columns] = grad_ref[...].astype(jnp.float32)
    grad_rim[2 + columns : 4 + columns] = high[:2]
    pre_rim[...] = jnp.zeros_like(pre_rim)
    pre_rim[:1] = low[2:3]
    pre_rim[1 : 1 + columns] = pre_ref[...].astype(jnp.float32)
    pre_rim[1 + columns : 2 + columns] = high[2:3]
    for n in range(2):
        part = grad_rim[n * half : n * half + rows].astype(jnp.bfloat16)
        for chip in range(sent_ref.shape[0] // 2):
            sent_ref[2 * chip + n] = part
    left = pre_rim[:rows].astype(jnp.bfloat16)
    right = pre_rim[half : half + rows].astype(jnp.bfloat16)
    mine_ref[...] = jnp.where(core == 0, left, right)
    partner_ref[...] = jnp.where(core == 0, right, left)


def shards(inputs, pre_one, pre_two, cotangent, filt_one, filt_two):
    columns = inputs.shape[2]
    half = columns // 2
    chip = lax.axis_index(CHIPS)
    core = lax.axis_index(CORE)
    place = jnp.stack([chip, core]).astype(jnp.int32)
    az_count = lax.axis_size(AZ)
    rot_count = lax.axis_size(ROT)
    chips = lax.axis_size(CHIPS)
    cell_count = rot_count * inputs.shape[1] * columns * az_count
    scale = cell_count ** (-0.5)
    padded = half + 8

    def narrow(*shape):
        return jax.ShapeDtypeStruct(shape, jnp.bfloat16)

    grad_two, pre, feats, feats_away, up, down = call(
        lanes_kernel,
        (
            narrow(columns, WIDE),
            narrow(columns, WIDE),
            narrow(columns, WIDE),
            narrow(columns, WIDE),
            narrow(8, WIDE),
            narrow(8, WIDE),
        ),
        [],
        inputs.size * 20,
        place,
        inputs,
        pre_one,
        pre_two,
        cotangent,
    )
    forward = [(i, (i + 1) % az_count) for i in range(az_count)]
    backward = [(target, source) for source, target in forward]
    low = lax.ppermute(up, AZ, forward)
    high = lax.ppermute(down, AZ, backward)
    sent, pre_here, pre_away = call(
        rims_kernel,
        (narrow(rot_count, padded, WIDE), narrow(padded, WIDE), narrow(padded, WIDE)),
        [pltpu.VMEM((columns + 8, WIDE), jnp.float32), pltpu.VMEM((columns + 8, WIDE), jnp.float32)],
        inputs.size * 20,
        place,
        grad_two,
        pre,
        low,
        high,
    )
    all_grad_two = exchange(sent, ROT)

    other_two = lax.ppermute(filt_two[0], CORE, SWAP)
    other_one = lax.ppermute(filt_one[0], CORE, SWAP)
    feats_partner = lax.ppermute(feats_away, CORE, SWAP)
    pre_partner = lax.ppermute(pre_away, CORE, SWAP)

    shares = conv(
        conv_two_kernel,
        place,
        all_grad_two,
        half + 2,
        padded,
        (chips, padded + columns, 2 * WIDE),
        filt_two[0],
        other_two,
        feats,
        feats_partner,
    )
    arrived = exchange(shares, CHIPS)
    copies = call(
        point_kernel,
        narrow(chips, padded, 2 * WIDE),
        [],
        arrived.size,
        place,
        arrived,
        pre_here,
        pre_partner,
    )
    all_grad_one = exchange(copies, CHIPS)
    pair_two = filter_terms(place, arrived, 0, half, all_grad_two, 3)
    pair_one = filter_terms(place, arrived, half, half, all_grad_one, 2)
    filt_grad_one, filt_grad_two = summed_over_az((pair_one, pair_two), scale)

    along_x = lax.axis_size(CHIPS[0])
    shares = conv(
        conv_one_kernel,
        place,
        all_grad_one,
        half,
        half,
        (2, along_x, half, 2 * WIDE),
        filt_one[0],
        other_one,
    )
    arrived_y = lax.ppermute(shares[1], CHIPS[1], SWAP)
    partial = (shares[0].astype(jnp.float32) + arrived_y.astype(jnp.float32)).astype(jnp.bfloat16)
    total = partial[0].astype(jnp.float32)
    for step in range(1, along_x):
        came = lax.ppermute(
            partial[step], CHIPS[0], [(i, (i + step) % along_x) for i in range(along_x)]
        )
        total = total + came.astype(jnp.float32)
    total = total.astype(jnp.bfloat16)
    left, right = total[:, :WIDE], total[:, WIDE:]
    mine = jnp.where(core == 0, left, right)
    theirs = lax.ppermute(jnp.where(core == 0, right, left), CORE, SWAP)
    whole = jnp.where(core == 0, jnp.concatenate([mine, theirs]), jnp.concatenate([theirs, mine]))
    input_grad = jnp.moveaxis(whole.reshape(columns, ROWS, CHAN), 1, 0)[None]
    return input_grad, filt_grad_one, filt_grad_two


def solution(mesh):
    finer = Mesh(mesh.devices.reshape(4, 2, 2, mesh.shape["az"]), (*ROT, AZ))
    field = P(ROT, None, AZ, None)
    bank = P(ROT, None, None, None, None)
    return jax.shard_map(
        shards,
        mesh=finer,
        in_specs=(field, field, field, field, bank, bank),
        out_specs=(field, bank, bank),
        check_vma=False,
    )
```

```python
import functools

import jax
import jax.numpy as jnp
from jax import lax
from jax.experimental import pallas as pl
from jax.experimental.pallas import tpu as pltpu
from jax.sharding import Mesh
from jax.sharding import PartitionSpec as P

CHIPS = ("rot_x", "rot_y")
CORE = "rot_c"
ROT = (*CHIPS, CORE)
AZ = "az"

ROWS = 4
CHAN = 128
WIDE = ROWS * CHAN
SWAP = [(0, 1), (1, 0)]
VMEM = pl.BlockSpec(memory_space=pltpu.VMEM)
HBM = pl.BlockSpec(memory_space=pltpu.HBM)


def slope(pre):
    logistic = 1.0 / (1.0 + jnp.exp(-pre))
    return logistic * (1.0 + pre * (1.0 - logistic))


def params(mebibytes):
    return pltpu.CompilerParams(vmem_limit_bytes=mebibytes * 1024 * 1024)


def here():
    return lax.axis_index(CHIPS[0]) * 2 + lax.axis_index(CHIPS[1]), lax.axis_index(CORE)


def call(kernel, out_shape, scratch, flops, *operands, space=VMEM, out_space=VMEM, room=40):
    n_bytes = sum(a.size * a.dtype.itemsize for a in operands)
    in_specs = list(space) if isinstance(space, tuple) else [space] * len(operands)
    out_specs = jax.tree.map(lambda _: out_space, out_shape)
    return pl.pallas_call(
        kernel,
        out_shape=out_shape,
        in_specs=in_specs,
        out_specs=out_specs,
        scratch_shapes=scratch,
        compiler_params=params(room),
        cost_estimate=pl.CostEstimate(flops=flops, bytes_accessed=2 * n_bytes, transcendentals=0),
    )(*operands)


def copy_all(pairs, done):
    copies = [pltpu.make_async_copy(a, b, done.at[n]) for n, (a, b) in enumerate(pairs)]
    for copy in copies:
        copy.start()
    for copy in copies:
        copy.wait()


def interleave(blocks_ref, rows_ref, orients, width, shift):
    per_block = blocks_ref.shape[2] // WIDE
    for g in range(orients):
        s = (g - shift) % orients
        lanes = slice((s % per_block) * WIDE, (s % per_block + 1) * WIDE)
        rows_ref[:, g, :] = blocks_ref[s // per_block, :width, lanes].astype(jnp.float32)


def band_weights(filt_ref, band_ref, slot):
    zero = jnp.zeros((CHAN, CHAN), jnp.bfloat16)
    for j in range(3):
        for out_row in range(ROWS):
            for in_row in range(ROWS):
                i = out_row - in_row + 1
                piece = filt_ref[i, j] if 0 <= i < 3 else zero
                band_ref[
                    slot,
                    j,
                    out_row * CHAN : (out_row + 1) * CHAN,
                    in_row * CHAN : (in_row + 1) * CHAN,
                ] = piece


def bands_kernel(mine_ref, other_ref, band_ref):
    _, core = here()
    band_weights(mine_ref, band_ref, core)
    band_weights(other_ref, band_ref, 1 - core)


def bands(mine, other):
    shape = jax.ShapeDtypeStruct((2, 3, WIDE, WIDE), jnp.bfloat16)
    return call(bands_kernel, shape, [], mine.size, mine, other)


def rotation_sums(orients, width, blocks_ref, band_ref, rows_0, rows_1, band, fetched):
    in_width = rows_0.shape[0]
    copies = [
        pltpu.make_async_copy(band_ref.at[n], band.at[n], fetched.at[n]) for n in range(2)
    ]
    for copy in copies:
        copy.start()
    interleave(blocks_ref, rows_0, orients, in_width, 0)
    interleave(blocks_ref, rows_1, orients, in_width, 1)
    total = None
    for slot, rows in ((0, rows_0), (1, rows_1)):
        copies[slot].wait()
        flat = rows[...].reshape(in_width * orients, WIDE).astype(jnp.bfloat16)
        for j in range(3):
            window = flat[(2 - j) * orients : (2 - j + width) * orients]
            term = lax.dot_general(
                window,
                band[slot, j],
                (((1,), (1,)), ((), ())),
                preferred_element_type=jnp.float32,
            )
            total = term if total is None else total + term
    return total.reshape(width, orients, WIDE)


def conv_two_kernel(orients, width, blocks_ref, band_ref, out_ref, *scratch):
    *rows, sums, held, done = scratch
    chip, _ = here()
    total = rotation_sums(orients, width, blocks_ref, band_ref, *rows)
    sums[width:] = jnp.zeros((sums.shape[0] - width, orients, WIDE), jnp.float32)
    sums[:width] = total
    chips = orients // 2
    copies = []
    for pair in range(chips):
        for half in range(2):
            held[pair, :, half * WIDE : (half + 1) * WIDE] = sums[:, 2 * pair + half, :].astype(
                jnp.bfloat16
            )
        to = lax.rem(pair + chip, chips)
        copies.append(pltpu.make_async_copy(held.at[pair], out_ref.at[to], done.at[pair]))
        copies[-1].start()
    for copy in copies:
        copy.wait()


def conv_one_kernel(orients, width, blocks_ref, band_ref, out_ref, *scratch):
    *rows, sums = scratch
    chip, _ = here()
    sums[...] = rotation_sums(orients, width, blocks_ref, band_ref, *rows)
    chips = orients // 2
    across = out_ref.shape[1]
    for pair in range(chips):
        to = lax.rem(pair + chip, chips)
        other = lax.rem(to + chip, 2)
        step = lax.rem(to // 2 - chip // 2 + across, across)
        for half in range(2):
            out_ref[other, step, :, half * WIDE : (half + 1) * WIDE] = sums[
                :, 2 * pair + half, :
            ].astype(jnp.bfloat16)


def conv(kernel, blocks, band, width, padded, out_shape, staging=(), out_space=VMEM, room=40):
    orients = 16
    in_width = blocks.shape[1]
    return call(
        functools.partial(kernel, orients, width),
        jax.ShapeDtypeStruct(out_shape, jnp.bfloat16),
        [
            pltpu.VMEM((in_width, orients, WIDE), jnp.float32),
            pltpu.VMEM((in_width, orients, WIDE), jnp.float32),
            pltpu.VMEM(band.shape, jnp.bfloat16),
            pltpu.SemaphoreType.DMA((2,)),
            pltpu.VMEM((padded, orients, WIDE), jnp.float32),
            *staging,
        ],
        2 * 6 * width * orients * WIDE * WIDE,
        blocks,
        band,
        space=(VMEM, HBM),
        out_space=out_space,
        room=room,
    )


def filter_kernel(
    orients, width, field, first, own, grad_ref, feat_ref, out_ref, feat_rows, grad_rows, held, done
):
    chip, core = here()
    slot = core if own else 1 - core
    in_width = grad_rows.shape[0]
    columns = pl.ds(pl.multiple_of(core * width, width), width)
    lanes = pl.ds(field * WIDE, WIDE)
    copy = pltpu.make_async_copy(feat_ref.at[:, columns, lanes], held, done)
    copy.start()
    interleave(grad_ref, grad_rows, orients, in_width, 0)
    grads = grad_rows[...].reshape(in_width * orients, WIDE).astype(jnp.bfloat16)
    copy.wait()
    for g in range(orients):
        s = lax.rem(g + 2 * chip + slot, orients)
        feat_rows[:, g, :] = held[s].astype(jnp.float32)
    feats = feat_rows[...].reshape(width * orients, WIDE).astype(jnp.bfloat16)
    for j in range(3):
        window = grads[(first - j) * orients : (first - j + width) * orients]
        product = lax.dot_general(
            feats,
            window,
            (((0,), (0,)), ((), ())),
            preferred_element_type=jnp.float32,
        )
        for i in range(3):
            total = None
            for row in range(ROWS):
                grad_row = row - i + 1
                if not 0 <= grad_row < ROWS:
                    continue
                piece = product[
                    row * CHAN : (row + 1) * CHAN, grad_row * CHAN : (grad_row + 1) * CHAN
                ]
                total = piece if total is None else total + piece
            out_ref[i, j] = total.astype(jnp.bfloat16)


def filter_terms(feats, field, width, grads, first):
    orients = feats.shape[0]
    in_width = grads.shape[1]

    def terms(own):
        return call(
            functools.partial(filter_kernel, orients, width, field, first, own),
            jax.ShapeDtypeStruct((3, 3, CHAN, CHAN), jnp.bfloat16),
            [
                pltpu.VMEM((width, orients, WIDE), jnp.float32),
                pltpu.VMEM((in_width, orients, WIDE), jnp.float32),
                pltpu.VMEM((orients, width, WIDE), jnp.bfloat16),
                pltpu.SemaphoreType.DMA,
            ],
            6 * width * orients * WIDE * WIDE,
            grads,
            feats,
            space=(VMEM, HBM),
            room=52,
        )

    theirs = lax.ppermute(terms(False), CORE, SWAP)
    return terms(True), theirs


def point_kernel(parts_ref, pre_ref, partner_ref, out_ref, held, done):
    _, core = here()
    total = parts_ref[0].astype(jnp.float32)
    for n in range(1, parts_ref.shape[0]):
        total = total + parts_ref[n].astype(jnp.float32)
    mine = slope(pre_ref[...].astype(jnp.float32))
    partner = slope(partner_ref[...].astype(jnp.float32))
    first = total[:, :WIDE] * jnp.where(core == 0, mine, partner)
    second = total[:, WIDE:] * jnp.where(core == 0, partner, mine)
    held[:, :WIDE] = first.astype(jnp.bfloat16)
    held[:, WIDE:] = second.astype(jnp.bfloat16)
    copy_all([(held, out_ref.at[n]) for n in range(out_ref.shape[0])], done)


def exchange(parts, axes):
    return lax.all_to_all(parts, axes, 0, 0, tiled=True)


def join_kernel(mine_1, theirs_1, mine_2, theirs_2, out_ref, held, done):
    size = mine_1.shape[1]
    for first, mine, theirs in ((0, mine_1, theirs_1), (size, mine_2, theirs_2)):
        both = mine[...].astype(jnp.float32) + theirs[...].astype(jnp.float32)
        held[:, first : first + size] = both.astype(jnp.bfloat16)
    copy_all([(held, out_ref)], done)


def reduce_kernel(parts_ref, out_ref, held, done):
    total = parts_ref[0].astype(jnp.float32)
    for n in range(1, parts_ref.shape[0]):
        total = total + parts_ref[n].astype(jnp.float32)
    held[...] = total.astype(jnp.bfloat16)
    copy_all([(held, out_ref.at[n]) for n in range(out_ref.shape[0])], done)


def summed_over_az(pairs, scale):
    count = lax.axis_size(AZ)
    banks = [bank.reshape(count, -1, CHAN) for pair in pairs for bank in pair]
    size = banks[0].shape[1]
    shape = jax.ShapeDtypeStruct((count, 2 * size, CHAN), jnp.bfloat16)
    work = count * size * CHAN
    held = [pltpu.VMEM(shape.shape, jnp.bfloat16), pltpu.SemaphoreType.DMA((1,))]
    joined = call(join_kernel, shape, held, work, *banks, out_space=HBM)
    held = [pltpu.VMEM(shape.shape[1:], jnp.bfloat16), pltpu.SemaphoreType.DMA((count,))]
    copies = call(reduce_kernel, shape, held, work, exchange(joined, AZ), out_space=HBM)
    whole = exchange(copies, AZ)
    one, two = whole[:, :size], whole[:, size:]
    return tuple(
        (part.astype(jnp.float32) * scale).reshape(1, 3, 3, CHAN, CHAN) for part in (one, two)
    )


def lanes_kernel(*refs):
    given, (grad_ref, pre_ref, feats_ref, up_ref, down_ref) = refs[:4], refs[4:9]
    held, done = refs[9:13], refs[13]
    copy_all(zip(given, held), done)
    inputs_ref, pre_one_ref, pre_two_ref, cotangent_ref = held
    for row in range(ROWS):
        lanes = slice(row * CHAN, (row + 1) * CHAN)
        pre = pre_one_ref[0, row]
        wide = pre.astype(jnp.float32)
        grad = cotangent_ref[0, row].astype(jnp.float32) * slope(
            pre_two_ref[0, row].astype(jnp.float32)
        )
        grad = grad.astype(jnp.bfloat16)
        grad_ref[:, lanes] = grad
        pre_ref[:, lanes] = pre
        feats_ref[:, lanes] = (wide / (1.0 + jnp.exp(-wide))).astype(jnp.bfloat16)
        feats_ref[:, WIDE + row * CHAN : WIDE + (row + 1) * CHAN] = inputs_ref[0, row]
        grad = grad.astype(jnp.float32)
        pad = jnp.zeros((5, CHAN), jnp.float32)
        up_ref[:, lanes] = jnp.concatenate([grad[-2:], wide[-1:], pad]).astype(jnp.bfloat16)
        down_ref[:, lanes] = jnp.concatenate([grad[:2], wide[:1], pad]).astype(jnp.bfloat16)


def rims_kernel(grad_ref, low_ref, high_ref, out_ref, grad_rim, held, done):
    columns = grad_ref.shape[0]
    rows = out_ref.shape[1]
    grad_rim[:2] = low_ref[...].astype(jnp.float32)[:2]
    grad_rim[2 : 2 + columns] = grad_ref[...].astype(jnp.float32)
    grad_rim[2 + columns :] = jnp.zeros((grad_rim.shape[0] - 2 - columns, WIDE), jnp.float32)
    grad_rim[2 + columns : 4 + columns] = high_ref[...].astype(jnp.float32)[:2]
    for n in range(2):
        first = n * columns // 2
        held[n] = grad_rim[first : first + rows].astype(jnp.bfloat16)
    copy_all([(held.at[n % 2], out_ref.at[n]) for n in range(out_ref.shape[0])], done)


def pre_kernel(pre_ref, low_ref, high_ref, mine_ref, partner_ref, pre_rim):
    _, core = here()
    columns = pre_ref.shape[0]
    half = columns // 2
    rows = mine_ref.shape[0]
    pre_rim[...] = jnp.zeros_like(pre_rim)
    pre_rim[:1] = low_ref[...].astype(jnp.float32)[2:3]
    pre_rim[1 : 1 + columns] = pre_ref[...].astype(jnp.float32)
    pre_rim[1 + columns : 2 + columns] = high_ref[...].astype(jnp.float32)[2:3]
    left = pre_rim[:rows].astype(jnp.bfloat16)
    right = pre_rim[half : half + rows].astype(jnp.bfloat16)
    mine_ref[...] = jnp.where(core == 0, left, right)
    partner_ref[...] = jnp.where(core == 0, right, left)


def shards(inputs, pre_one, pre_two, cotangent, filt_one, filt_two):
    columns = inputs.shape[2]
    half = columns // 2
    core = lax.axis_index(CORE)
    az_count = lax.axis_size(AZ)
    rot_count = lax.axis_size(ROT)
    chips = lax.axis_size(CHIPS)
    cell_count = rot_count * inputs.shape[1] * columns * az_count
    scale = cell_count ** (-0.5)
    padded = half + 8

    def narrow(*shape):
        return jax.ShapeDtypeStruct(shape, jnp.bfloat16)

    grad_two, pre, feats, up, down = call(
        lanes_kernel,
        (
            narrow(columns, WIDE),
            narrow(columns, WIDE),
            narrow(columns, 2 * WIDE),
            narrow(8, WIDE),
            narrow(8, WIDE),
        ),
        [pltpu.VMEM(inputs.shape, jnp.bfloat16)] * 4 + [pltpu.SemaphoreType.DMA((4,))],
        inputs.size * 20,
        inputs,
        pre_one,
        pre_two,
        cotangent,
        space=HBM,
        room=60,
    )
    all_feats = lax.all_gather(feats, ROT)
    forward = [(i, (i + 1) % az_count) for i in range(az_count)]
    backward = [(target, source) for source, target in forward]
    low = lax.ppermute(up, AZ, forward)
    high = lax.ppermute(down, AZ, backward)
    rim = pltpu.VMEM((columns + 8, WIDE), jnp.float32)
    sent = call(
        rims_kernel,
        narrow(rot_count, padded, WIDE),
        [
            rim,
            pltpu.VMEM((2, padded, WIDE), jnp.bfloat16),
            pltpu.SemaphoreType.DMA((rot_count,)),
        ],
        inputs.size * 20,
        grad_two,
        low,
        high,
        out_space=HBM,
    )
    all_grad_two = exchange(sent, ROT)

    pre_here, pre_away = call(
        pre_kernel,
        (narrow(padded, WIDE), narrow(padded, WIDE)),
        [rim],
        inputs.size,
        pre,
        low,
        high,
    )

    other_two = lax.ppermute(filt_two[0], CORE, SWAP)
    other_one = lax.ppermute(filt_one[0], CORE, SWAP)
    pre_partner = lax.ppermute(pre_away, CORE, SWAP)
    bands_two = bands(filt_two[0], other_two)
    bands_one = bands(filt_one[0], other_one)

    shares = conv(
        conv_two_kernel,
        all_grad_two,
        bands_two,
        half + 2,
        padded,
        (chips, padded, 2 * WIDE),
        [
            pltpu.VMEM((chips, padded, 2 * WIDE), jnp.bfloat16),
            pltpu.SemaphoreType.DMA((chips,)),
        ],
        HBM,
        52,
    )
    arrived = exchange(shares, CHIPS)
    copies = call(
        point_kernel,
        narrow(chips, padded, 2 * WIDE),
        [pltpu.VMEM((padded, 2 * WIDE), jnp.bfloat16), pltpu.SemaphoreType.DMA((chips,))],
        arrived.size,
        arrived,
        pre_here,
        pre_partner,
        out_space=HBM,
    )
    copies, all_feats = lax.optimization_barrier((copies, all_feats))
    all_grad_one = exchange(copies, CHIPS)
    pair_two = filter_terms(all_feats, 0, half, all_grad_two, 3)
    all_grad_one, pair_two = lax.optimization_barrier((all_grad_one, pair_two))
    pair_one = filter_terms(all_feats, 1, half, all_grad_one, 2)
    filt_grad_one, filt_grad_two = summed_over_az((pair_one, pair_two), scale)

    along_x = lax.axis_size(CHIPS[0])
    shares = conv(
        conv_one_kernel,
        all_grad_one,
        bands_one,
        half,
        half,
        (2, along_x, half, 2 * WIDE),
    )
    arrived_y = lax.ppermute(shares[1], CHIPS[1], SWAP)
    partial = (shares[0].astype(jnp.float32) + arrived_y.astype(jnp.float32)).astype(jnp.bfloat16)
    total = partial[0].astype(jnp.float32)
    for step in range(1, along_x):
        came = lax.ppermute(
            partial[step], CHIPS[0], [(i, (i + step) % along_x) for i in range(along_x)]
        )
        total = total + came.astype(jnp.float32)
    total = total.astype(jnp.bfloat16)
    left, right = total[:, :WIDE], total[:, WIDE:]
    mine = jnp.where(core == 0, left, right)
    theirs = lax.ppermute(jnp.where(core == 0, right, left), CORE, SWAP)
    whole = jnp.where(core == 0, jnp.concatenate([mine, theirs]), jnp.concatenate([theirs, mine]))
    input_grad = jnp.moveaxis(whole.reshape(columns, ROWS, CHAN), 1, 0)[None]
    return input_grad, filt_grad_one, filt_grad_two


def solution(mesh):
    finer = Mesh(mesh.devices.reshape(4, 2, 2, mesh.shape["az"]), (*ROT, AZ))
    field = P(ROT, None, AZ, None)
    bank = P(ROT, None, None, None, None)
    return jax.shard_map(
        shards,
        mesh=finer,
        in_specs=(field, field, field, field, bank, bank),
        out_specs=(field, bank, bank),
        check_vma=False,
    )
```

```python
import functools

import jax
import jax.numpy as jnp
from jax import lax
from jax.experimental import pallas as pl
from jax.experimental.pallas import tpu as pltpu
from jax.sharding import Mesh
from jax.sharding import PartitionSpec as P

CHIPS = ("rot_x", "rot_y")
CORE = "rot_c"
ROT = (*CHIPS, CORE)
AZ = "az"

ROWS = 4
CHAN = 128
WIDE = ROWS * CHAN
SWAP = [(0, 1), (1, 0)]
VMEM = pl.BlockSpec(memory_space=pltpu.VMEM)
HBM = pl.BlockSpec(memory_space=pltpu.HBM)


def slope(pre):
    logistic = 1.0 / (1.0 + jnp.exp(-pre))
    return logistic * (1.0 + pre * (1.0 - logistic))


def params(mebibytes):
    return pltpu.CompilerParams(vmem_limit_bytes=mebibytes * 1024 * 1024)


def here():
    return lax.axis_index(CHIPS[0]) * 2 + lax.axis_index(CHIPS[1]), lax.axis_index(CORE)


def call(kernel, out_shape, scratch, flops, *operands, space=VMEM, out_space=VMEM, room=40):
    n_bytes = sum(a.size * a.dtype.itemsize for a in operands)
    in_specs = list(space) if isinstance(space, tuple) else [space] * len(operands)
    out_specs = jax.tree.map(lambda _: out_space, out_shape)
    return pl.pallas_call(
        kernel,
        out_shape=out_shape,
        in_specs=in_specs,
        out_specs=out_specs,
        scratch_shapes=scratch,
        compiler_params=params(room),
        cost_estimate=pl.CostEstimate(flops=flops, bytes_accessed=2 * n_bytes, transcendentals=0),
    )(*operands)


def copy_all(pairs, done):
    copies = [pltpu.make_async_copy(a, b, done.at[n]) for n, (a, b) in enumerate(pairs)]
    for copy in copies:
        copy.start()
    for copy in copies:
        copy.wait()


def interleave(blocks_ref, rows_ref, orients, width, shift):
    per_block = blocks_ref.shape[2] // WIDE
    for g in range(orients):
        s = (g - shift) % orients
        lanes = slice((s % per_block) * WIDE, (s % per_block + 1) * WIDE)
        rows_ref[:, g, :] = blocks_ref[s // per_block, :width, lanes].astype(jnp.float32)


def band_weights(filt_ref, band_ref, slot):
    zero = jnp.zeros((CHAN, CHAN), jnp.bfloat16)
    for j in range(3):
        for out_row in range(ROWS):
            for in_row in range(ROWS):
                i = out_row - in_row + 1
                piece = filt_ref[i, j] if 0 <= i < 3 else zero
                band_ref[
                    slot,
                    j,
                    out_row * CHAN : (out_row + 1) * CHAN,
                    in_row * CHAN : (in_row + 1) * CHAN,
                ] = piece


def bands_kernel(mine_ref, other_ref, band_ref):
    _, core = here()
    band_weights(mine_ref, band_ref, core)
    band_weights(other_ref, band_ref, 1 - core)


def bands(mine, other):
    shape = jax.ShapeDtypeStruct((2, 3, WIDE, WIDE), jnp.bfloat16)
    return call(bands_kernel, shape, [], mine.size, mine, other)


def rotation_sums(orients, width, blocks_ref, band_ref, rows_0, rows_1, band, fetched):
    in_width = rows_0.shape[0]
    copies = [
        pltpu.make_async_copy(band_ref.at[n], band.at[n], fetched.at[n]) for n in range(2)
    ]
    for copy in copies:
        copy.start()
    interleave(blocks_ref, rows_0, orients, in_width, 0)
    interleave(blocks_ref, rows_1, orients, in_width, 1)
    total = None
    for slot, rows in ((0, rows_0), (1, rows_1)):
        copies[slot].wait()
        flat = rows[...].reshape(in_width * orients, WIDE).astype(jnp.bfloat16)
        for j in range(3):
            window = flat[(2 - j) * orients : (2 - j + width) * orients]
            term = lax.dot_general(
                window,
                band[slot, j],
                (((1,), (1,)), ((), ())),
                preferred_element_type=jnp.float32,
            )
            total = term if total is None else total + term
    return total.reshape(width, orients, WIDE)


def conv_two_kernel(orients, width, blocks_ref, band_ref, out_ref, *scratch):
    *rows, sums, held, done = scratch
    chip, _ = here()
    total = rotation_sums(orients, width, blocks_ref, band_ref, *rows)
    sums[width:] = jnp.zeros((sums.shape[0] - width, orients, WIDE), jnp.float32)
    sums[:width] = total
    chips = orients // 2
    copies = []
    for pair in range(chips):
        for half in range(2):
            held[pair, :, half * WIDE : (half + 1) * WIDE] = sums[:, 2 * pair + half, :].astype(
                jnp.bfloat16
            )
        to = lax.rem(pair + chip, chips)
        copies.append(pltpu.make_async_copy(held.at[pair], out_ref.at[to], done.at[pair]))
        copies[-1].start()
    for copy in copies:
        copy.wait()


def conv_one_kernel(orients, width, blocks_ref, band_ref, out_ref, *scratch):
    *rows, sums = scratch
    chip, _ = here()
    sums[...] = rotation_sums(orients, width, blocks_ref, band_ref, *rows)
    chips = orients // 2
    across = out_ref.shape[1]
    for pair in range(chips):
        to = lax.rem(pair + chip, chips)
        other = lax.rem(to + chip, 2)
        step = lax.rem(to // 2 - chip // 2 + across, across)
        for half in range(2):
            out_ref[other, step, :, half * WIDE : (half + 1) * WIDE] = sums[
                :, 2 * pair + half, :
            ].astype(jnp.bfloat16)


def conv(kernel, blocks, band, width, padded, out_shape, staging=(), out_space=VMEM, room=40):
    orients = 16
    in_width = blocks.shape[1]
    return call(
        functools.partial(kernel, orients, width),
        jax.ShapeDtypeStruct(out_shape, jnp.bfloat16),
        [
            pltpu.VMEM((in_width, orients, WIDE), jnp.float32),
            pltpu.VMEM((in_width, orients, WIDE), jnp.float32),
            pltpu.VMEM(band.shape, jnp.bfloat16),
            pltpu.SemaphoreType.DMA((2,)),
            pltpu.VMEM((padded, orients, WIDE), jnp.float32),
            *staging,
        ],
        2 * 6 * width * orients * WIDE * WIDE,
        blocks,
        band,
        space=(VMEM, HBM),
        out_space=out_space,
        room=room,
    )


def filter_kernel(
    orients, width, field, first, own, grad_ref, *refs
):
    feat_refs, (out_ref, feat_rows, grad_rows, held, done) = refs[:-5], refs[-5:]
    chip, core = here()
    slot = core if own else 1 - core
    in_width = grad_rows.shape[0]
    lanes = pl.ds(field * WIDE, WIDE)
    copies = []
    for step, feat_ref in enumerate(feat_refs):
        row = lax.rem(chip // 2 - step + len(feat_refs), len(feat_refs))
        for y in range(2):
            for c in range(2):
                s = (row * 2 + (chip + y) % 2) * 2 + (core + c) % 2
                copy = pltpu.make_async_copy(
                    feat_ref.at[y, c, :, lanes], held.at[s], done.at[len(copies)]
                )
                copy.start()
                copies.append(copy)
    interleave(grad_ref, grad_rows, orients, in_width, 0)
    grads = grad_rows[...].reshape(in_width * orients, WIDE).astype(jnp.bfloat16)
    for copy in copies:
        copy.wait()
    for g in range(orients):
        s = lax.rem(g + 2 * chip + slot, orients)
        feat_rows[:, g, :] = held[s].astype(jnp.float32)
    feats = feat_rows[...].reshape(width * orients, WIDE).astype(jnp.bfloat16)
    for j in range(3):
        window = grads[(first - j) * orients : (first - j + width) * orients]
        product = lax.dot_general(
            feats,
            window,
            (((0,), (0,)), ((), ())),
            preferred_element_type=jnp.float32,
        )
        for i in range(3):
            total = None
            for row in range(ROWS):
                grad_row = row - i + 1
                if not 0 <= grad_row < ROWS:
                    continue
                piece = product[
                    row * CHAN : (row + 1) * CHAN, grad_row * CHAN : (grad_row + 1) * CHAN
                ]
                total = piece if total is None else total + piece
            out_ref[i, j] = total.astype(jnp.bfloat16)


def filter_terms(feats, field, width, grads, first):
    orients = len(feats) * 4
    in_width = grads.shape[1]

    def terms(own):
        return call(
            functools.partial(filter_kernel, orients, width, field, first, own),
            jax.ShapeDtypeStruct((3, 3, CHAN, CHAN), jnp.bfloat16),
            [
                pltpu.VMEM((width, orients, WIDE), jnp.float32),
                pltpu.VMEM((in_width, orients, WIDE), jnp.float32),
                pltpu.VMEM((orients, width, WIDE), jnp.bfloat16),
                pltpu.SemaphoreType.DMA((orients,)),
            ],
            6 * width * orients * WIDE * WIDE,
            grads,
            *feats,
            space=(VMEM, *[HBM] * len(feats)),
            room=52,
        )

    theirs = lax.ppermute(terms(False), CORE, SWAP)
    return terms(True), theirs


def point_kernel(parts_ref, pre_ref, partner_ref, out_ref, held, done):
    _, core = here()
    total = parts_ref[0].astype(jnp.float32)
    for n in range(1, parts_ref.shape[0]):
        total = total + parts_ref[n].astype(jnp.float32)
    mine = slope(pre_ref[...].astype(jnp.float32))
    partner = slope(partner_ref[...].astype(jnp.float32))
    first = total[:, :WIDE] * jnp.where(core == 0, mine, partner)
    second = total[:, WIDE:] * jnp.where(core == 0, partner, mine)
    held[:, :WIDE] = first.astype(jnp.bfloat16)
    held[:, WIDE:] = second.astype(jnp.bfloat16)
    copy_all([(held, out_ref.at[n]) for n in range(out_ref.shape[0])], done)


def exchange(parts, axes):
    return lax.all_to_all(parts, axes, 0, 0, tiled=True)


def chunks(pair):
    count = lax.axis_size(AZ)
    return [bank.reshape(count, -1, CHAN) for bank in pair]


def after(array, first):
    return lax.optimization_barrier((array, first))[0]


def halves_kernel(mine, theirs, stay_ref, leave_ref, both_ref):
    half = stay_ref.shape[0]
    side = lax.axis_index(AZ) // half
    both_ref[...] = mine[...].astype(jnp.float32) + theirs[...].astype(jnp.float32)
    stay_ref[...] = both_ref[pl.ds(side * half, half)].astype(jnp.bfloat16)
    leave_ref[...] = both_ref[pl.ds((1 - side) * half, half)].astype(jnp.bfloat16)


def deal_kernel(stay, came, out_ref):
    both = stay[...].astype(jnp.float32) + came[...].astype(jnp.float32)
    lines = both.reshape(-1, CHAN)
    count, size, _ = out_ref.shape
    lines = jnp.concatenate([lines, jnp.zeros((count * size - lines.shape[0], CHAN), jnp.float32)])
    out_ref[...] = lines.reshape(out_ref.shape).astype(jnp.bfloat16)


def half_terms(pair):
    mine, theirs = chunks(pair)
    count, size, _ = mine.shape
    half = jax.ShapeDtypeStruct((count // 2, size, CHAN), jnp.bfloat16)
    both = pltpu.VMEM(mine.shape, jnp.float32)
    stay, leave = call(halves_kernel, (half, half), [both], mine.size, mine, theirs)
    came = lax.ppermute(leave, AZ, [(i, (i + count // 2) % count) for i in range(count)])
    dealt = -(-size // 16) * 8
    shape = jax.ShapeDtypeStruct((count, dealt, CHAN), jnp.bfloat16)
    return leave, call(deal_kernel, shape, [], mine.size, stay, came)


def join_kernel(mine, theirs, also, out_ref, held, done):
    size = mine.shape[1]
    both = mine[...].astype(jnp.float32) + theirs[...].astype(jnp.float32)
    held[:, :size] = both.astype(jnp.bfloat16)
    held[:, size:] = also[...]
    copy_all([(held, out_ref)], done)


def joined_terms(pair, also):
    mine, theirs = chunks(pair)
    count, size, _ = mine.shape
    shape = jax.ShapeDtypeStruct((count, size + also.shape[1], CHAN), jnp.bfloat16)
    held = [pltpu.VMEM(shape.shape, jnp.bfloat16), pltpu.SemaphoreType.DMA((1,))]
    return call(join_kernel, shape, held, mine.size, mine, theirs, also, out_space=HBM)


def reduce_kernel(size, parts_ref, out_ref, held, done):
    count = parts_ref.shape[0]
    dealt = parts_ref.shape[1] - size
    total = [parts_ref[n].astype(jnp.float32) for n in (0, count // 2)]
    for n in range(1, count // 2):
        total[0] = total[0] + parts_ref[n].astype(jnp.float32)
        total[1] = total[1] + parts_ref[count // 2 + n].astype(jnp.float32)
    held[:size] = (total[0][:size] + total[1][:size]).astype(jnp.bfloat16)
    held[size : size + dealt] = total[0][size:].astype(jnp.bfloat16)
    held[size + dealt :] = total[1][size:].astype(jnp.bfloat16)
    copy_all([(held, out_ref.at[n]) for n in range(count)], done)


def finish_kernel(size, scale, whole_ref, one_ref, two_ref, held_one, held_two, done):
    count = whole_ref.shape[0]
    dealt = (whole_ref.shape[1] - size) // 2
    lines = two_ref.shape[1]
    held_one[...] = whole_ref[:, :size].astype(jnp.float32) * scale
    first = pltpu.make_async_copy(held_one, one_ref, done.at[0])
    first.start()
    for side in range(2):
        for n in range(count):
            start, end = n * dealt, min((n + 1) * dealt, lines)
            if end > start:
                row = size + side * dealt
                part = whole_ref[n, row : row + dealt].astype(jnp.float32) * scale
                held_two[side, start:end] = part[: end - start]
    second = pltpu.make_async_copy(held_two, two_ref, done.at[1])
    second.start()
    first.wait()
    second.wait()


def summed_over_az(joined, size, scale):
    count, both, _ = joined.shape
    dealt = both - size
    held = [pltpu.VMEM((size + 2 * dealt, CHAN), jnp.bfloat16), pltpu.SemaphoreType.DMA((count,))]
    shape = jax.ShapeDtypeStruct((count, size + 2 * dealt, CHAN), jnp.bfloat16)
    copies = call(
        functools.partial(reduce_kernel, size),
        shape,
        held,
        joined.size,
        exchange(joined, AZ),
        out_space=HBM,
    )
    one = (count, size, CHAN)
    two = (2, count * size // 2, CHAN)
    banks = call(
        functools.partial(finish_kernel, size, scale),
        (jax.ShapeDtypeStruct(one, jnp.float32), jax.ShapeDtypeStruct(two, jnp.float32)),
        [
            pltpu.VMEM(one, jnp.float32),
            pltpu.VMEM(two, jnp.float32),
            pltpu.SemaphoreType.DMA((2,)),
        ],
        joined.size,
        exchange(copies, AZ),
        out_space=HBM,
        room=52,
    )
    return tuple(bank.reshape(1, 3, 3, CHAN, CHAN) for bank in banks)


def lanes_kernel(*refs):
    given, (grad_ref, pre_ref, feats_ref, away_ref, up_ref, down_ref) = refs[:4], refs[4:10]
    held, done = refs[10:14], refs[14]
    _, core = here()
    half = feats_ref.shape[0]
    copy_all(zip(given, held), done)
    inputs_ref, pre_one_ref, pre_two_ref, cotangent_ref = held
    for row in range(ROWS):
        lanes = slice(row * CHAN, (row + 1) * CHAN)
        pre = pre_one_ref[0, row]
        wide = pre.astype(jnp.float32)
        grad = cotangent_ref[0, row].astype(jnp.float32) * slope(
            pre_two_ref[0, row].astype(jnp.float32)
        )
        grad = grad.astype(jnp.bfloat16)
        grad_ref[:, lanes] = grad
        pre_ref[:, lanes] = pre
        act = (wide / (1.0 + jnp.exp(-wide))).astype(jnp.bfloat16)
        for first, field in ((0, act), (WIDE, inputs_ref[0, row])):
            low, high = field[:half], field[half:]
            place = slice(first + row * CHAN, first + (row + 1) * CHAN)
            feats_ref[:, place] = jnp.where(core == 0, low, high)
            away_ref[:, place] = jnp.where(core == 0, high, low)
        grad = grad.astype(jnp.float32)
        pad = jnp.zeros((5, CHAN), jnp.float32)
        up_ref[:, lanes] = jnp.concatenate([grad[-2:], wide[-1:], pad]).astype(jnp.bfloat16)
        down_ref[:, lanes] = jnp.concatenate([grad[:2], wide[:1], pad]).astype(jnp.bfloat16)


def rims_kernel(grad_ref, low_ref, high_ref, out_ref, grad_rim, held, done):
    columns = grad_ref.shape[0]
    rows = out_ref.shape[1]
    grad_rim[:2] = low_ref[...].astype(jnp.float32)[:2]
    grad_rim[2 : 2 + columns] = grad_ref[...].astype(jnp.float32)
    grad_rim[2 + columns :] = jnp.zeros((grad_rim.shape[0] - 2 - columns, WIDE), jnp.float32)
    grad_rim[2 + columns : 4 + columns] = high_ref[...].astype(jnp.float32)[:2]
    for n in range(2):
        first = n * columns // 2
        held[n] = grad_rim[first : first + rows].astype(jnp.bfloat16)
    copy_all([(held.at[n % 2], out_ref.at[n]) for n in range(out_ref.shape[0])], done)


def pre_kernel(pre_ref, low_ref, high_ref, mine_ref, partner_ref, pre_rim):
    _, core = here()
    columns = pre_ref.shape[0]
    half = columns // 2
    rows = mine_ref.shape[0]
    pre_rim[...] = jnp.zeros_like(pre_rim)
    pre_rim[:1] = low_ref[...].astype(jnp.float32)[2:3]
    pre_rim[1 : 1 + columns] = pre_ref[...].astype(jnp.float32)
    pre_rim[1 + columns : 2 + columns] = high_ref[...].astype(jnp.float32)[2:3]
    left = pre_rim[:rows].astype(jnp.bfloat16)
    right = pre_rim[half : half + rows].astype(jnp.bfloat16)
    mine_ref[...] = jnp.where(core == 0, left, right)
    partner_ref[...] = jnp.where(core == 0, right, left)


def shards(inputs, pre_one, pre_two, cotangent, filt_one, filt_two):
    columns = inputs.shape[2]
    half = columns // 2
    core = lax.axis_index(CORE)
    az_count = lax.axis_size(AZ)
    rot_count = lax.axis_size(ROT)
    chips = lax.axis_size(CHIPS)
    cell_count = rot_count * inputs.shape[1] * columns * az_count
    scale = cell_count ** (-0.5)
    padded = half + 8

    def narrow(*shape):
        return jax.ShapeDtypeStruct(shape, jnp.bfloat16)

    grad_two, pre, feats, feats_away, up, down = call(
        lanes_kernel,
        (
            narrow(columns, WIDE),
            narrow(columns, WIDE),
            narrow(half, 2 * WIDE),
            narrow(half, 2 * WIDE),
            narrow(8, WIDE),
            narrow(8, WIDE),
        ),
        [pltpu.VMEM(inputs.shape, jnp.bfloat16)] * 4 + [pltpu.SemaphoreType.DMA((4,))],
        inputs.size * 20,
        inputs,
        pre_one,
        pre_two,
        cotangent,
        space=HBM,
        room=60,
    )
    forward = [(i, (i + 1) % az_count) for i in range(az_count)]
    backward = [(target, source) for source, target in forward]
    low = lax.ppermute(up, AZ, forward)
    high = lax.ppermute(down, AZ, backward)
    rim = pltpu.VMEM((columns + 8, WIDE), jnp.float32)
    sent = call(
        rims_kernel,
        narrow(rot_count, padded, WIDE),
        [
            rim,
            pltpu.VMEM((2, padded, WIDE), jnp.bfloat16),
            pltpu.SemaphoreType.DMA((rot_count,)),
        ],
        inputs.size * 20,
        grad_two,
        low,
        high,
        out_space=HBM,
    )
    all_grad_two = exchange(sent, ROT)

    pre_here, pre_away = call(
        pre_kernel,
        (narrow(padded, WIDE), narrow(padded, WIDE)),
        [rim],
        inputs.size,
        pre,
        low,
        high,
    )

    pair = jnp.stack([feats, lax.ppermute(feats_away, CORE, SWAP)])
    chip_pair = jnp.stack([pair, lax.ppermute(pair, CHIPS[1], SWAP)])
    along_x = lax.axis_size(CHIPS[0])
    all_feats = [chip_pair] + [
        lax.ppermute(chip_pair, CHIPS[0], [(i, (i + step) % along_x) for i in range(along_x)])
        for step in range(1, along_x)
    ]
    other_two = lax.ppermute(filt_two[0], CORE, SWAP)
    other_one = lax.ppermute(filt_one[0], CORE, SWAP)
    pre_partner = lax.ppermute(pre_away, CORE, SWAP)
    bands_two = bands(filt_two[0], other_two)
    bands_one = bands(filt_one[0], other_one)

    shares = conv(
        conv_two_kernel,
        after(all_grad_two, chip_pair),
        bands_two,
        half + 2,
        padded,
        (chips, padded, 2 * WIDE),
        [
            pltpu.VMEM((chips, padded, 2 * WIDE), jnp.bfloat16),
            pltpu.SemaphoreType.DMA((chips,)),
        ],
        HBM,
        52,
    )
    pair_two = filter_terms(all_feats, 0, half, all_grad_two, 3)
    leave, terms_two = half_terms(pair_two)
    arrived = after(exchange(shares, CHIPS), leave)
    copies = call(
        point_kernel,
        narrow(chips, padded, 2 * WIDE),
        [pltpu.VMEM((padded, 2 * WIDE), jnp.bfloat16), pltpu.SemaphoreType.DMA((chips,))],
        arrived.size,
        arrived,
        pre_here,
        pre_partner,
        out_space=HBM,
    )
    all_grad_one = after(exchange(copies, CHIPS), terms_two)
    joined = joined_terms(filter_terms(all_feats, 1, half, all_grad_one, 2), terms_two)
    filt_grad_one, filt_grad_two = summed_over_az(joined, filt_one.size // CHAN // az_count, scale)

    shares = conv(
        conv_one_kernel,
        after(all_grad_one, joined),
        bands_one,
        half,
        half,
        (2, along_x, half, 2 * WIDE),
    )
    arrived_y = lax.ppermute(shares[1], CHIPS[1], SWAP)
    partial = (shares[0].astype(jnp.float32) + arrived_y.astype(jnp.float32)).astype(jnp.bfloat16)
    total = partial[0].astype(jnp.float32)
    for step in range(1, along_x):
        came = lax.ppermute(
            partial[step], CHIPS[0], [(i, (i + step) % along_x) for i in range(along_x)]
        )
        total = total + came.astype(jnp.float32)
    total = total.astype(jnp.bfloat16)
    left, right = total[:, :WIDE], total[:, WIDE:]
    mine = jnp.where(core == 0, left, right)
    theirs = lax.ppermute(jnp.where(core == 0, right, left), CORE, SWAP)
    whole = jnp.where(core == 0, jnp.concatenate([mine, theirs]), jnp.concatenate([theirs, mine]))
    input_grad = jnp.moveaxis(whole.reshape(columns, ROWS, CHAN), 1, 0)[None]
    return input_grad, filt_grad_one, filt_grad_two


def solution(mesh):
    finer = Mesh(mesh.devices.reshape(4, 2, 2, mesh.shape["az"]), (*ROT, AZ))
    field = P(ROT, None, AZ, None)
    bank = P(ROT, None, None, None, None)
    return jax.shard_map(
        shards,
        mesh=finer,
        in_specs=(field, field, field, field, bank, bank),
        out_specs=(field, bank, bank),
        check_vma=False,
    )
```

```python
import functools

import jax
import jax.numpy as jnp
from jax import lax
from jax.experimental import pallas as pl
from jax.experimental.pallas import tpu as pltpu
from jax.sharding import Mesh
from jax.sharding import PartitionSpec as P

CHIPS = ("rot_x", "rot_y")
CORE = "rot_c"
ROT = (*CHIPS, CORE)
AZ = "az"

ROWS = 4
CHAN = 128
WIDE = ROWS * CHAN
SWAP = [(0, 1), (1, 0)]
VMEM = pl.BlockSpec(memory_space=pltpu.VMEM)
HBM = pl.BlockSpec(memory_space=pltpu.HBM)


def slope(pre):
    logistic = 1.0 / (1.0 + jnp.exp(-pre))
    return logistic * (1.0 + pre * (1.0 - logistic))


def params(mebibytes):
    return pltpu.CompilerParams(vmem_limit_bytes=mebibytes * 1024 * 1024)


def here():
    return lax.axis_index(CHIPS[0]) * 2 + lax.axis_index(CHIPS[1]), lax.axis_index(CORE)


def call(kernel, out_shape, scratch, flops, *operands, space=VMEM, out_space=VMEM, room=40):
    n_bytes = sum(a.size * a.dtype.itemsize for a in operands)
    in_specs = list(space) if isinstance(space, tuple) else [space] * len(operands)
    out_specs = out_space
    if not isinstance(out_space, tuple):
        out_specs = jax.tree.map(lambda _: out_space, out_shape)
    return pl.pallas_call(
        kernel,
        out_shape=out_shape,
        in_specs=in_specs,
        out_specs=out_specs,
        scratch_shapes=scratch,
        compiler_params=params(room),
        cost_estimate=pl.CostEstimate(flops=flops, bytes_accessed=2 * n_bytes, transcendentals=0),
    )(*operands)


def copy_all(pairs, done):
    copies = [pltpu.make_async_copy(a, b, done.at[n]) for n, (a, b) in enumerate(pairs)]
    for copy in copies:
        copy.start()
    for copy in copies:
        copy.wait()


def interleave(blocks_ref, rows_ref, orients, first, shift):
    for g in range(orients):
        s = (g - shift) % orients
        lanes = slice((s % 2) * WIDE, (s % 2 + 1) * WIDE)
        rows_ref[:, g, :] = blocks_ref[s // 2, first:, lanes].astype(jnp.float32)


def band_weights(filt_ref, band_ref, slot):
    zero = jnp.zeros((CHAN, CHAN), jnp.bfloat16)
    for j in range(3):
        for out_row in range(ROWS):
            for in_row in range(ROWS):
                i = out_row - in_row + 1
                piece = filt_ref[i, j] if 0 <= i < 3 else zero
                band_ref[
                    slot,
                    j,
                    out_row * CHAN : (out_row + 1) * CHAN,
                    in_row * CHAN : (in_row + 1) * CHAN,
                ] = piece


def bands_kernel(mine_ref, other_ref, band_ref):
    _, core = here()
    band_weights(mine_ref, band_ref, core)
    band_weights(other_ref, band_ref, 1 - core)


def bands(mine, other):
    shape = jax.ShapeDtypeStruct((2, 3, WIDE, WIDE), jnp.bfloat16)
    return call(bands_kernel, shape, [], mine.size, mine, other)


def rotation_sums(orients, width, blocks_ref, band_ref, rows_0, rows_1, band, fetched):
    in_width = rows_0.shape[0]
    copies = [
        pltpu.make_async_copy(band_ref.at[n], band.at[n], fetched.at[n]) for n in range(2)
    ]
    for copy in copies:
        copy.start()
    first = blocks_ref.shape[1] - in_width
    interleave(blocks_ref, rows_0, orients, first, 0)
    interleave(blocks_ref, rows_1, orients, first, 1)
    total = None
    for slot, rows in ((0, rows_0), (1, rows_1)):
        copies[slot].wait()
        flat = rows[...].reshape(in_width * orients, WIDE).astype(jnp.bfloat16)
        for j in range(3):
            window = flat[(2 - j) * orients : (2 - j + width) * orients]
            term = lax.dot_general(
                window,
                band[slot, j],
                (((1,), (1,)), ((), ())),
                preferred_element_type=jnp.float32,
            )
            total = term if total is None else total + term
    return total.reshape(width, orients, WIDE)


def conv_two_kernel(orients, width, blocks_ref, band_ref, out_ref, *scratch):
    *rows, sums, held, done = scratch
    chip, _ = here()
    total = rotation_sums(orients, width, blocks_ref, band_ref, *rows)
    sums[width:] = jnp.zeros((sums.shape[0] - width, orients, WIDE), jnp.float32)
    sums[:width] = total
    chips = orients // 2
    copies = []
    for pair in range(chips):
        for half in range(2):
            held[pair, :, half * WIDE : (half + 1) * WIDE] = sums[:, 2 * pair + half, :].astype(
                jnp.bfloat16
            )
        to = lax.rem(pair + chip, chips)
        copies.append(pltpu.make_async_copy(held.at[pair], out_ref.at[to], done.at[pair]))
        copies[-1].start()
    for copy in copies:
        copy.wait()


def conv_one_kernel(orients, width, blocks_ref, band_ref, out_ref, *scratch):
    *rows, sums = scratch
    chip, _ = here()
    sums[...] = rotation_sums(orients, width, blocks_ref, band_ref, *rows)
    chips = orients // 2
    across = out_ref.shape[1]
    for pair in range(chips):
        to = lax.rem(pair + chip, chips)
        other = lax.rem(to + chip, 2)
        step = lax.rem(to // 2 - chip // 2 + across, across)
        for half in range(2):
            out_ref[other, step, :, half * WIDE : (half + 1) * WIDE] = sums[
                :, 2 * pair + half, :
            ].astype(jnp.bfloat16)


def conv(kernel, blocks, in_width, band, width, padded, out_shape, staging=(), out_space=VMEM, room=40):
    orients = 2 * blocks.shape[0]
    return call(
        functools.partial(kernel, orients, width),
        jax.ShapeDtypeStruct(out_shape, jnp.bfloat16),
        [
            pltpu.VMEM((in_width, orients, WIDE), jnp.float32),
            pltpu.VMEM((in_width, orients, WIDE), jnp.float32),
            pltpu.VMEM(band.shape, jnp.bfloat16),
            pltpu.SemaphoreType.DMA((2,)),
            pltpu.VMEM((padded, orients, WIDE), jnp.float32),
            *staging,
        ],
        2 * 6 * width * orients * WIDE * WIDE,
        blocks,
        band,
        space=(VMEM, HBM),
        out_space=out_space,
        room=room,
    )


def filter_kernel(
    orients, width, field, first, own, grad_ref, feat_ref, out_ref, feat_rows, grad_rows, held, done
):
    chip, core = here()
    slot = core if own else 1 - core
    in_width = grad_rows.shape[0]
    copies = [
        pltpu.make_async_copy(
            feat_ref.at[:, pl.ds(field * width, width), pl.ds(half * WIDE, WIDE)],
            held.at[:, half],
            done.at[half],
        )
        for half in range(2)
    ]
    for copy in copies:
        copy.start()
    interleave(grad_ref, grad_rows, orients, grad_ref.shape[1] - in_width, 0)
    grads = grad_rows[...].reshape(in_width * orients, WIDE).astype(jnp.bfloat16)
    for copy in copies:
        copy.wait()
    for g in range(orients):
        s = lax.rem(g + 2 * chip + slot, orients)
        feat_rows[:, g, :] = held[s // 2, lax.rem(s, 2)].astype(jnp.float32)
    feats = feat_rows[...].reshape(width * orients, WIDE).astype(jnp.bfloat16)
    for j in range(3):
        window = grads[(first - j) * orients : (first - j + width) * orients]
        product = lax.dot_general(
            feats,
            window,
            (((0,), (0,)), ((), ())),
            preferred_element_type=jnp.float32,
        )
        for i in range(3):
            total = None
            for row in range(ROWS):
                grad_row = row - i + 1
                if not 0 <= grad_row < ROWS:
                    continue
                piece = product[
                    row * CHAN : (row + 1) * CHAN, grad_row * CHAN : (grad_row + 1) * CHAN
                ]
                total = piece if total is None else total + piece
            out_ref[i, j] = total.astype(jnp.bfloat16)


def filter_terms(feats, field, width, grads, in_width, first):
    orients = 2 * feats.shape[0]

    def terms(own):
        return call(
            functools.partial(filter_kernel, orients, width, field, first, own),
            jax.ShapeDtypeStruct((3, 3, CHAN, CHAN), jnp.bfloat16),
            [
                pltpu.VMEM((width, orients, WIDE), jnp.float32),
                pltpu.VMEM((in_width, orients, WIDE), jnp.float32),
                pltpu.VMEM((orients // 2, 2, width, WIDE), jnp.bfloat16),
                pltpu.SemaphoreType.DMA((2,)),
            ],
            6 * width * orients * WIDE * WIDE,
            grads,
            feats,
            space=(VMEM, HBM),
            room=52,
        )

    theirs = lax.ppermute(terms(False), CORE, SWAP)
    return terms(True), theirs


def point_kernel(parts_ref, pre_ref, out_ref, held, done):
    total = parts_ref[0].astype(jnp.float32)
    for n in range(1, parts_ref.shape[0]):
        total = total + parts_ref[n].astype(jnp.float32)
    held[...] = (total * slope(pre_ref[...].astype(jnp.float32))).astype(jnp.bfloat16)
    copy_all([(held, out_ref.at[n]) for n in range(out_ref.shape[0])], done)


def exchange(parts, axes):
    return lax.all_to_all(parts, axes, 0, 0, tiled=True)


def chunks(pair):
    count = lax.axis_size(AZ)
    return [bank.reshape(count, -1, CHAN) for bank in pair]


def after(array, first):
    return lax.optimization_barrier((array, first))[0]


def halves_kernel(mine, theirs, stay_ref, leave_ref, both_ref):
    half = stay_ref.shape[0]
    side = lax.axis_index(AZ) // half
    both_ref[...] = mine[...].astype(jnp.float32) + theirs[...].astype(jnp.float32)
    stay_ref[...] = both_ref[pl.ds(side * half, half)].astype(jnp.bfloat16)
    leave_ref[...] = both_ref[pl.ds((1 - side) * half, half)].astype(jnp.bfloat16)


def deal_kernel(stay, came, out_ref):
    both = stay[...].astype(jnp.float32) + came[...].astype(jnp.float32)
    lines = both.reshape(-1, CHAN)
    count, size, _ = out_ref.shape
    lines = jnp.concatenate([lines, jnp.zeros((count * size - lines.shape[0], CHAN), jnp.float32)])
    out_ref[...] = lines.reshape(out_ref.shape).astype(jnp.bfloat16)


def half_terms(pair):
    mine, theirs = chunks(pair)
    count, size, _ = mine.shape
    half = jax.ShapeDtypeStruct((count // 2, size, CHAN), jnp.bfloat16)
    both = pltpu.VMEM(mine.shape, jnp.float32)
    stay, leave = call(halves_kernel, (half, half), [both], mine.size, mine, theirs)
    came = lax.ppermute(leave, AZ, [(i, (i + count // 2) % count) for i in range(count)])
    dealt = -(-size // 16) * 8
    shape = jax.ShapeDtypeStruct((count, dealt, CHAN), jnp.bfloat16)
    return leave, call(deal_kernel, shape, [], mine.size, stay, came)


def join_kernel(mine, theirs, also, out_ref, held, done):
    size = mine.shape[1]
    both = mine[...].astype(jnp.float32) + theirs[...].astype(jnp.float32)
    held[:, :size] = both.astype(jnp.bfloat16)
    held[:, size:] = also[...]
    copy_all([(held, out_ref)], done)


def joined_terms(pair, also):
    mine, theirs = chunks(pair)
    count, size, _ = mine.shape
    shape = jax.ShapeDtypeStruct((count, size + also.shape[1], CHAN), jnp.bfloat16)
    held = [pltpu.VMEM(shape.shape, jnp.bfloat16), pltpu.SemaphoreType.DMA((1,))]
    return call(join_kernel, shape, held, mine.size, mine, theirs, also, out_space=HBM)


def reduce_kernel(size, parts_ref, out_ref, held, done):
    count = parts_ref.shape[0]
    dealt = parts_ref.shape[1] - size
    total = [parts_ref[n].astype(jnp.float32) for n in (0, count // 2)]
    for n in range(1, count // 2):
        total[0] = total[0] + parts_ref[n].astype(jnp.float32)
        total[1] = total[1] + parts_ref[count // 2 + n].astype(jnp.float32)
    held[:size] = (total[0][:size] + total[1][:size]).astype(jnp.bfloat16)
    held[size : size + dealt] = total[0][size:].astype(jnp.bfloat16)
    held[size + dealt :] = total[1][size:].astype(jnp.bfloat16)
    copy_all([(held, out_ref.at[n]) for n in range(count)], done)


def finish_kernel(size, scale, whole_ref, one_ref, two_ref, held_one, held_two, done):
    count = whole_ref.shape[0]
    dealt = (whole_ref.shape[1] - size) // 2
    lines = two_ref.shape[1]
    held_one[...] = whole_ref[:, :size].astype(jnp.float32) * scale
    first = pltpu.make_async_copy(held_one, one_ref, done.at[0])
    first.start()
    for side in range(2):
        for n in range(count):
            start, end = n * dealt, min((n + 1) * dealt, lines)
            if end > start:
                row = size + side * dealt
                part = whole_ref[n, row : row + dealt].astype(jnp.float32) * scale
                held_two[side, start:end] = part[: end - start]
    second = pltpu.make_async_copy(held_two, two_ref, done.at[1])
    second.start()
    first.wait()
    second.wait()


def summed_over_az(joined, size, scale):
    count, both, _ = joined.shape
    dealt = both - size
    held = [pltpu.VMEM((size + 2 * dealt, CHAN), jnp.bfloat16), pltpu.SemaphoreType.DMA((count,))]
    shape = jax.ShapeDtypeStruct((count, size + 2 * dealt, CHAN), jnp.bfloat16)
    copies = call(
        functools.partial(reduce_kernel, size),
        shape,
        held,
        joined.size,
        exchange(joined, AZ),
        out_space=HBM,
    )
    one = (count, size, CHAN)
    two = (2, count * size // 2, CHAN)
    banks = call(
        functools.partial(finish_kernel, size, scale),
        (jax.ShapeDtypeStruct(one, jnp.float32), jax.ShapeDtypeStruct(two, jnp.float32)),
        [
            pltpu.VMEM(one, jnp.float32),
            pltpu.VMEM(two, jnp.float32),
            pltpu.SemaphoreType.DMA((2,)),
        ],
        joined.size,
        exchange(copies, AZ),
        out_space=HBM,
        room=52,
    )
    return tuple(bank.reshape(1, 3, 3, CHAN, CHAN) for bank in banks)


def stacked(act, given, grad, pre, side):
    half = act.shape[0] // 2
    zeros = jnp.zeros((8, CHAN), jnp.float32)
    if side == 0:
        grad = [zeros[:2], grad[: half + 2], zeros[:4]]
        pre = [zeros[:1], pre[: half + 1], zeros[:6]]
    else:
        grad = [grad[half - 2 :], zeros[:6]]
        pre = [pre[half - 1 :], zeros[:7]]
    own = slice(side * half, (side + 1) * half)
    return jnp.concatenate([act[own], given[own], *grad, *pre])


def lanes_kernel(*refs):
    given, (mine_ref, away_ref, same_ref, cross_ref) = refs[:4], refs[4:8]
    held, done = refs[8:12], refs[12]
    _, core = here()
    copy_all(zip(given, held), done)
    inputs_ref, pre_one_ref, pre_two_ref, cotangent_ref = held
    for row in range(ROWS):
        lanes = slice(row * CHAN, (row + 1) * CHAN)
        pre = pre_one_ref[0, row].astype(jnp.float32)
        grad = cotangent_ref[0, row].astype(jnp.float32) * slope(
            pre_two_ref[0, row].astype(jnp.float32)
        )
        act = pre / (1.0 + jnp.exp(-pre))
        fields = (act, inputs_ref[0, row].astype(jnp.float32), grad, pre)
        left, right = stacked(*fields, 0), stacked(*fields, 1)
        mine_ref[:, lanes] = jnp.where(core == 0, left, right).astype(jnp.bfloat16)
        away_ref[:, lanes] = jnp.where(core == 0, right, left).astype(jnp.bfloat16)
        pad = jnp.zeros((5, CHAN), jnp.float32)
        low = jnp.concatenate([grad[:2], pre[:1], pad])
        high = jnp.concatenate([grad[-2:], pre[-1:], pad])
        same_ref[:, lanes] = jnp.where(core == 0, high, low).astype(jnp.bfloat16)
        cross_ref[:, lanes] = jnp.where(core == 0, low, high).astype(jnp.bfloat16)


def rims_kernel(mine_ref, partner_ref, same_ref, cross_ref, out_ref, pre_ref, held, done):
    _, core = here()
    ahead = held.shape[0] - pre_ref.shape[0]
    rows = pre_ref.shape[0]
    used = rows - 8
    at = lax.broadcasted_iota(jnp.int32, (rows, WIDE), 0)
    grad_at = jnp.where(core == 0, 0, used + 2)
    pre_at = jnp.where(core == 0, 0, used + 1)
    filled = []
    for body_ref, edge_ref in ((mine_ref, same_ref), (partner_ref, cross_ref)):
        body = body_ref[...].astype(jnp.float32)
        edge = edge_ref[...].astype(jnp.float32)
        grad = body[ahead : ahead + rows]
        grad = jnp.where(at == grad_at, edge[0:1], grad)
        grad = jnp.where(at == grad_at + 1, edge[1:2], grad)
        pre = jnp.where(at == pre_at, edge[2:3], body[ahead + rows :])
        filled.append(jnp.concatenate([body[:ahead], grad, pre]).astype(jnp.bfloat16))
    first = jnp.where(core == 0, filled[0], filled[1])
    second = jnp.where(core == 0, filled[1], filled[0])
    for lanes, part in ((slice(0, WIDE), first), (slice(WIDE, 2 * WIDE), second)):
        held[:, lanes] = part[: ahead + rows]
        pre_ref[:, lanes] = part[ahead + rows :]
    copy_all([(held, out_ref.at[n]) for n in range(out_ref.shape[0])], done)


def shards(inputs, pre_one, pre_two, cotangent, filt_one, filt_two):
    columns = inputs.shape[2]
    half = columns // 2
    core = lax.axis_index(CORE)
    az_count = lax.axis_size(AZ)
    rot_count = lax.axis_size(ROT)
    chips = lax.axis_size(CHIPS)
    cell_count = rot_count * inputs.shape[1] * columns * az_count
    scale = cell_count ** (-0.5)
    padded = half + 8

    def narrow(*shape):
        return jax.ShapeDtypeStruct(shape, jnp.bfloat16)

    rows = columns + 2 * padded
    mine, away, same, cross = call(
        lanes_kernel,
        (narrow(rows, WIDE), narrow(rows, WIDE), narrow(8, WIDE), narrow(8, WIDE)),
        [pltpu.VMEM(inputs.shape, jnp.bfloat16)] * 4 + [pltpu.SemaphoreType.DMA((4,))],
        inputs.size * 20,
        inputs,
        pre_one,
        pre_two,
        cotangent,
        space=HBM,
        room=60,
    )
    after_me = [(i, (i + 1) % az_count) for i in range(az_count)]
    before_me = [(i, (i - 1) % az_count) for i in range(az_count)]
    place = lambda c, pairs, d: [(c * az_count + i, d * az_count + j) for i, j in pairs]
    same = lax.ppermute(same, (CORE, AZ), place(0, after_me, 0) + place(1, before_me, 1))
    cross = lax.ppermute(cross, (CORE, AZ), place(1, after_me, 0) + place(0, before_me, 1))
    partner = lax.ppermute(away, CORE, SWAP)
    sent, pre_pair = call(
        rims_kernel,
        (narrow(chips, columns + padded, 2 * WIDE), narrow(padded, 2 * WIDE)),
        [
            pltpu.VMEM((columns + padded, 2 * WIDE), jnp.bfloat16),
            pltpu.SemaphoreType.DMA((chips,)),
        ],
        inputs.size * 20,
        mine,
        partner,
        same,
        cross,
        out_space=(HBM, VMEM),
    )
    first_blocks = exchange(sent, CHIPS)

    other_two = lax.ppermute(filt_two[0], CORE, SWAP)
    other_one = lax.ppermute(filt_one[0], CORE, SWAP)
    bands_two = bands(filt_two[0], other_two)
    bands_one = bands(filt_one[0], other_one)

    shares = conv(
        conv_two_kernel,
        first_blocks,
        padded,
        bands_two,
        half + 2,
        padded,
        (chips, padded, 2 * WIDE),
        [
            pltpu.VMEM((chips, padded, 2 * WIDE), jnp.bfloat16),
            pltpu.SemaphoreType.DMA((chips,)),
        ],
        HBM,
        52,
    )
    pair_two = filter_terms(first_blocks, 0, half, first_blocks, padded, 3)
    leave, terms_two = half_terms(pair_two)
    arrived = after(exchange(shares, CHIPS), leave)
    copies = call(
        point_kernel,
        narrow(chips, padded, 2 * WIDE),
        [pltpu.VMEM((padded, 2 * WIDE), jnp.bfloat16), pltpu.SemaphoreType.DMA((chips,))],
        arrived.size,
        arrived,
        pre_pair,
        out_space=HBM,
    )
    all_grad_one = after(exchange(copies, CHIPS), terms_two)
    joined = joined_terms(filter_terms(first_blocks, 1, half, all_grad_one, padded, 2), terms_two)
    filt_grad_one, filt_grad_two = summed_over_az(joined, filt_one.size // CHAN // az_count, scale)

    along_x = lax.axis_size(CHIPS[0])

    shares = conv(
        conv_one_kernel,
        after(all_grad_one, joined),
        padded,
        bands_one,
        half,
        half,
        (2, along_x, half, 2 * WIDE),
    )
    arrived_y = lax.ppermute(shares[1], CHIPS[1], SWAP)
    partial = (shares[0].astype(jnp.float32) + arrived_y.astype(jnp.float32)).astype(jnp.bfloat16)
    total = partial[0].astype(jnp.float32)
    for step in range(1, along_x):
        came = lax.ppermute(
            partial[step], CHIPS[0], [(i, (i + step) % along_x) for i in range(along_x)]
        )
        total = total + came.astype(jnp.float32)
    total = total.astype(jnp.bfloat16)
    left, right = total[:, :WIDE], total[:, WIDE:]
    mine = jnp.where(core == 0, left, right)
    theirs = lax.ppermute(jnp.where(core == 0, right, left), CORE, SWAP)
    whole = jnp.where(core == 0, jnp.concatenate([mine, theirs]), jnp.concatenate([theirs, mine]))
    input_grad = jnp.moveaxis(whole.reshape(columns, ROWS, CHAN), 1, 0)[None]
    return input_grad, filt_grad_one, filt_grad_two


def solution(mesh):
    finer = Mesh(mesh.devices.reshape(4, 2, 2, mesh.shape["az"]), (*ROT, AZ))
    field = P(ROT, None, AZ, None)
    bank = P(ROT, None, None, None, None)
    return jax.shard_map(
        shards,
        mesh=finer,
        in_specs=(field, field, field, field, bank, bank),
        out_specs=(field, bank, bank),
        check_vma=False,
    )
```

```python
import functools

import jax
import jax.numpy as jnp
from jax import lax
from jax.experimental import pallas as pl
from jax.experimental.pallas import tpu as pltpu
from jax.sharding import Mesh
from jax.sharding import PartitionSpec as P

CHIPS = ("rot_x", "rot_y")
CORE = "rot_c"
ROT = (*CHIPS, CORE)
AZ = "az"

ROWS = 4
CHAN = 128
WIDE = ROWS * CHAN
SWAP = [(0, 1), (1, 0)]
VMEM = pl.BlockSpec(memory_space=pltpu.VMEM)
HBM = pl.BlockSpec(memory_space=pltpu.HBM)


def slope(pre):
    logistic = 1.0 / (1.0 + jnp.exp(-pre))
    return logistic * (1.0 + pre * (1.0 - logistic))


def params(mebibytes):
    return pltpu.CompilerParams(vmem_limit_bytes=mebibytes * 1024 * 1024)


def here():
    return lax.axis_index(CHIPS[0]) * 2 + lax.axis_index(CHIPS[1]), lax.axis_index(CORE)


def call(kernel, out_shape, scratch, flops, *operands, space=VMEM, out_space=VMEM, room=40):
    n_bytes = sum(a.size * a.dtype.itemsize for a in operands)
    in_specs = list(space) if isinstance(space, tuple) else [space] * len(operands)
    out_specs = out_space
    if not isinstance(out_space, tuple):
        out_specs = jax.tree.map(lambda _: out_space, out_shape)
    return pl.pallas_call(
        kernel,
        out_shape=out_shape,
        in_specs=in_specs,
        out_specs=out_specs,
        scratch_shapes=scratch,
        compiler_params=params(room),
        cost_estimate=pl.CostEstimate(flops=flops, bytes_accessed=2 * n_bytes, transcendentals=0),
    )(*operands)


def copy_all(pairs, done):
    copies = [pltpu.make_async_copy(a, b, done.at[n]) for n, (a, b) in enumerate(pairs)]
    for copy in copies:
        copy.start()
    for copy in copies:
        copy.wait()


def interleave(blocks_ref, rows_ref, orients, first, shift):
    for g in range(orients):
        s = (g - shift) % orients
        lanes = slice((s % 2) * WIDE, (s % 2 + 1) * WIDE)
        rows_ref[:, g, :] = blocks_ref[s // 2, first:, lanes].astype(jnp.float32)


def band_weights(filt_ref, band_ref, slot):
    zero = jnp.zeros((CHAN, CHAN), jnp.bfloat16)
    for j in range(3):
        for out_row in range(ROWS):
            for in_row in range(ROWS):
                i = out_row - in_row + 1
                piece = filt_ref[i, j] if 0 <= i < 3 else zero
                band_ref[
                    slot,
                    j,
                    out_row * CHAN : (out_row + 1) * CHAN,
                    in_row * CHAN : (in_row + 1) * CHAN,
                ] = piece


def rotation_sums(orients, width, blocks_ref, mine_ref, other_ref, rows_0, rows_1, band):
    in_width = rows_0.shape[0]
    _, core = here()
    band_weights(mine_ref, band, core)
    band_weights(other_ref, band, 1 - core)
    first = blocks_ref.shape[1] - in_width
    interleave(blocks_ref, rows_0, orients, first, 0)
    interleave(blocks_ref, rows_1, orients, first, 1)
    total = None
    for slot, rows in ((0, rows_0), (1, rows_1)):
        flat = rows[...].reshape(in_width * orients, WIDE).astype(jnp.bfloat16)
        for j in range(3):
            window = flat[(2 - j) * orients : (2 - j + width) * orients]
            term = lax.dot_general(
                window,
                band[slot, j],
                (((1,), (1,)), ((), ())),
                preferred_element_type=jnp.float32,
            )
            total = term if total is None else total + term
    return total.reshape(width, orients, WIDE)


def conv_two_kernel(orients, width, blocks_ref, mine_ref, other_ref, out_ref, *scratch):
    *rows, sums, held, done = scratch
    chip, _ = here()
    total = rotation_sums(orients, width, blocks_ref, mine_ref, other_ref, *rows)
    sums[width:] = jnp.zeros((sums.shape[0] - width, orients, WIDE), jnp.float32)
    sums[:width] = total
    chips = orients // 2
    copies = []
    for pair in range(chips):
        for half in range(2):
            held[pair, :, half * WIDE : (half + 1) * WIDE] = sums[:, 2 * pair + half, :].astype(
                jnp.bfloat16
            )
        to = lax.rem(pair + chip, chips)
        copies.append(pltpu.make_async_copy(held.at[pair], out_ref.at[to], done.at[pair]))
        copies[-1].start()
    for copy in copies:
        copy.wait()


def conv_one_kernel(orients, width, blocks_ref, mine_ref, other_ref, out_ref, *scratch):
    *rows, sums = scratch
    chip, _ = here()
    sums[...] = rotation_sums(orients, width, blocks_ref, mine_ref, other_ref, *rows)
    chips = orients // 2
    across = out_ref.shape[1]
    for pair in range(chips):
        to = lax.rem(pair + chip, chips)
        other = lax.rem(to + chip, 2)
        step = lax.rem(to // 2 - chip // 2 + across, across)
        for half in range(2):
            out_ref[other, step, :, half * WIDE : (half + 1) * WIDE] = sums[
                :, 2 * pair + half, :
            ].astype(jnp.bfloat16)


def conv(kernel, blocks, in_width, mine, other, width, padded, out_shape, staging=(), out_space=VMEM, room=40):
    orients = 2 * blocks.shape[0]
    return call(
        functools.partial(kernel, orients, width),
        jax.ShapeDtypeStruct(out_shape, jnp.bfloat16),
        [
            pltpu.VMEM((in_width, orients, WIDE), jnp.float32),
            pltpu.VMEM((in_width, orients, WIDE), jnp.float32),
            pltpu.VMEM((2, 3, WIDE, WIDE), jnp.bfloat16),
            pltpu.VMEM((padded, orients, WIDE), jnp.float32),
            *staging,
        ],
        2 * 6 * width * orients * WIDE * WIDE,
        blocks,
        mine,
        other,
        out_space=out_space,
        room=room,
    )


def filter_kernel(
    orients, width, field, first, own, grad_ref, feat_ref, out_ref, feat_rows, grad_rows, held, done
):
    chip, core = here()
    slot = core if own else 1 - core
    in_width = grad_rows.shape[0]
    copies = [
        pltpu.make_async_copy(
            feat_ref.at[:, pl.ds(field * width, width), pl.ds(half * WIDE, WIDE)],
            held.at[:, half],
            done.at[half],
        )
        for half in range(2)
    ]
    for copy in copies:
        copy.start()
    interleave(grad_ref, grad_rows, orients, grad_ref.shape[1] - in_width, 0)
    grads = grad_rows[...].reshape(in_width * orients, WIDE).astype(jnp.bfloat16)
    for copy in copies:
        copy.wait()
    for g in range(orients):
        s = lax.rem(g + 2 * chip + slot, orients)
        feat_rows[:, g, :] = held[s // 2, lax.rem(s, 2)].astype(jnp.float32)
    feats = feat_rows[...].reshape(width * orients, WIDE).astype(jnp.bfloat16)
    for j in range(3):
        window = grads[(first - j) * orients : (first - j + width) * orients]
        product = lax.dot_general(
            feats,
            window,
            (((0,), (0,)), ((), ())),
            preferred_element_type=jnp.float32,
        )
        for i in range(3):
            total = None
            for row in range(ROWS):
                grad_row = row - i + 1
                if not 0 <= grad_row < ROWS:
                    continue
                piece = product[
                    row * CHAN : (row + 1) * CHAN, grad_row * CHAN : (grad_row + 1) * CHAN
                ]
                total = piece if total is None else total + piece
            out_ref[i, j] = total.astype(jnp.bfloat16)


def filter_terms(feats, field, width, grads, in_width, first):
    orients = 2 * feats.shape[0]

    def terms(own):
        return call(
            functools.partial(filter_kernel, orients, width, field, first, own),
            jax.ShapeDtypeStruct((3, 3, CHAN, CHAN), jnp.bfloat16),
            [
                pltpu.VMEM((width, orients, WIDE), jnp.float32),
                pltpu.VMEM((in_width, orients, WIDE), jnp.float32),
                pltpu.VMEM((orients // 2, 2, width, WIDE), jnp.bfloat16),
                pltpu.SemaphoreType.DMA((2,)),
            ],
            6 * width * orients * WIDE * WIDE,
            grads,
            feats,
            space=(VMEM, HBM),
            room=52,
        )

    theirs = lax.ppermute(terms(False), CORE, SWAP)
    return terms(True), theirs


def point_kernel(parts_ref, pre_ref, out_ref, held, done):
    total = parts_ref[0].astype(jnp.float32)
    for n in range(1, parts_ref.shape[0]):
        total = total + parts_ref[n].astype(jnp.float32)
    held[...] = (total * slope(pre_ref[...].astype(jnp.float32))).astype(jnp.bfloat16)
    copy_all([(held, out_ref.at[n]) for n in range(out_ref.shape[0])], done)


def exchange(parts, axes):
    return lax.all_to_all(parts, axes, 0, 0, tiled=True)


def chunks(pair):
    count = lax.axis_size(AZ)
    return [bank.reshape(count, -1, CHAN) for bank in pair]


def after(array, first):
    return lax.optimization_barrier((array, first))[0]


def halves_kernel(mine, theirs, stay_ref, leave_ref, both_ref):
    half = stay_ref.shape[0]
    side = lax.axis_index(AZ) // half
    both_ref[...] = mine[...].astype(jnp.float32) + theirs[...].astype(jnp.float32)
    stay_ref[...] = both_ref[pl.ds(side * half, half)].astype(jnp.bfloat16)
    leave_ref[...] = both_ref[pl.ds((1 - side) * half, half)].astype(jnp.bfloat16)


def deal_kernel(stay, came, out_ref):
    both = stay[...].astype(jnp.float32) + came[...].astype(jnp.float32)
    lines = both.reshape(-1, CHAN)
    count, size, _ = out_ref.shape
    lines = jnp.concatenate([lines, jnp.zeros((count * size - lines.shape[0], CHAN), jnp.float32)])
    out_ref[...] = lines.reshape(out_ref.shape).astype(jnp.bfloat16)


def half_terms(pair):
    mine, theirs = chunks(pair)
    count, size, _ = mine.shape
    half = jax.ShapeDtypeStruct((count // 2, size, CHAN), jnp.bfloat16)
    both = pltpu.VMEM(mine.shape, jnp.float32)
    stay, leave = call(halves_kernel, (half, half), [both], mine.size, mine, theirs)
    came = lax.ppermute(leave, AZ, [(i, (i + count // 2) % count) for i in range(count)])
    dealt = -(-size // 16) * 8
    shape = jax.ShapeDtypeStruct((count, dealt, CHAN), jnp.bfloat16)
    return leave, call(deal_kernel, shape, [], mine.size, stay, came)


def join_kernel(mine, theirs, also, out_ref, held, done):
    size = mine.shape[1]
    both = mine[...].astype(jnp.float32) + theirs[...].astype(jnp.float32)
    held[:, :size] = both.astype(jnp.bfloat16)
    held[:, size:] = also[...]
    copy_all([(held, out_ref)], done)


def joined_terms(pair, also):
    mine, theirs = chunks(pair)
    count, size, _ = mine.shape
    shape = jax.ShapeDtypeStruct((count, size + also.shape[1], CHAN), jnp.bfloat16)
    held = [pltpu.VMEM(shape.shape, jnp.bfloat16), pltpu.SemaphoreType.DMA((1,))]
    return call(join_kernel, shape, held, mine.size, mine, theirs, also, out_space=HBM)


def reduce_kernel(size, parts_ref, out_ref, held, done):
    count = parts_ref.shape[0]
    dealt = parts_ref.shape[1] - size
    total = [parts_ref[n].astype(jnp.float32) for n in (0, count // 2)]
    for n in range(1, count // 2):
        total[0] = total[0] + parts_ref[n].astype(jnp.float32)
        total[1] = total[1] + parts_ref[count // 2 + n].astype(jnp.float32)
    held[:size] = (total[0][:size] + total[1][:size]).astype(jnp.bfloat16)
    held[size : size + dealt] = total[0][size:].astype(jnp.bfloat16)
    held[size + dealt :] = total[1][size:].astype(jnp.bfloat16)
    copy_all([(held, out_ref.at[n]) for n in range(count)], done)


def finish_kernel(size, scale, whole_ref, one_ref, two_ref, held_one, held_two, done):
    count = whole_ref.shape[0]
    dealt = (whole_ref.shape[1] - size) // 2
    lines = two_ref.shape[1]
    held_one[...] = whole_ref[:, :size].astype(jnp.float32) * scale
    first = pltpu.make_async_copy(held_one, one_ref, done.at[0])
    first.start()
    for side in range(2):
        for n in range(count):
            start, end = n * dealt, min((n + 1) * dealt, lines)
            if end > start:
                row = size + side * dealt
                part = whole_ref[n, row : row + dealt].astype(jnp.float32) * scale
                held_two[side, start:end] = part[: end - start]
    second = pltpu.make_async_copy(held_two, two_ref, done.at[1])
    second.start()
    first.wait()
    second.wait()


def summed_over_az(joined, size, scale):
    count, both, _ = joined.shape
    dealt = both - size
    held = [pltpu.VMEM((size + 2 * dealt, CHAN), jnp.bfloat16), pltpu.SemaphoreType.DMA((count,))]
    shape = jax.ShapeDtypeStruct((count, size + 2 * dealt, CHAN), jnp.bfloat16)
    copies = call(
        functools.partial(reduce_kernel, size),
        shape,
        held,
        joined.size,
        exchange(joined, AZ),
        out_space=HBM,
    )
    one = (count, size, CHAN)
    two = (2, count * size // 2, CHAN)
    banks = call(
        functools.partial(finish_kernel, size, scale),
        (jax.ShapeDtypeStruct(one, jnp.float32), jax.ShapeDtypeStruct(two, jnp.float32)),
        [
            pltpu.VMEM(one, jnp.float32),
            pltpu.VMEM(two, jnp.float32),
            pltpu.SemaphoreType.DMA((2,)),
        ],
        joined.size,
        exchange(copies, AZ),
        out_space=HBM,
        room=52,
    )
    return tuple(bank.reshape(1, 3, 3, CHAN, CHAN) for bank in banks)


def stacked(act, given, grad, pre, side):
    half = act.shape[0] // 2
    zeros = jnp.zeros((8, CHAN), jnp.float32)
    if side == 0:
        grad = [zeros[:2], grad[: half + 2], zeros[:4]]
        pre = [zeros[:1], pre[: half + 1], zeros[:6]]
    else:
        grad = [grad[half - 2 :], zeros[:6]]
        pre = [pre[half - 1 :], zeros[:7]]
    own = slice(side * half, (side + 1) * half)
    return jnp.concatenate([act[own], given[own], *grad, *pre])


def lanes_kernel(*refs):
    given, (mine_ref, away_ref, same_ref, cross_ref) = refs[:4], refs[4:8]
    held, done = refs[8:12], refs[12]
    _, core = here()
    copy_all(zip(given, held), done)
    inputs_ref, pre_one_ref, pre_two_ref, cotangent_ref = held
    for row in range(ROWS):
        lanes = slice(row * CHAN, (row + 1) * CHAN)
        pre = pre_one_ref[0, row].astype(jnp.float32)
        grad = cotangent_ref[0, row].astype(jnp.float32) * slope(
            pre_two_ref[0, row].astype(jnp.float32)
        )
        act = pre / (1.0 + jnp.exp(-pre))
        fields = (act, inputs_ref[0, row].astype(jnp.float32), grad, pre)
        left, right = stacked(*fields, 0), stacked(*fields, 1)
        mine_ref[:, lanes] = jnp.where(core == 0, left, right).astype(jnp.bfloat16)
        away_ref[:, lanes] = jnp.where(core == 0, right, left).astype(jnp.bfloat16)
        pad = jnp.zeros((5, CHAN), jnp.float32)
        low = jnp.concatenate([grad[:2], pre[:1], pad])
        high = jnp.concatenate([grad[-2:], pre[-1:], pad])
        same_ref[:, lanes] = jnp.where(core == 0, high, low).astype(jnp.bfloat16)
        cross_ref[:, lanes] = jnp.where(core == 0, low, high).astype(jnp.bfloat16)


def rims_kernel(mine_ref, partner_ref, same_ref, cross_ref, out_ref, pre_ref, held, done):
    _, core = here()
    ahead = held.shape[0] - pre_ref.shape[0]
    rows = pre_ref.shape[0]
    used = rows - 8
    at = lax.broadcasted_iota(jnp.int32, (rows, WIDE), 0)
    grad_at = jnp.where(core == 0, 0, used + 2)
    pre_at = jnp.where(core == 0, 0, used + 1)
    filled = []
    for body_ref, edge_ref in ((mine_ref, same_ref), (partner_ref, cross_ref)):
        body = body_ref[...].astype(jnp.float32)
        edge = edge_ref[...].astype(jnp.float32)
        grad = body[ahead : ahead + rows]
        grad = jnp.where(at == grad_at, edge[0:1], grad)
        grad = jnp.where(at == grad_at + 1, edge[1:2], grad)
        pre = jnp.where(at == pre_at, edge[2:3], body[ahead + rows :])
        filled.append(jnp.concatenate([body[:ahead], grad, pre]).astype(jnp.bfloat16))
    first = jnp.where(core == 0, filled[0], filled[1])
    second = jnp.where(core == 0, filled[1], filled[0])
    for lanes, part in ((slice(0, WIDE), first), (slice(WIDE, 2 * WIDE), second)):
        held[:, lanes] = part[: ahead + rows]
        pre_ref[:, lanes] = part[ahead + rows :]
    copy_all([(held, out_ref.at[n]) for n in range(out_ref.shape[0])], done)


def shards(inputs, pre_one, pre_two, cotangent, filt_one, filt_two):
    columns = inputs.shape[2]
    half = columns // 2
    core = lax.axis_index(CORE)
    az_count = lax.axis_size(AZ)
    rot_count = lax.axis_size(ROT)
    chips = lax.axis_size(CHIPS)
    cell_count = rot_count * inputs.shape[1] * columns * az_count
    scale = cell_count ** (-0.5)
    padded = half + 8

    def narrow(*shape):
        return jax.ShapeDtypeStruct(shape, jnp.bfloat16)

    rows = columns + 2 * padded
    mine, away, same, cross = call(
        lanes_kernel,
        (narrow(rows, WIDE), narrow(rows, WIDE), narrow(8, WIDE), narrow(8, WIDE)),
        [pltpu.VMEM(inputs.shape, jnp.bfloat16)] * 4 + [pltpu.SemaphoreType.DMA((4,))],
        inputs.size * 20,
        inputs,
        pre_one,
        pre_two,
        cotangent,
        space=HBM,
        room=60,
    )
    after_me = [(i, (i + 1) % az_count) for i in range(az_count)]
    before_me = [(i, (i - 1) % az_count) for i in range(az_count)]
    place = lambda c, pairs, d: [(c * az_count + i, d * az_count + j) for i, j in pairs]
    same = lax.ppermute(same, (CORE, AZ), place(0, after_me, 0) + place(1, before_me, 1))
    cross = lax.ppermute(cross, (CORE, AZ), place(1, after_me, 0) + place(0, before_me, 1))
    partner = lax.ppermute(away, CORE, SWAP)
    sent, pre_pair = call(
        rims_kernel,
        (narrow(chips, columns + padded, 2 * WIDE), narrow(padded, 2 * WIDE)),
        [
            pltpu.VMEM((columns + padded, 2 * WIDE), jnp.bfloat16),
            pltpu.SemaphoreType.DMA((chips,)),
        ],
        inputs.size * 20,
        mine,
        partner,
        same,
        cross,
        out_space=(HBM, VMEM),
    )
    other_two = lax.ppermute(filt_two[0], CORE, SWAP)
    other_one = lax.ppermute(filt_one[0], CORE, SWAP)
    first_blocks = exchange(after(sent, (other_two, other_one)), CHIPS)

    shares = conv(
        conv_two_kernel,
        first_blocks,
        padded,
        filt_two[0],
        other_two,
        half + 2,
        padded,
        (chips, padded, 2 * WIDE),
        [
            pltpu.VMEM((chips, padded, 2 * WIDE), jnp.bfloat16),
            pltpu.SemaphoreType.DMA((chips,)),
        ],
        HBM,
        52,
    )
    pair_two = filter_terms(first_blocks, 0, half, first_blocks, padded, 3)
    leave, terms_two = half_terms(pair_two)
    arrived = after(exchange(shares, CHIPS), leave)
    copies = call(
        point_kernel,
        narrow(chips, padded, 2 * WIDE),
        [pltpu.VMEM((padded, 2 * WIDE), jnp.bfloat16), pltpu.SemaphoreType.DMA((chips,))],
        arrived.size,
        arrived,
        pre_pair,
        out_space=HBM,
    )
    all_grad_one = after(exchange(copies, CHIPS), terms_two)
    joined = joined_terms(filter_terms(first_blocks, 1, half, all_grad_one, padded, 2), terms_two)
    filt_grad_one, filt_grad_two = summed_over_az(joined, filt_one.size // CHAN // az_count, scale)

    along_x = lax.axis_size(CHIPS[0])

    shares = conv(
        conv_one_kernel,
        after(all_grad_one, joined),
        padded,
        filt_one[0],
        other_one,
        half,
        half,
        (2, along_x, half, 2 * WIDE),
    )
    arrived_y = lax.ppermute(shares[1], CHIPS[1], SWAP)
    partial = (shares[0].astype(jnp.float32) + arrived_y.astype(jnp.float32)).astype(jnp.bfloat16)
    total = partial[0].astype(jnp.float32)
    for step in range(1, along_x):
        came = lax.ppermute(
            partial[step], CHIPS[0], [(i, (i + step) % along_x) for i in range(along_x)]
        )
        total = total + came.astype(jnp.float32)
    total = total.astype(jnp.bfloat16)
    left, right = total[:, :WIDE], total[:, WIDE:]
    mine = jnp.where(core == 0, left, right)
    theirs = lax.ppermute(jnp.where(core == 0, right, left), CORE, SWAP)
    whole = jnp.where(core == 0, jnp.concatenate([mine, theirs]), jnp.concatenate([theirs, mine]))
    input_grad = jnp.moveaxis(whole.reshape(columns, ROWS, CHAN), 1, 0)[None]
    return input_grad, filt_grad_one, filt_grad_two


def solution(mesh):
    finer = Mesh(mesh.devices.reshape(4, 2, 2, mesh.shape["az"]), (*ROT, AZ))
    field = P(ROT, None, AZ, None)
    bank = P(ROT, None, None, None, None)
    return jax.shard_map(
        shards,
        mesh=finer,
        in_specs=(field, field, field, field, bank, bank),
        out_specs=(field, bank, bank),
        check_vma=False,
    )
```

```python
import functools

import jax
import jax.numpy as jnp
from jax import lax
from jax.experimental import pallas as pl
from jax.experimental.pallas import tpu as pltpu
from jax.sharding import Mesh
from jax.sharding import PartitionSpec as P

CHIPS = ("rot_x", "rot_y")
CORE = "rot_c"
ROT = (*CHIPS, CORE)
AZ = "az"

ROWS = 4
CHAN = 128
WIDE = ROWS * CHAN
SWAP = [(0, 1), (1, 0)]
VMEM = pl.BlockSpec(memory_space=pltpu.VMEM)
HBM = pl.BlockSpec(memory_space=pltpu.HBM)


def slope(pre):
    logistic = 1.0 / (1.0 + jnp.exp(-pre))
    return logistic * (1.0 + pre * (1.0 - logistic))


def params(mebibytes):
    return pltpu.CompilerParams(vmem_limit_bytes=mebibytes * 1024 * 1024)


def here():
    return lax.axis_index(CHIPS[0]) * 2 + lax.axis_index(CHIPS[1]), lax.axis_index(CORE)


def call(kernel, out_shape, scratch, flops, *operands, space=VMEM, out_space=VMEM, room=40):
    n_bytes = sum(a.size * a.dtype.itemsize for a in operands)
    in_specs = list(space) if isinstance(space, tuple) else [space] * len(operands)
    out_specs = out_space
    if not isinstance(out_space, tuple):
        out_specs = jax.tree.map(lambda _: out_space, out_shape)
    return pl.pallas_call(
        kernel,
        out_shape=out_shape,
        in_specs=in_specs,
        out_specs=out_specs,
        scratch_shapes=scratch,
        compiler_params=params(room),
        cost_estimate=pl.CostEstimate(flops=flops, bytes_accessed=2 * n_bytes, transcendentals=0),
    )(*operands)


def copy_all(pairs, done):
    copies = [pltpu.make_async_copy(a, b, done.at[n]) for n, (a, b) in enumerate(pairs)]
    for copy in copies:
        copy.start()
    for copy in copies:
        copy.wait()


def interleave(blocks_ref, rows_ref, orients, first, shift):
    for g in range(orients):
        s = (g - shift) % orients
        lanes = slice((s % 2) * WIDE, (s % 2 + 1) * WIDE)
        rows_ref[:, g, :] = blocks_ref[s // 2, first:, lanes].astype(jnp.float32)


def band_weights(filt_ref, band_ref, slot):
    zero = jnp.zeros((CHAN, CHAN), jnp.bfloat16)
    for j in range(3):
        for out_row in range(ROWS):
            for in_row in range(ROWS):
                i = out_row - in_row + 1
                piece = filt_ref[i, j] if 0 <= i < 3 else zero
                band_ref[
                    slot,
                    j,
                    out_row * CHAN : (out_row + 1) * CHAN,
                    in_row * CHAN : (in_row + 1) * CHAN,
                ] = piece


def rotation_sums(orients, width, blocks_ref, mine_ref, other_ref, rows_0, rows_1, band):
    in_width = rows_0.shape[0]
    _, core = here()
    band_weights(mine_ref, band, core)
    band_weights(other_ref, band, 1 - core)
    first = blocks_ref.shape[1] - in_width
    interleave(blocks_ref, rows_0, orients, first, 0)
    interleave(blocks_ref, rows_1, orients, first, 1)
    total = None
    for slot, rows in ((0, rows_0), (1, rows_1)):
        flat = rows[...].reshape(in_width * orients, WIDE).astype(jnp.bfloat16)
        for j in range(3):
            window = flat[(2 - j) * orients : (2 - j + width) * orients]
            term = lax.dot_general(
                window,
                band[slot, j],
                (((1,), (1,)), ((), ())),
                preferred_element_type=jnp.float32,
            )
            total = term if total is None else total + term
    return total.reshape(width, orients, WIDE)


def conv_two_kernel(orients, width, blocks_ref, mine_ref, other_ref, out_ref, *scratch):
    *rows, sums, held, done = scratch
    chip, _ = here()
    total = rotation_sums(orients, width, blocks_ref, mine_ref, other_ref, *rows)
    sums[width:] = jnp.zeros((sums.shape[0] - width, orients, WIDE), jnp.float32)
    sums[:width] = total
    chips = orients // 2
    copies = []
    for pair in range(chips):
        for half in range(2):
            held[pair, :, half * WIDE : (half + 1) * WIDE] = sums[:, 2 * pair + half, :].astype(
                jnp.bfloat16
            )
        to = lax.rem(pair + chip, chips)
        copies.append(pltpu.make_async_copy(held.at[pair], out_ref.at[to], done.at[pair]))
        copies[-1].start()
    for copy in copies:
        copy.wait()


def conv_one_kernel(orients, width, blocks_ref, mine_ref, other_ref, out_ref, *scratch):
    *rows, sums = scratch
    chip, _ = here()
    sums[...] = rotation_sums(orients, width, blocks_ref, mine_ref, other_ref, *rows)
    chips = orients // 2
    across = out_ref.shape[1]
    for pair in range(chips):
        to = lax.rem(pair + chip, chips)
        other = lax.rem(to + chip, 2)
        step = lax.rem(to // 2 - chip // 2 + across, across)
        for half in range(2):
            out_ref[other, step, :, half * WIDE : (half + 1) * WIDE] = sums[
                :, 2 * pair + half, :
            ].astype(jnp.bfloat16)


def conv(kernel, blocks, in_width, mine, other, width, padded, out_shape, staging=(), out_space=VMEM, room=40):
    orients = 2 * blocks.shape[0]
    return call(
        functools.partial(kernel, orients, width),
        jax.ShapeDtypeStruct(out_shape, jnp.bfloat16),
        [
            pltpu.VMEM((in_width, orients, WIDE), jnp.float32),
            pltpu.VMEM((in_width, orients, WIDE), jnp.float32),
            pltpu.VMEM((2, 3, WIDE, WIDE), jnp.bfloat16),
            pltpu.VMEM((padded, orients, WIDE), jnp.float32),
            *staging,
        ],
        2 * 6 * width * orients * WIDE * WIDE,
        blocks,
        mine,
        other,
        out_space=out_space,
        room=room,
    )


def filter_kernel(
    orients, width, field, first, own, grad_ref, feat_ref, out_ref, feat_rows, grad_rows, held, done
):
    chip, core = here()
    slot = core if own else 1 - core
    in_width = grad_rows.shape[0]
    copies = [
        pltpu.make_async_copy(
            feat_ref.at[:, pl.ds(field * width, width), pl.ds(half * WIDE, WIDE)],
            held.at[:, half],
            done.at[half],
        )
        for half in range(2)
    ]
    for copy in copies:
        copy.start()
    interleave(grad_ref, grad_rows, orients, grad_ref.shape[1] - in_width, 0)
    grads = grad_rows[...].reshape(in_width * orients, WIDE).astype(jnp.bfloat16)
    for copy in copies:
        copy.wait()
    for g in range(orients):
        s = lax.rem(g + 2 * chip + slot, orients)
        feat_rows[:, g, :] = held[s // 2, lax.rem(s, 2)].astype(jnp.float32)
    feats = feat_rows[...].reshape(width * orients, WIDE).astype(jnp.bfloat16)
    for j in range(3):
        window = grads[(first - j) * orients : (first - j + width) * orients]
        product = lax.dot_general(
            feats,
            window,
            (((0,), (0,)), ((), ())),
            preferred_element_type=jnp.float32,
        )
        for i in range(3):
            total = None
            for row in range(ROWS):
                grad_row = row - i + 1
                if not 0 <= grad_row < ROWS:
                    continue
                piece = product[
                    row * CHAN : (row + 1) * CHAN, grad_row * CHAN : (grad_row + 1) * CHAN
                ]
                total = piece if total is None else total + piece
            out_ref[i, j] = total.astype(jnp.bfloat16)


def filter_terms(feats, field, width, grads, in_width, first):
    orients = 2 * feats.shape[0]

    def terms(own):
        return call(
            functools.partial(filter_kernel, orients, width, field, first, own),
            jax.ShapeDtypeStruct((3, 3, CHAN, CHAN), jnp.bfloat16),
            [
                pltpu.VMEM((width, orients, WIDE), jnp.float32),
                pltpu.VMEM((in_width, orients, WIDE), jnp.float32),
                pltpu.VMEM((orients // 2, 2, width, WIDE), jnp.bfloat16),
                pltpu.SemaphoreType.DMA((2,)),
            ],
            6 * width * orients * WIDE * WIDE,
            grads,
            feats,
            space=(VMEM, HBM),
            room=52,
        )

    theirs = lax.ppermute(terms(False), CORE, SWAP)
    return terms(True), theirs


def point_kernel(parts_ref, pre_ref, out_ref, held, done):
    total = parts_ref[0].astype(jnp.float32)
    for n in range(1, parts_ref.shape[0]):
        total = total + parts_ref[n].astype(jnp.float32)
    held[...] = (total * slope(pre_ref[...].astype(jnp.float32))).astype(jnp.bfloat16)
    copy_all([(held, out_ref.at[n]) for n in range(out_ref.shape[0])], done)


def exchange(parts, axes):
    return lax.all_to_all(parts, axes, 0, 0, tiled=True)


def chunks(pair):
    count = lax.axis_size(AZ)
    return [bank.reshape(count, -1, CHAN) for bank in pair]


def after(array, first):
    return lax.optimization_barrier((array, first))[0]


def both_kernel(mine, theirs, out_ref):
    both = mine[...].astype(jnp.float32) + theirs[...].astype(jnp.float32)
    out_ref[...] = both.astype(jnp.bfloat16)


def both_cores(pair):
    mine, theirs = chunks(pair)
    shape = jax.ShapeDtypeStruct(mine.shape, jnp.bfloat16)
    return call(both_kernel, shape, [], mine.size, mine, theirs)


def join_kernel(mine, theirs, also, out_ref, held, done):
    size = mine.shape[1]
    both = mine[...].astype(jnp.float32) + theirs[...].astype(jnp.float32)
    held[:, :size] = both.astype(jnp.bfloat16)
    held[:, size:] = also[...]
    copy_all([(held, out_ref)], done)


def joined_terms(pair, also):
    mine, theirs = chunks(pair)
    count, size, _ = mine.shape
    shape = jax.ShapeDtypeStruct((count, size + also.shape[1], CHAN), jnp.bfloat16)
    held = [pltpu.VMEM(shape.shape, jnp.bfloat16), pltpu.SemaphoreType.DMA((1,))]
    return call(join_kernel, shape, held, mine.size, mine, theirs, also, out_space=HBM)


def reduce_kernel(parts_ref, out_ref, held, done):
    total = parts_ref[0].astype(jnp.float32)
    for n in range(1, parts_ref.shape[0]):
        total = total + parts_ref[n].astype(jnp.float32)
    held[...] = total.astype(jnp.bfloat16)
    copy_all([(held, out_ref.at[n]) for n in range(out_ref.shape[0])], done)


def finish_kernel(scale, whole_ref, one_ref, two_ref, held, done):
    size = one_ref.shape[1]
    copies = []
    for n, out_ref in enumerate((one_ref, two_ref)):
        held[n] = whole_ref[:, n * size : (n + 1) * size].astype(jnp.float32) * scale
        copies.append(pltpu.make_async_copy(held.at[n], out_ref, done.at[n]))
        copies[n].start()
    for copy in copies:
        copy.wait()


def summed_over_az(joined, scale):
    count, both, _ = joined.shape
    held = [pltpu.VMEM((both, CHAN), jnp.bfloat16), pltpu.SemaphoreType.DMA((count,))]
    shape = jax.ShapeDtypeStruct(joined.shape, jnp.bfloat16)
    copies = call(reduce_kernel, shape, held, joined.size, exchange(joined, AZ), out_space=HBM)
    bank = jax.ShapeDtypeStruct((count, both // 2, CHAN), jnp.float32)
    banks = call(
        functools.partial(finish_kernel, scale),
        (bank, bank),
        [pltpu.VMEM((2, *bank.shape), jnp.float32), pltpu.SemaphoreType.DMA((2,))],
        joined.size,
        exchange(copies, AZ),
        out_space=HBM,
        room=52,
    )
    return tuple(bank.reshape(1, 3, 3, CHAN, CHAN) for bank in banks)


def stacked(act, given, grad, pre, side):
    half = act.shape[0] // 2
    zeros = jnp.zeros((8, CHAN), jnp.float32)
    if side == 0:
        grad = [zeros[:2], grad[: half + 2], zeros[:4]]
        pre = [zeros[:1], pre[: half + 1], zeros[:6]]
    else:
        grad = [grad[half - 2 :], zeros[:6]]
        pre = [pre[half - 1 :], zeros[:7]]
    own = slice(side * half, (side + 1) * half)
    return jnp.concatenate([act[own], given[own], *grad, *pre])


def lanes_kernel(*refs):
    given, (mine_ref, away_ref, same_ref, cross_ref) = refs[:4], refs[4:8]
    held, done = refs[8:12], refs[12]
    _, core = here()
    copy_all(zip(given, held), done)
    inputs_ref, pre_one_ref, pre_two_ref, cotangent_ref = held
    for row in range(ROWS):
        lanes = slice(row * CHAN, (row + 1) * CHAN)
        pre = pre_one_ref[0, row].astype(jnp.float32)
        grad = cotangent_ref[0, row].astype(jnp.float32) * slope(
            pre_two_ref[0, row].astype(jnp.float32)
        )
        act = pre / (1.0 + jnp.exp(-pre))
        fields = (act, inputs_ref[0, row].astype(jnp.float32), grad, pre)
        left, right = stacked(*fields, 0), stacked(*fields, 1)
        mine_ref[:, lanes] = jnp.where(core == 0, left, right).astype(jnp.bfloat16)
        away_ref[:, lanes] = jnp.where(core == 0, right, left).astype(jnp.bfloat16)
        pad = jnp.zeros((5, CHAN), jnp.float32)
        low = jnp.concatenate([grad[:2], pre[:1], pad])
        high = jnp.concatenate([grad[-2:], pre[-1:], pad])
        same_ref[:, lanes] = jnp.where(core == 0, high, low).astype(jnp.bfloat16)
        cross_ref[:, lanes] = jnp.where(core == 0, low, high).astype(jnp.bfloat16)


def rims_kernel(mine_ref, partner_ref, same_ref, cross_ref, out_ref, pre_ref, held, done):
    _, core = here()
    ahead = held.shape[0] - pre_ref.shape[0]
    rows = pre_ref.shape[0]
    used = rows - 8
    at = lax.broadcasted_iota(jnp.int32, (rows, WIDE), 0)
    grad_at = jnp.where(core == 0, 0, used + 2)
    pre_at = jnp.where(core == 0, 0, used + 1)
    filled = []
    for body_ref, edge_ref in ((mine_ref, same_ref), (partner_ref, cross_ref)):
        body = body_ref[...].astype(jnp.float32)
        edge = edge_ref[...].astype(jnp.float32)
        grad = body[ahead : ahead + rows]
        grad = jnp.where(at == grad_at, edge[0:1], grad)
        grad = jnp.where(at == grad_at + 1, edge[1:2], grad)
        pre = jnp.where(at == pre_at, edge[2:3], body[ahead + rows :])
        filled.append(jnp.concatenate([body[:ahead], grad, pre]).astype(jnp.bfloat16))
    first = jnp.where(core == 0, filled[0], filled[1])
    second = jnp.where(core == 0, filled[1], filled[0])
    for lanes, part in ((slice(0, WIDE), first), (slice(WIDE, 2 * WIDE), second)):
        held[:, lanes] = part[: ahead + rows]
        pre_ref[:, lanes] = part[ahead + rows :]
    copy_all([(held, out_ref.at[n]) for n in range(out_ref.shape[0])], done)


def shards(inputs, pre_one, pre_two, cotangent, filt_one, filt_two):
    columns = inputs.shape[2]
    half = columns // 2
    core = lax.axis_index(CORE)
    az_count = lax.axis_size(AZ)
    rot_count = lax.axis_size(ROT)
    chips = lax.axis_size(CHIPS)
    cell_count = rot_count * inputs.shape[1] * columns * az_count
    scale = cell_count ** (-0.5)
    padded = half + 8

    def narrow(*shape):
        return jax.ShapeDtypeStruct(shape, jnp.bfloat16)

    rows = columns + 2 * padded
    mine, away, same, cross = call(
        lanes_kernel,
        (narrow(rows, WIDE), narrow(rows, WIDE), narrow(8, WIDE), narrow(8, WIDE)),
        [pltpu.VMEM(inputs.shape, jnp.bfloat16)] * 4 + [pltpu.SemaphoreType.DMA((4,))],
        inputs.size * 20,
        inputs,
        pre_one,
        pre_two,
        cotangent,
        space=HBM,
        room=60,
    )
    after_me = [(i, (i + 1) % az_count) for i in range(az_count)]
    before_me = [(i, (i - 1) % az_count) for i in range(az_count)]
    place = lambda c, pairs, d: [(c * az_count + i, d * az_count + j) for i, j in pairs]
    same = lax.ppermute(same, (CORE, AZ), place(0, after_me, 0) + place(1, before_me, 1))
    cross = lax.ppermute(cross, (CORE, AZ), place(1, after_me, 0) + place(0, before_me, 1))
    partner = lax.ppermute(away, CORE, SWAP)
    sent, pre_pair = call(
        rims_kernel,
        (narrow(chips, columns + padded, 2 * WIDE), narrow(padded, 2 * WIDE)),
        [
            pltpu.VMEM((columns + padded, 2 * WIDE), jnp.bfloat16),
            pltpu.SemaphoreType.DMA((chips,)),
        ],
        inputs.size * 20,
        mine,
        partner,
        same,
        cross,
        out_space=(HBM, VMEM),
    )
    other_two = lax.ppermute(filt_two[0], CORE, SWAP)
    other_one = lax.ppermute(filt_one[0], CORE, SWAP)
    first_blocks = exchange(after(sent, (other_two, other_one)), CHIPS)

    shares = conv(
        conv_two_kernel,
        first_blocks,
        padded,
        filt_two[0],
        other_two,
        half + 2,
        padded,
        (chips, padded, 2 * WIDE),
        [
            pltpu.VMEM((chips, padded, 2 * WIDE), jnp.bfloat16),
            pltpu.SemaphoreType.DMA((chips,)),
        ],
        HBM,
        52,
    )
    pair_two = filter_terms(first_blocks, 0, half, first_blocks, padded, 3)
    terms_two = both_cores(pair_two)
    arrived = after(exchange(shares, CHIPS), terms_two)
    copies = call(
        point_kernel,
        narrow(chips, padded, 2 * WIDE),
        [pltpu.VMEM((padded, 2 * WIDE), jnp.bfloat16), pltpu.SemaphoreType.DMA((chips,))],
        arrived.size,
        arrived,
        pre_pair,
        out_space=HBM,
    )
    all_grad_one = exchange(copies, CHIPS)
    joined = joined_terms(filter_terms(first_blocks, 1, half, all_grad_one, padded, 2), terms_two)
    filt_grad_one, filt_grad_two = summed_over_az(joined, scale)

    along_x = lax.axis_size(CHIPS[0])

    shares = conv(
        conv_one_kernel,
        after(all_grad_one, joined),
        padded,
        filt_one[0],
        other_one,
        half,
        half,
        (2, along_x, half, 2 * WIDE),
    )
    arrived_y = lax.ppermute(shares[1], CHIPS[1], SWAP)
    partial = (shares[0].astype(jnp.float32) + arrived_y.astype(jnp.float32)).astype(jnp.bfloat16)
    total = partial[0].astype(jnp.float32)
    for step in range(1, along_x):
        came = lax.ppermute(
            partial[step], CHIPS[0], [(i, (i + step) % along_x) for i in range(along_x)]
        )
        total = total + came.astype(jnp.float32)
    total = total.astype(jnp.bfloat16)
    left, right = total[:, :WIDE], total[:, WIDE:]
    mine = jnp.where(core == 0, left, right)
    theirs = lax.ppermute(jnp.where(core == 0, right, left), CORE, SWAP)
    whole = jnp.where(core == 0, jnp.concatenate([mine, theirs]), jnp.concatenate([theirs, mine]))
    input_grad = jnp.moveaxis(whole.reshape(columns, ROWS, CHAN), 1, 0)[None]
    return input_grad, filt_grad_one, filt_grad_two


def solution(mesh):
    finer = Mesh(mesh.devices.reshape(4, 2, 2, mesh.shape["az"]), (*ROT, AZ))
    field = P(ROT, None, AZ, None)
    bank = P(ROT, None, None, None, None)
    return jax.shard_map(
        shards,
        mesh=finer,
        in_specs=(field, field, field, field, bank, bank),
        out_specs=(field, bank, bank),
        check_vma=False,
    )
```

```python
import functools

import jax
import jax.numpy as jnp
from jax import lax
from jax.experimental import pallas as pl
from jax.experimental.pallas import tpu as pltpu
from jax.sharding import Mesh
from jax.sharding import PartitionSpec as P

CHIPS = ("rot_x", "rot_y")
CORE = "rot_c"
ROT = (*CHIPS, CORE)
AZ = "az"

ROWS = 4
CHAN = 128
WIDE = ROWS * CHAN
SWAP = [(0, 1), (1, 0)]
VMEM = pl.BlockSpec(memory_space=pltpu.VMEM)
HBM = pl.BlockSpec(memory_space=pltpu.HBM)


def slope(pre):
    logistic = 1.0 / (1.0 + jnp.exp(-pre))
    return logistic * (1.0 + pre * (1.0 - logistic))


def params(mebibytes):
    return pltpu.CompilerParams(vmem_limit_bytes=mebibytes * 1024 * 1024)


def here():
    return lax.axis_index(CHIPS[0]) * 2 + lax.axis_index(CHIPS[1]), lax.axis_index(CORE)


def call(kernel, out_shape, scratch, flops, *operands, space=VMEM, out_space=VMEM, room=40):
    n_bytes = sum(a.size * a.dtype.itemsize for a in operands)
    in_specs = list(space) if isinstance(space, tuple) else [space] * len(operands)
    out_specs = out_space
    if not isinstance(out_space, tuple):
        out_specs = jax.tree.map(lambda _: out_space, out_shape)
    return pl.pallas_call(
        kernel,
        out_shape=out_shape,
        in_specs=in_specs,
        out_specs=out_specs,
        scratch_shapes=scratch,
        compiler_params=params(room),
        cost_estimate=pl.CostEstimate(flops=flops, bytes_accessed=2 * n_bytes, transcendentals=0),
    )(*operands)


def copy_all(pairs, done):
    copies = [pltpu.make_async_copy(a, b, done.at[n]) for n, (a, b) in enumerate(pairs)]
    for copy in copies:
        copy.start()
    for copy in copies:
        copy.wait()


def interleave(blocks_ref, rows_ref, orients, first, shift):
    for g in range(orients):
        s = (g - shift) % orients
        lanes = slice((s % 2) * WIDE, (s % 2 + 1) * WIDE)
        rows_ref[:, g, :] = blocks_ref[s // 2, first:, lanes].astype(jnp.float32)


def band_weights(filt_ref, band_ref, slot):
    zero = jnp.zeros((CHAN, CHAN), jnp.bfloat16)
    for j in range(3):
        for out_row in range(ROWS):
            for in_row in range(ROWS):
                i = out_row - in_row + 1
                piece = filt_ref[i, j] if 0 <= i < 3 else zero
                band_ref[
                    slot,
                    j,
                    out_row * CHAN : (out_row + 1) * CHAN,
                    in_row * CHAN : (in_row + 1) * CHAN,
                ] = piece


def rotation_sums(orients, width, blocks_ref, mine_ref, other_ref, rows_0, rows_1, band):
    in_width = rows_0.shape[0]
    _, core = here()
    band_weights(mine_ref, band, core)
    band_weights(other_ref, band, 1 - core)
    first = blocks_ref.shape[1] - in_width
    interleave(blocks_ref, rows_0, orients, first, 0)
    interleave(blocks_ref, rows_1, orients, first, 1)
    total = None
    for slot, rows in ((0, rows_0), (1, rows_1)):
        flat = rows[...].reshape(in_width * orients, WIDE).astype(jnp.bfloat16)
        for j in range(3):
            window = flat[(2 - j) * orients : (2 - j + width) * orients]
            term = lax.dot_general(
                window,
                band[slot, j],
                (((1,), (1,)), ((), ())),
                preferred_element_type=jnp.float32,
            )
            total = term if total is None else total + term
    return total.reshape(width, orients, WIDE)


def conv_two_kernel(orients, width, blocks_ref, mine_ref, other_ref, out_ref, *scratch):
    *rows, sums, held, done = scratch
    chip, _ = here()
    total = rotation_sums(orients, width, blocks_ref, mine_ref, other_ref, *rows)
    sums[width:] = jnp.zeros((sums.shape[0] - width, orients, WIDE), jnp.float32)
    sums[:width] = total
    chips = orients // 2
    copies = []
    for pair in range(chips):
        for half in range(2):
            held[pair, :, half * WIDE : (half + 1) * WIDE] = sums[:, 2 * pair + half, :].astype(
                jnp.bfloat16
            )
        to = lax.rem(pair + chip, chips)
        copies.append(pltpu.make_async_copy(held.at[pair], out_ref.at[to], done.at[pair]))
        copies[-1].start()
    for copy in copies:
        copy.wait()


def conv_one_kernel(orients, width, blocks_ref, mine_ref, other_ref, out_ref, *scratch):
    *rows, sums = scratch
    chip, _ = here()
    sums[...] = rotation_sums(orients, width, blocks_ref, mine_ref, other_ref, *rows)
    chips = orients // 2
    across = out_ref.shape[1]
    for pair in range(chips):
        to = lax.rem(pair + chip, chips)
        other = lax.rem(to + chip, 2)
        step = lax.rem(to // 2 - chip // 2 + across, across)
        for half in range(2):
            out_ref[other, step, :, half * WIDE : (half + 1) * WIDE] = sums[
                :, 2 * pair + half, :
            ].astype(jnp.bfloat16)


def conv(kernel, blocks, in_width, mine, other, width, padded, out_shape, staging=(), out_space=VMEM, room=40):
    orients = 2 * blocks.shape[0]
    return call(
        functools.partial(kernel, orients, width),
        jax.ShapeDtypeStruct(out_shape, jnp.bfloat16),
        [
            pltpu.VMEM((in_width, orients, WIDE), jnp.float32),
            pltpu.VMEM((in_width, orients, WIDE), jnp.float32),
            pltpu.VMEM((2, 3, WIDE, WIDE), jnp.bfloat16),
            pltpu.VMEM((padded, orients, WIDE), jnp.float32),
            *staging,
        ],
        2 * 6 * width * orients * WIDE * WIDE,
        blocks,
        mine,
        other,
        out_space=out_space,
        room=room,
    )


def filter_kernel(
    orients, width, field, first, own, grad_ref, *refs
):
    feat_refs, (out_ref, feat_rows, grad_rows, held, done) = refs[:-5], refs[-5:]
    chip, core = here()
    slot = core if own else 1 - core
    in_width = grad_rows.shape[0]
    part = pl.ds(field * width, width)
    copies = []
    for step, feat_ref in enumerate(feat_refs):
        row = lax.rem(chip // 2 - step + len(feat_refs), len(feat_refs))
        for y in range(2):
            for c in range(2):
                s = (row * 2 + lax.rem(chip + y, 2)) * 2 + lax.rem(core + c, 2)
                source = feat_ref.at[y, c, part]
                copies.append(pltpu.make_async_copy(source, held.at[s], done.at[len(copies)]))
                copies[-1].start()
    interleave(grad_ref, grad_rows, orients, grad_ref.shape[1] - in_width, 0)
    grads = grad_rows[...].reshape(in_width * orients, WIDE).astype(jnp.bfloat16)
    for copy in copies:
        copy.wait()
    for g in range(orients):
        s = lax.rem(g + 2 * chip + slot, orients)
        feat_rows[:, g, :] = held[s].astype(jnp.float32)
    feats = feat_rows[...].reshape(width * orients, WIDE).astype(jnp.bfloat16)
    for j in range(3):
        window = grads[(first - j) * orients : (first - j + width) * orients]
        product = lax.dot_general(
            feats,
            window,
            (((0,), (0,)), ((), ())),
            preferred_element_type=jnp.float32,
        )
        for i in range(3):
            total = None
            for row in range(ROWS):
                grad_row = row - i + 1
                if not 0 <= grad_row < ROWS:
                    continue
                piece = product[
                    row * CHAN : (row + 1) * CHAN, grad_row * CHAN : (grad_row + 1) * CHAN
                ]
                total = piece if total is None else total + piece
            out_ref[i, j] = total.astype(jnp.bfloat16)


def filter_terms(feats, field, width, grads, in_width, first):
    orients = 4 * len(feats)

    def terms(own):
        return call(
            functools.partial(filter_kernel, orients, width, field, first, own),
            jax.ShapeDtypeStruct((3, 3, CHAN, CHAN), jnp.bfloat16),
            [
                pltpu.VMEM((width, orients, WIDE), jnp.float32),
                pltpu.VMEM((in_width, orients, WIDE), jnp.float32),
                pltpu.VMEM((orients, width, WIDE), jnp.bfloat16),
                pltpu.SemaphoreType.DMA((orients,)),
            ],
            6 * width * orients * WIDE * WIDE,
            grads,
            *feats,
            space=(VMEM, *[HBM] * len(feats)),
            room=52,
        )

    theirs = lax.ppermute(terms(False), CORE, SWAP)
    return terms(True), theirs


def point_kernel(parts_ref, pre_ref, out_ref, held, done):
    total = parts_ref[0].astype(jnp.float32)
    for n in range(1, parts_ref.shape[0]):
        total = total + parts_ref[n].astype(jnp.float32)
    held[...] = (total * slope(pre_ref[...].astype(jnp.float32))).astype(jnp.bfloat16)
    copy_all([(held, out_ref.at[n]) for n in range(out_ref.shape[0])], done)


def exchange(parts, axes):
    return lax.all_to_all(parts, axes, 0, 0, tiled=True)


def chunks(pair):
    count = lax.axis_size(AZ)
    return [bank.reshape(count, -1, CHAN) for bank in pair]


def after(array, first):
    return lax.optimization_barrier((array, first))[0]


def halves_kernel(mine, theirs, stay_ref, leave_ref, both_ref):
    half = stay_ref.shape[0]
    side = lax.axis_index(AZ) // half
    both_ref[...] = mine[...].astype(jnp.float32) + theirs[...].astype(jnp.float32)
    stay_ref[...] = both_ref[pl.ds(side * half, half)].astype(jnp.bfloat16)
    leave_ref[...] = both_ref[pl.ds((1 - side) * half, half)].astype(jnp.bfloat16)


def deal_kernel(stay, came, out_ref):
    both = stay[...].astype(jnp.float32) + came[...].astype(jnp.float32)
    lines = both.reshape(-1, CHAN)
    count, size, _ = out_ref.shape
    for n in range(count):
        out_ref[n] = lines[n * size : (n + 1) * size].astype(jnp.bfloat16)


def half_terms(pair):
    mine, theirs = chunks(pair)
    count, size, _ = mine.shape
    half = jax.ShapeDtypeStruct((count // 2, size, CHAN), jnp.bfloat16)
    both = pltpu.VMEM(mine.shape, jnp.float32)
    stay, leave = call(halves_kernel, (half, half), [both], mine.size, mine, theirs)
    came = lax.ppermute(leave, AZ, [(i, (i + count // 2) % count) for i in range(count)])
    shape = jax.ShapeDtypeStruct((count, size // 2, CHAN), jnp.bfloat16)
    return leave, call(deal_kernel, shape, [], mine.size, stay, came)


def join_kernel(mine, theirs, also, out_ref, held, done):
    size = mine.shape[1]
    both = mine[...].astype(jnp.float32) + theirs[...].astype(jnp.float32)
    held[:, :size] = both.astype(jnp.bfloat16)
    held[:, size:] = also[...]
    copy_all([(held, out_ref)], done)


def joined_terms(pair, also):
    mine, theirs = chunks(pair)
    count, size, _ = mine.shape
    shape = jax.ShapeDtypeStruct((count, size + also.shape[1], CHAN), jnp.bfloat16)
    held = [pltpu.VMEM(shape.shape, jnp.bfloat16), pltpu.SemaphoreType.DMA((1,))]
    return call(join_kernel, shape, held, mine.size, mine, theirs, also, out_space=HBM)


def reduce_kernel(size, parts_ref, out_ref, held, done):
    count = parts_ref.shape[0]
    total = [parts_ref[n].astype(jnp.float32) for n in (0, count // 2)]
    for n in range(1, count // 2):
        total[0] = total[0] + parts_ref[n].astype(jnp.float32)
        total[1] = total[1] + parts_ref[count // 2 + n].astype(jnp.float32)
    whole = [total[0][:size] + total[1][:size], total[0][size:], total[1][size:]]
    held[...] = jnp.concatenate(whole).astype(jnp.bfloat16)
    copy_all([(held, out_ref.at[n]) for n in range(count)], done)


def finish_kernel(size, scale, whole_ref, one_ref, two_ref, held_one, held_two, done):
    count = whole_ref.shape[0]
    dealt = (whole_ref.shape[1] - size) // 2
    held_one[...] = whole_ref[:, :size].astype(jnp.float32) * scale
    first = pltpu.make_async_copy(held_one, one_ref, done.at[0])
    first.start()
    for side in range(2):
        for n in range(count):
            part = whole_ref[n, size:].astype(jnp.float32) * scale
            held_two[side, n * dealt : (n + 1) * dealt] = part[side * dealt : (side + 1) * dealt]
    second = pltpu.make_async_copy(held_two, two_ref, done.at[1])
    second.start()
    first.wait()
    second.wait()


def summed_over_az(joined, size, scale):
    count, both, _ = joined.shape
    dealt = both - size
    held = [pltpu.VMEM((size + 2 * dealt, CHAN), jnp.bfloat16), pltpu.SemaphoreType.DMA((count,))]
    shape = jax.ShapeDtypeStruct((count, size + 2 * dealt, CHAN), jnp.bfloat16)
    copies = call(
        functools.partial(reduce_kernel, size),
        shape,
        held,
        joined.size,
        exchange(joined, AZ),
        out_space=HBM,
    )
    one = (count, size, CHAN)
    two = (2, count * size // 2, CHAN)
    banks = call(
        functools.partial(finish_kernel, size, scale),
        (jax.ShapeDtypeStruct(one, jnp.float32), jax.ShapeDtypeStruct(two, jnp.float32)),
        [
            pltpu.VMEM(one, jnp.float32),
            pltpu.VMEM(two, jnp.float32),
            pltpu.SemaphoreType.DMA((2,)),
        ],
        joined.size,
        exchange(copies, AZ),
        out_space=HBM,
        room=52,
    )
    return tuple(bank.reshape(1, 3, 3, CHAN, CHAN) for bank in banks)


def stacked(act, given, grad, pre, side):
    half = act.shape[0] // 2
    zeros = jnp.zeros((8, CHAN), jnp.float32)
    if side == 0:
        grad = [zeros[:2], grad[: half + 2], zeros[:4]]
        pre = [zeros[:1], pre[: half + 1], zeros[:6]]
    else:
        grad = [grad[half - 2 :], zeros[:6]]
        pre = [pre[half - 1 :], zeros[:7]]
    own = slice(side * half, (side + 1) * half)
    return jnp.concatenate([act[own], given[own]]), jnp.concatenate([*grad, *pre])


def lanes_kernel(*refs):
    given, (same_ref, cross_ref), sides = refs[:4], refs[4:6], refs[6:10]
    held, done = refs[10:14], refs[14]
    _, core = here()
    copy_all(zip(given, held), done)
    inputs_ref, pre_one_ref, pre_two_ref, cotangent_ref = held
    for row in range(ROWS):
        lanes = slice(row * CHAN, (row + 1) * CHAN)
        pre = pre_one_ref[0, row].astype(jnp.float32)
        grad = cotangent_ref[0, row].astype(jnp.float32) * slope(
            pre_two_ref[0, row].astype(jnp.float32)
        )
        act = pre / (1.0 + jnp.exp(-pre))
        fields = (act, inputs_ref[0, row].astype(jnp.float32), grad, pre)
        for n, (left, right) in enumerate(zip(stacked(*fields, 0), stacked(*fields, 1))):
            mine_ref, away_ref = sides[2 * n : 2 * n + 2]
            mine_ref[:, lanes] = jnp.where(core == 0, left, right).astype(jnp.bfloat16)
            away_ref[:, lanes] = jnp.where(core == 0, right, left).astype(jnp.bfloat16)
        pad = jnp.zeros((5, CHAN), jnp.float32)
        low = jnp.concatenate([grad[:2], pre[:1], pad])
        high = jnp.concatenate([grad[-2:], pre[-1:], pad])
        same_ref[:, lanes] = jnp.where(core == 0, high, low).astype(jnp.bfloat16)
        cross_ref[:, lanes] = jnp.where(core == 0, low, high).astype(jnp.bfloat16)


def rims_kernel(mine_ref, partner_ref, same_ref, cross_ref, out_ref, pre_ref, held, done):
    _, core = here()
    rows = pre_ref.shape[0]
    used = rows - 8
    at = lax.broadcasted_iota(jnp.int32, (rows, WIDE), 0)
    grad_at = jnp.where(core == 0, 0, used + 2)
    pre_at = jnp.where(core == 0, 0, used + 1)
    filled = []
    for body_ref, edge_ref in ((mine_ref, same_ref), (partner_ref, cross_ref)):
        body = body_ref[...].astype(jnp.float32)
        edge = edge_ref[...].astype(jnp.float32)
        grad = body[:rows]
        grad = jnp.where(at == grad_at, edge[0:1], grad)
        grad = jnp.where(at == grad_at + 1, edge[1:2], grad)
        pre = jnp.where(at == pre_at, edge[2:3], body[rows:])
        filled.append(jnp.concatenate([grad, pre]).astype(jnp.bfloat16))
    first = jnp.where(core == 0, filled[0], filled[1])
    second = jnp.where(core == 0, filled[1], filled[0])
    for lanes, part in ((slice(0, WIDE), first), (slice(WIDE, 2 * WIDE), second)):
        held[:, lanes] = part[:rows]
        pre_ref[:, lanes] = part[rows:]
    copy_all([(held, out_ref.at[n]) for n in range(out_ref.shape[0])], done)


def shards(inputs, pre_one, pre_two, cotangent, filt_one, filt_two):
    columns = inputs.shape[2]
    half = columns // 2
    core = lax.axis_index(CORE)
    az_count = lax.axis_size(AZ)
    rot_count = lax.axis_size(ROT)
    chips = lax.axis_size(CHIPS)
    cell_count = rot_count * inputs.shape[1] * columns * az_count
    scale = cell_count ** (-0.5)
    padded = half + 8

    def narrow(*shape):
        return jax.ShapeDtypeStruct(shape, jnp.bfloat16)

    edge, block, rims = narrow(8, WIDE), narrow(columns, WIDE), narrow(2 * padded, WIDE)
    same, cross, feats, feats_away, mine, away = call(
        lanes_kernel,
        (edge, edge, block, block, rims, rims),
        [pltpu.VMEM(inputs.shape, jnp.bfloat16)] * 4 + [pltpu.SemaphoreType.DMA((4,))],
        inputs.size * 20,
        inputs,
        pre_one,
        pre_two,
        cotangent,
        space=HBM,
        room=60,
    )
    after_me = [(i, (i + 1) % az_count) for i in range(az_count)]
    before_me = [(i, (i - 1) % az_count) for i in range(az_count)]
    place = lambda c, pairs, d: [(c * az_count + i, d * az_count + j) for i, j in pairs]
    same = lax.ppermute(same, (CORE, AZ), place(0, after_me, 0) + place(1, before_me, 1))
    cross = lax.ppermute(cross, (CORE, AZ), place(1, after_me, 0) + place(0, before_me, 1))
    partner = lax.ppermute(away, CORE, SWAP)
    pair = [feats, lax.ppermute(feats_away, CORE, SWAP)]
    along_y = [lax.ppermute(part, CHIPS[1], SWAP) for part in pair]
    sent, pre_pair = call(
        rims_kernel,
        (narrow(chips, padded, 2 * WIDE), narrow(padded, 2 * WIDE)),
        [
            pltpu.VMEM((padded, 2 * WIDE), jnp.bfloat16),
            pltpu.SemaphoreType.DMA((chips,)),
        ],
        inputs.size * 20,
        mine,
        partner,
        same,
        cross,
        out_space=(HBM, VMEM),
    )
    other_two = lax.ppermute(filt_two[0], CORE, SWAP)
    other_one = lax.ppermute(filt_one[0], CORE, SWAP)
    first_blocks = exchange(after(sent, (other_two, other_one, along_y)), CHIPS)

    along_x = lax.axis_size(CHIPS[0])
    near = jnp.stack([jnp.stack(pair), jnp.stack(along_y)])
    all_feats = [near] + [
        lax.ppermute(near, CHIPS[0], [(i, (i + step) % along_x) for i in range(along_x)])
        for step in range(1, along_x)
    ]
    first_blocks = after(first_blocks, near)

    shares = conv(
        conv_two_kernel,
        first_blocks,
        padded,
        filt_two[0],
        other_two,
        half + 2,
        padded,
        (chips, padded, 2 * WIDE),
        [
            pltpu.VMEM((chips, padded, 2 * WIDE), jnp.bfloat16),
            pltpu.SemaphoreType.DMA((chips,)),
        ],
        HBM,
        52,
    )
    pair_two = filter_terms(all_feats, 0, half, first_blocks, padded, 3)
    leave, terms_two = half_terms(pair_two)
    arrived = after(exchange(shares, CHIPS), leave)
    copies = call(
        point_kernel,
        narrow(chips, padded, 2 * WIDE),
        [pltpu.VMEM((padded, 2 * WIDE), jnp.bfloat16), pltpu.SemaphoreType.DMA((chips,))],
        arrived.size,
        arrived,
        pre_pair,
        out_space=HBM,
    )
    all_grad_one = after(exchange(copies, CHIPS), terms_two)
    joined = joined_terms(filter_terms(all_feats, 1, half, all_grad_one, padded, 2), terms_two)
    filt_grad_one, filt_grad_two = summed_over_az(joined, filt_one.size // CHAN // az_count, scale)

    shares = conv(
        conv_one_kernel,
        after(all_grad_one, joined),
        padded,
        filt_one[0],
        other_one,
        half,
        half,
        (2, along_x, half, 2 * WIDE),
    )
    arrived_y = lax.ppermute(shares[1], CHIPS[1], SWAP)
    partial = (shares[0].astype(jnp.float32) + arrived_y.astype(jnp.float32)).astype(jnp.bfloat16)
    total = partial[0].astype(jnp.float32)
    for step in range(1, along_x):
        came = lax.ppermute(
            partial[step], CHIPS[0], [(i, (i + step) % along_x) for i in range(along_x)]
        )
        total = total + came.astype(jnp.float32)
    total = total.astype(jnp.bfloat16)
    left, right = total[:, :WIDE], total[:, WIDE:]
    mine = jnp.where(core == 0, left, right)
    theirs = lax.ppermute(jnp.where(core == 0, right, left), CORE, SWAP)
    whole = jnp.where(core == 0, jnp.concatenate([mine, theirs]), jnp.concatenate([theirs, mine]))
    input_grad = jnp.moveaxis(whole.reshape(columns, ROWS, CHAN), 1, 0)[None]
    return input_grad, filt_grad_one, filt_grad_two


def solution(mesh):
    finer = Mesh(mesh.devices.reshape(4, 2, 2, mesh.shape["az"]), (*ROT, AZ))
    field = P(ROT, None, AZ, None)
    bank = P(ROT, None, None, None, None)
    return jax.shard_map(
        shards,
        mesh=finer,
        in_specs=(field, field, field, field, bank, bank),
        out_specs=(field, bank, bank),
        check_vma=False,
    )
```

```python
import functools

import jax
import jax.numpy as jnp
from jax import lax
from jax.experimental import pallas as pl
from jax.experimental.pallas import tpu as pltpu
from jax.sharding import Mesh
from jax.sharding import PartitionSpec as P

CHIPS = ("rot_x", "rot_y")
CORE = "rot_c"
ROT = (*CHIPS, CORE)
AZ = "az"

ROWS = 4
CHAN = 128
WIDE = ROWS * CHAN
SWAP = [(0, 1), (1, 0)]
VMEM = pl.BlockSpec(memory_space=pltpu.VMEM)
HBM = pl.BlockSpec(memory_space=pltpu.HBM)


def slope(pre):
    logistic = 1.0 / (1.0 + jnp.exp(-pre))
    return logistic * (1.0 + pre * (1.0 - logistic))


def params(mebibytes):
    return pltpu.CompilerParams(vmem_limit_bytes=mebibytes * 1024 * 1024)


def here():
    return lax.axis_index(CHIPS[0]) * 2 + lax.axis_index(CHIPS[1]), lax.axis_index(CORE)


def call(kernel, out_shape, scratch, flops, *operands, space=VMEM, out_space=VMEM, room=40):
    n_bytes = sum(a.size * a.dtype.itemsize for a in operands)
    in_specs = list(space) if isinstance(space, tuple) else [space] * len(operands)
    out_specs = out_space
    if not isinstance(out_space, tuple):
        out_specs = jax.tree.map(lambda _: out_space, out_shape)
    return pl.pallas_call(
        kernel,
        out_shape=out_shape,
        in_specs=in_specs,
        out_specs=out_specs,
        scratch_shapes=scratch,
        compiler_params=params(room),
        cost_estimate=pl.CostEstimate(flops=flops, bytes_accessed=2 * n_bytes, transcendentals=0),
    )(*operands)


def copy_all(pairs, done):
    copies = [pltpu.make_async_copy(a, b, done.at[n]) for n, (a, b) in enumerate(pairs)]
    for copy in copies:
        copy.start()
    for copy in copies:
        copy.wait()


def interleave(blocks_ref, rows_ref, orients, first, shift):
    for g in range(orients):
        s = (g - shift) % orients
        lanes = slice((s % 2) * WIDE, (s % 2 + 1) * WIDE)
        rows_ref[:, g, :] = blocks_ref[s // 2, first:, lanes].astype(jnp.float32)


def band_weights(filt_ref, band_ref, slot):
    zero = jnp.zeros((CHAN, CHAN), jnp.bfloat16)
    for j in range(3):
        for out_row in range(ROWS):
            for in_row in range(ROWS):
                i = out_row - in_row + 1
                piece = filt_ref[i, j] if 0 <= i < 3 else zero
                band_ref[
                    slot,
                    j,
                    out_row * CHAN : (out_row + 1) * CHAN,
                    in_row * CHAN : (in_row + 1) * CHAN,
                ] = piece


def rotation_sums(orients, width, blocks_ref, mine_ref, other_ref, rows_0, rows_1, band):
    in_width = rows_0.shape[0]
    _, core = here()
    band_weights(mine_ref, band, core)
    band_weights(other_ref, band, 1 - core)
    first = blocks_ref.shape[1] - in_width
    interleave(blocks_ref, rows_0, orients, first, 0)
    interleave(blocks_ref, rows_1, orients, first, 1)
    total = None
    for slot, rows in ((0, rows_0), (1, rows_1)):
        flat = rows[...].reshape(in_width * orients, WIDE).astype(jnp.bfloat16)
        for j in range(3):
            window = flat[(2 - j) * orients : (2 - j + width) * orients]
            term = lax.dot_general(
                window,
                band[slot, j],
                (((1,), (1,)), ((), ())),
                preferred_element_type=jnp.float32,
            )
            total = term if total is None else total + term
    return total.reshape(width, orients, WIDE)


def conv_two_kernel(orients, width, blocks_ref, mine_ref, other_ref, out_ref, *scratch):
    *rows, sums, held, done = scratch
    chip, _ = here()
    total = rotation_sums(orients, width, blocks_ref, mine_ref, other_ref, *rows)
    sums[width:] = jnp.zeros((sums.shape[0] - width, orients, WIDE), jnp.float32)
    sums[:width] = total
    chips = orients // 2
    copies = []
    for pair in range(chips):
        for half in range(2):
            held[pair, :, half * WIDE : (half + 1) * WIDE] = sums[:, 2 * pair + half, :].astype(
                jnp.bfloat16
            )
        to = lax.rem(pair + chip, chips)
        copies.append(pltpu.make_async_copy(held.at[pair], out_ref.at[to], done.at[pair]))
        copies[-1].start()
    for copy in copies:
        copy.wait()


def conv_one_kernel(orients, width, blocks_ref, mine_ref, other_ref, out_ref, *scratch):
    *rows, sums = scratch
    chip, _ = here()
    sums[...] = rotation_sums(orients, width, blocks_ref, mine_ref, other_ref, *rows)
    chips = orients // 2
    across = out_ref.shape[1]
    for pair in range(chips):
        to = lax.rem(pair + chip, chips)
        other = lax.rem(to + chip, 2)
        step = lax.rem(to // 2 - chip // 2 + across, across)
        for half in range(2):
            out_ref[other, step, :, half * WIDE : (half + 1) * WIDE] = sums[
                :, 2 * pair + half, :
            ].astype(jnp.bfloat16)


def conv(kernel, blocks, in_width, mine, other, width, padded, out_shape, staging=(), out_space=VMEM, room=40):
    orients = 2 * blocks.shape[0]
    return call(
        functools.partial(kernel, orients, width),
        jax.ShapeDtypeStruct(out_shape, jnp.bfloat16),
        [
            pltpu.VMEM((in_width, orients, WIDE), jnp.float32),
            pltpu.VMEM((in_width, orients, WIDE), jnp.float32),
            pltpu.VMEM((2, 3, WIDE, WIDE), jnp.bfloat16),
            pltpu.VMEM((padded, orients, WIDE), jnp.float32),
            *staging,
        ],
        2 * 6 * width * orients * WIDE * WIDE,
        blocks,
        mine,
        other,
        out_space=out_space,
        room=room,
    )


def filter_kernel(
    orients, width, field, first, own, grad_ref, feat_ref, out_ref, feat_rows, grad_rows, held, done
):
    chip, core = here()
    slot = core if own else 1 - core
    in_width = grad_rows.shape[0]
    copies = [
        pltpu.make_async_copy(
            feat_ref.at[:, pl.ds(field * width, width), pl.ds(half * WIDE, WIDE)],
            held.at[:, half],
            done.at[half],
        )
        for half in range(2)
    ]
    for copy in copies:
        copy.start()
    interleave(grad_ref, grad_rows, orients, grad_ref.shape[1] - in_width, 0)
    grads = grad_rows[...].reshape(in_width * orients, WIDE).astype(jnp.bfloat16)
    for copy in copies:
        copy.wait()
    for g in range(orients):
        s = lax.rem(g + 2 * chip + slot, orients)
        feat_rows[:, g, :] = held[s // 2, lax.rem(s, 2)].astype(jnp.float32)
    feats = feat_rows[...].reshape(width * orients, WIDE).astype(jnp.bfloat16)
    for j in range(3):
        window = grads[(first - j) * orients : (first - j + width) * orients]
        product = lax.dot_general(
            feats,
            window,
            (((0,), (0,)), ((), ())),
            preferred_element_type=jnp.float32,
        )
        for i in range(3):
            total = None
            for row in range(ROWS):
                grad_row = row - i + 1
                if not 0 <= grad_row < ROWS:
                    continue
                piece = product[
                    row * CHAN : (row + 1) * CHAN, grad_row * CHAN : (grad_row + 1) * CHAN
                ]
                total = piece if total is None else total + piece
            out_ref[i, j] = total.astype(jnp.bfloat16)


def filter_terms(feats, field, width, grads, in_width, first):
    orients = 2 * feats.shape[0]

    def terms(own):
        return call(
            functools.partial(filter_kernel, orients, width, field, first, own),
            jax.ShapeDtypeStruct((3, 3, CHAN, CHAN), jnp.bfloat16),
            [
                pltpu.VMEM((width, orients, WIDE), jnp.float32),
                pltpu.VMEM((in_width, orients, WIDE), jnp.float32),
                pltpu.VMEM((orients // 2, 2, width, WIDE), jnp.bfloat16),
                pltpu.SemaphoreType.DMA((2,)),
            ],
            6 * width * orients * WIDE * WIDE,
            grads,
            feats,
            space=(VMEM, HBM),
            room=52,
        )

    theirs = lax.ppermute(terms(False), CORE, SWAP)
    return terms(True), theirs


def point_kernel(parts_ref, pre_ref, out_ref, held, done):
    total = parts_ref[0].astype(jnp.float32)
    for n in range(1, parts_ref.shape[0]):
        total = total + parts_ref[n].astype(jnp.float32)
    held[...] = (total * slope(pre_ref[...].astype(jnp.float32))).astype(jnp.bfloat16)
    copy_all([(held, out_ref.at[n]) for n in range(out_ref.shape[0])], done)


def exchange(parts, axes):
    return lax.all_to_all(parts, axes, 0, 0, tiled=True)


def chunks(pair):
    count = lax.axis_size(AZ)
    return [bank.reshape(count, -1, CHAN) for bank in pair]


def after(array, first):
    return lax.optimization_barrier((array, first))[0]


def halves_kernel(mine, theirs, stay_ref, leave_ref, both_ref):
    half = stay_ref.shape[0]
    side = lax.axis_index(AZ) // half
    both_ref[...] = mine[...].astype(jnp.float32) + theirs[...].astype(jnp.float32)
    stay_ref[...] = both_ref[pl.ds(side * half, half)].astype(jnp.bfloat16)
    leave_ref[...] = both_ref[pl.ds((1 - side) * half, half)].astype(jnp.bfloat16)


def deal_kernel(stay, came, out_ref):
    both = stay[...].astype(jnp.float32) + came[...].astype(jnp.float32)
    lines = both.reshape(-1, CHAN)
    count, size, _ = out_ref.shape
    for n in range(count):
        out_ref[n] = lines[n * size : (n + 1) * size].astype(jnp.bfloat16)


def half_terms(pair):
    mine, theirs = chunks(pair)
    count, size, _ = mine.shape
    half = jax.ShapeDtypeStruct((count // 2, size, CHAN), jnp.bfloat16)
    both = pltpu.VMEM(mine.shape, jnp.float32)
    stay, leave = call(halves_kernel, (half, half), [both], mine.size, mine, theirs)
    came = lax.ppermute(leave, AZ, [(i, (i + count // 2) % count) for i in range(count)])
    shape = jax.ShapeDtypeStruct((count, size // 2, CHAN), jnp.bfloat16)
    return leave, call(deal_kernel, shape, [], mine.size, stay, came)


def join_kernel(mine, theirs, also, out_ref, held, done):
    size = mine.shape[1]
    both = mine[...].astype(jnp.float32) + theirs[...].astype(jnp.float32)
    held[:, :size] = both.astype(jnp.bfloat16)
    held[:, size:] = also[...]
    copy_all([(held, out_ref)], done)


def joined_terms(pair, also):
    mine, theirs = chunks(pair)
    count, size, _ = mine.shape
    shape = jax.ShapeDtypeStruct((count, size + also.shape[1], CHAN), jnp.bfloat16)
    held = [pltpu.VMEM(shape.shape, jnp.bfloat16), pltpu.SemaphoreType.DMA((1,))]
    return call(join_kernel, shape, held, mine.size, mine, theirs, also, out_space=HBM)


def reduce_kernel(size, parts_ref, out_ref, held, done):
    count = parts_ref.shape[0]
    total = [parts_ref[n].astype(jnp.float32) for n in (0, count // 2)]
    for n in range(1, count // 2):
        total[0] = total[0] + parts_ref[n].astype(jnp.float32)
        total[1] = total[1] + parts_ref[count // 2 + n].astype(jnp.float32)
    whole = [total[0][:size] + total[1][:size], total[0][size:], total[1][size:]]
    held[...] = jnp.concatenate(whole).astype(jnp.bfloat16)
    copy_all([(held, out_ref.at[n]) for n in range(count)], done)


def finish_kernel(size, scale, whole_ref, one_ref, two_ref, held_one, held_two, done):
    count = whole_ref.shape[0]
    dealt = (whole_ref.shape[1] - size) // 2
    held_one[...] = whole_ref[:, :size].astype(jnp.float32) * scale
    first = pltpu.make_async_copy(held_one, one_ref, done.at[0])
    first.start()
    for side in range(2):
        for n in range(count):
            part = whole_ref[n, size:].astype(jnp.float32) * scale
            held_two[side, n * dealt : (n + 1) * dealt] = part[side * dealt : (side + 1) * dealt]
    second = pltpu.make_async_copy(held_two, two_ref, done.at[1])
    second.start()
    first.wait()
    second.wait()


def summed_over_az(joined, size, scale):
    count, both, _ = joined.shape
    dealt = both - size
    held = [pltpu.VMEM((size + 2 * dealt, CHAN), jnp.bfloat16), pltpu.SemaphoreType.DMA((count,))]
    shape = jax.ShapeDtypeStruct((count, size + 2 * dealt, CHAN), jnp.bfloat16)
    copies = call(
        functools.partial(reduce_kernel, size),
        shape,
        held,
        joined.size,
        exchange(joined, AZ),
        out_space=HBM,
    )
    one = (count, size, CHAN)
    two = (2, count * size // 2, CHAN)
    banks = call(
        functools.partial(finish_kernel, size, scale),
        (jax.ShapeDtypeStruct(one, jnp.float32), jax.ShapeDtypeStruct(two, jnp.float32)),
        [
            pltpu.VMEM(one, jnp.float32),
            pltpu.VMEM(two, jnp.float32),
            pltpu.SemaphoreType.DMA((2,)),
        ],
        joined.size,
        exchange(copies, AZ),
        out_space=HBM,
        room=52,
    )
    return tuple(bank.reshape(1, 3, 3, CHAN, CHAN) for bank in banks)


def stacked(act, given, grad, pre, side):
    half = act.shape[0] // 2
    zeros = jnp.zeros((8, CHAN), jnp.float32)
    if side == 0:
        grad = [zeros[:2], grad[: half + 2], zeros[:4]]
        pre = [zeros[:1], pre[: half + 1], zeros[:6]]
    else:
        grad = [grad[half - 2 :], zeros[:6]]
        pre = [pre[half - 1 :], zeros[:7]]
    own = slice(side * half, (side + 1) * half)
    return jnp.concatenate([act[own], given[own], *grad, *pre])


def lanes_kernel(*refs):
    given, (mine_ref, away_ref, same_ref, cross_ref) = refs[:4], refs[4:8]
    held, done = refs[8:12], refs[12]
    _, core = here()
    copy_all(zip(given, held), done)
    inputs_ref, pre_one_ref, pre_two_ref, cotangent_ref = held
    for row in range(ROWS):
        lanes = slice(row * CHAN, (row + 1) * CHAN)
        pre = pre_one_ref[0, row].astype(jnp.float32)
        grad = cotangent_ref[0, row].astype(jnp.float32) * slope(
            pre_two_ref[0, row].astype(jnp.float32)
        )
        act = pre / (1.0 + jnp.exp(-pre))
        fields = (act, inputs_ref[0, row].astype(jnp.float32), grad, pre)
        left, right = stacked(*fields, 0), stacked(*fields, 1)
        mine_ref[:, lanes] = jnp.where(core == 0, left, right).astype(jnp.bfloat16)
        away_ref[:, lanes] = jnp.where(core == 0, right, left).astype(jnp.bfloat16)
        pad = jnp.zeros((5, CHAN), jnp.float32)
        low = jnp.concatenate([grad[:2], pre[:1], pad])
        high = jnp.concatenate([grad[-2:], pre[-1:], pad])
        same_ref[:, lanes] = jnp.where(core == 0, high, low).astype(jnp.bfloat16)
        cross_ref[:, lanes] = jnp.where(core == 0, low, high).astype(jnp.bfloat16)


def rims_kernel(mine_ref, partner_ref, same_ref, cross_ref, out_ref, pre_ref, held, done):
    _, core = here()
    ahead = held.shape[0] - pre_ref.shape[0]
    rows = pre_ref.shape[0]
    used = rows - 8
    at = lax.broadcasted_iota(jnp.int32, (rows, WIDE), 0)
    grad_at = jnp.where(core == 0, 0, used + 2)
    pre_at = jnp.where(core == 0, 0, used + 1)
    filled = []
    for body_ref, edge_ref in ((mine_ref, same_ref), (partner_ref, cross_ref)):
        body = body_ref[...].astype(jnp.float32)
        edge = edge_ref[...].astype(jnp.float32)
        grad = body[ahead : ahead + rows]
        grad = jnp.where(at == grad_at, edge[0:1], grad)
        grad = jnp.where(at == grad_at + 1, edge[1:2], grad)
        pre = jnp.where(at == pre_at, edge[2:3], body[ahead + rows :])
        filled.append(jnp.concatenate([body[:ahead], grad, pre]).astype(jnp.bfloat16))
    first = jnp.where(core == 0, filled[0], filled[1])
    second = jnp.where(core == 0, filled[1], filled[0])
    for lanes, part in ((slice(0, WIDE), first), (slice(WIDE, 2 * WIDE), second)):
        held[:, lanes] = part[: ahead + rows]
        pre_ref[:, lanes] = part[ahead + rows :]
    copy_all([(held, out_ref.at[n]) for n in range(out_ref.shape[0])], done)


def shards(inputs, pre_one, pre_two, cotangent, filt_one, filt_two):
    columns = inputs.shape[2]
    half = columns // 2
    core = lax.axis_index(CORE)
    az_count = lax.axis_size(AZ)
    rot_count = lax.axis_size(ROT)
    chips = lax.axis_size(CHIPS)
    cell_count = rot_count * inputs.shape[1] * columns * az_count
    scale = cell_count ** (-0.5)
    padded = half + 8

    def narrow(*shape):
        return jax.ShapeDtypeStruct(shape, jnp.bfloat16)

    rows = columns + 2 * padded
    mine, away, same, cross = call(
        lanes_kernel,
        (narrow(rows, WIDE), narrow(rows, WIDE), narrow(8, WIDE), narrow(8, WIDE)),
        [pltpu.VMEM(inputs.shape, jnp.bfloat16)] * 4 + [pltpu.SemaphoreType.DMA((4,))],
        inputs.size * 20,
        inputs,
        pre_one,
        pre_two,
        cotangent,
        space=HBM,
        room=60,
    )
    after_me = [(i, (i + 1) % az_count) for i in range(az_count)]
    before_me = [(i, (i - 1) % az_count) for i in range(az_count)]
    place = lambda c, pairs, d: [(c * az_count + i, d * az_count + j) for i, j in pairs]
    same = lax.ppermute(same, (CORE, AZ), place(0, after_me, 0) + place(1, before_me, 1))
    cross = lax.ppermute(cross, (CORE, AZ), place(1, after_me, 0) + place(0, before_me, 1))
    partner = lax.ppermute(away, CORE, SWAP)
    mine = mine + lax.shift_right_logical(core, 1).astype(mine.dtype)
    sent, pre_pair = call(
        rims_kernel,
        (narrow(chips, columns + padded, 2 * WIDE), narrow(padded, 2 * WIDE)),
        [
            pltpu.VMEM((columns + padded, 2 * WIDE), jnp.bfloat16),
            pltpu.SemaphoreType.DMA((chips,)),
        ],
        inputs.size * 20,
        mine,
        partner,
        same,
        cross,
        out_space=(HBM, VMEM),
    )
    other_two = lax.ppermute(filt_two[0], CORE, SWAP)
    other_one = lax.ppermute(filt_one[0], CORE, SWAP)
    first_blocks = exchange(after(sent, (other_two, other_one)), CHIPS)

    shares = conv(
        conv_two_kernel,
        first_blocks,
        padded,
        filt_two[0],
        other_two,
        half + 2,
        padded,
        (chips, padded, 2 * WIDE),
        [
            pltpu.VMEM((chips, padded, 2 * WIDE), jnp.bfloat16),
            pltpu.SemaphoreType.DMA((chips,)),
        ],
        HBM,
        52,
    )
    pair_two = filter_terms(first_blocks, 0, half, first_blocks, padded, 3)
    leave, terms_two = half_terms(pair_two)
    arrived = after(exchange(shares, CHIPS), leave)
    copies = call(
        point_kernel,
        narrow(chips, padded, 2 * WIDE),
        [pltpu.VMEM((padded, 2 * WIDE), jnp.bfloat16), pltpu.SemaphoreType.DMA((chips,))],
        arrived.size,
        arrived,
        pre_pair,
        out_space=HBM,
    )
    all_grad_one = after(exchange(copies, CHIPS), terms_two)
    joined = joined_terms(filter_terms(first_blocks, 1, half, all_grad_one, padded, 2), terms_two)
    filt_grad_one, filt_grad_two = summed_over_az(joined, filt_one.size // CHAN // az_count, scale)

    along_x = lax.axis_size(CHIPS[0])

    shares = conv(
        conv_one_kernel,
        after(all_grad_one, joined),
        padded,
        filt_one[0],
        other_one,
        half,
        half,
        (2, along_x, half, 2 * WIDE),
    )
    arrived_y = lax.ppermute(shares[1], CHIPS[1], SWAP)
    partial = (shares[0].astype(jnp.float32) + arrived_y.astype(jnp.float32)).astype(jnp.bfloat16)
    total = partial[0].astype(jnp.float32)
    for step in range(1, along_x):
        came = lax.ppermute(
            partial[step], CHIPS[0], [(i, (i + step) % along_x) for i in range(along_x)]
        )
        total = total + came.astype(jnp.float32)
    total = total.astype(jnp.bfloat16)
    left, right = total[:, :WIDE], total[:, WIDE:]
    mine = jnp.where(core == 0, left, right)
    theirs = lax.ppermute(jnp.where(core == 0, right, left), CORE, SWAP)
    whole = jnp.where(core == 0, jnp.concatenate([mine, theirs]), jnp.concatenate([theirs, mine]))
    input_grad = jnp.moveaxis(whole.reshape(columns, ROWS, CHAN), 1, 0)[None]
    return input_grad, filt_grad_one, filt_grad_two


def solution(mesh):
    finer = Mesh(mesh.devices.reshape(4, 2, 2, mesh.shape["az"]), (*ROT, AZ))
    field = P(ROT, None, AZ, None)
    bank = P(ROT, None, None, None, None)
    return jax.shard_map(
        shards,
        mesh=finer,
        in_specs=(field, field, field, field, bank, bank),
        out_specs=(field, bank, bank),
        check_vma=False,
    )
```

```python
import functools

import jax
import jax.numpy as jnp
from jax import lax
from jax.experimental import pallas as pl
from jax.experimental.pallas import tpu as pltpu
from jax.sharding import Mesh
from jax.sharding import PartitionSpec as P

CHIPS = ("rot_x", "rot_y")
CORE = "rot_c"
ROT = (*CHIPS, CORE)
AZ = "az"

ROWS = 4
CHAN = 128
WIDE = ROWS * CHAN
SWAP = [(0, 1), (1, 0)]
VMEM = pl.BlockSpec(memory_space=pltpu.VMEM)
HBM = pl.BlockSpec(memory_space=pltpu.HBM)


def slope(pre):
    logistic = 1.0 / (1.0 + jnp.exp(-pre))
    return logistic * (1.0 + pre * (1.0 - logistic))


def params(mebibytes):
    return pltpu.CompilerParams(vmem_limit_bytes=mebibytes * 1024 * 1024)


def here():
    return lax.axis_index(CHIPS[0]) * 2 + lax.axis_index(CHIPS[1]), lax.axis_index(CORE)


def call(kernel, out_shape, scratch, flops, *operands, space=VMEM, out_space=VMEM, room=40):
    n_bytes = sum(a.size * a.dtype.itemsize for a in operands)
    in_specs = list(space) if isinstance(space, tuple) else [space] * len(operands)
    out_specs = out_space
    if not isinstance(out_space, tuple):
        out_specs = jax.tree.map(lambda _: out_space, out_shape)
    return pl.pallas_call(
        kernel,
        out_shape=out_shape,
        in_specs=in_specs,
        out_specs=out_specs,
        scratch_shapes=scratch,
        compiler_params=params(room),
        cost_estimate=pl.CostEstimate(flops=flops, bytes_accessed=2 * n_bytes, transcendentals=0),
    )(*operands)


def copy_all(pairs, done):
    copies = [pltpu.make_async_copy(a, b, done.at[n]) for n, (a, b) in enumerate(pairs)]
    for copy in copies:
        copy.start()
    for copy in copies:
        copy.wait()


def lanes_of(row):
    return slice(row * CHAN, (row + 1) * CHAN)


def interleave(blocks_ref, rows_ref, stage):
    in_width, orients, _ = rows_ref.shape
    lines = blocks_ref.shape[2] == CHAN
    for n in range(orients // 2):
        if lines:
            stage[n] = blocks_ref[n].astype(jnp.float32).reshape(stage.shape[1:])
        for half in range(2):
            g = 2 * n + half
            if not lines:
                lanes = slice(half * WIDE, (half + 1) * WIDE)
                first = blocks_ref.shape[1] - in_width
                rows_ref[:, g, :] = blocks_ref[n, first:, lanes].astype(jnp.float32)
                continue
            for row in range(ROWS):
                rows_ref[:, g, lanes_of(row)] = stage[n, :, half * ROWS + row, :]


def band_weights(filt_ref, band_ref, slot):
    zero = jnp.zeros((CHAN, CHAN), jnp.bfloat16)
    for j in range(3):
        for out_row in range(ROWS):
            for in_row in range(ROWS):
                i = out_row - in_row + 1
                piece = filt_ref[i, j] if 0 <= i < 3 else zero
                band_ref[
                    slot,
                    j,
                    out_row * CHAN : (out_row + 1) * CHAN,
                    in_row * CHAN : (in_row + 1) * CHAN,
                ] = piece


def rotation_sums(orients, width, blocks_ref, mine_ref, other_ref, rows_0, rows_1, band, stage):
    in_width = rows_0.shape[0]
    _, core = here()
    band_weights(mine_ref, band, core)
    band_weights(other_ref, band, 1 - core)
    interleave(blocks_ref, rows_0, stage)
    for g in range(orients):
        rows_1[:, g, :] = rows_0[:, (g - 1) % orients, :]
    total = None
    for slot, rows in ((0, rows_0), (1, rows_1)):
        flat = rows[...].reshape(in_width * orients, WIDE).astype(jnp.bfloat16)
        for j in range(3):
            window = flat[(2 - j) * orients : (2 - j + width) * orients]
            term = lax.dot_general(
                window,
                band[slot, j],
                (((1,), (1,)), ((), ())),
                preferred_element_type=jnp.float32,
            )
            total = term if total is None else total + term
    return total.reshape(width, orients, WIDE)


def conv_two_kernel(orients, width, blocks_ref, mine_ref, other_ref, out_ref, *scratch):
    *rows, stage, sums, held, done = scratch
    chip, _ = here()
    sums[...] = rotation_sums(orients, width, blocks_ref, mine_ref, other_ref, *rows, stage)
    chips = orients // 2
    copies = []
    for pair in range(chips):
        for half in range(2):
            for row in range(ROWS):
                stage[pair, :, half * ROWS + row, :] = sums[:, 2 * pair + half, lanes_of(row)]
        held[pair] = stage[pair].reshape(held.shape[1:]).astype(jnp.bfloat16)
        to = lax.rem(pair + chip, chips)
        copies.append(pltpu.make_async_copy(held.at[pair], out_ref.at[to], done.at[pair]))
        copies[-1].start()
    for copy in copies:
        copy.wait()


def conv_one_kernel(orients, width, blocks_ref, mine_ref, other_ref, out_ref, *scratch):
    *rows, stage, sums = scratch
    chip, _ = here()
    sums[...] = rotation_sums(orients, width, blocks_ref, mine_ref, other_ref, *rows, stage)
    chips = orients // 2
    across = out_ref.shape[1]
    for pair in range(chips):
        to = lax.rem(pair + chip, chips)
        other = lax.rem(to + chip, 2)
        step = lax.rem(to // 2 - chip // 2 + across, across)
        for half in range(2):
            out_ref[other, step, :, half * WIDE : (half + 1) * WIDE] = sums[
                :, 2 * pair + half, :
            ].astype(jnp.bfloat16)


def conv(kernel, blocks, in_width, lined, mine, other, width, padded, out_shape, staging=(), out_space=VMEM, room=40):
    orients = 2 * blocks.shape[0]
    return call(
        functools.partial(kernel, orients, width),
        jax.ShapeDtypeStruct(out_shape, jnp.bfloat16),
        [
            pltpu.VMEM((in_width, orients, WIDE), jnp.float32),
            pltpu.VMEM((in_width, orients, WIDE), jnp.float32),
            pltpu.VMEM((2, 3, WIDE, WIDE), jnp.bfloat16),
            pltpu.VMEM((orients // 2, lined, 2 * ROWS, CHAN), jnp.float32),
            pltpu.VMEM((padded, orients, WIDE), jnp.float32),
            *staging,
        ],
        2 * 6 * width * orients * WIDE * WIDE,
        blocks,
        mine,
        other,
        out_space=out_space,
        room=room,
    )


def filter_kernel(
    orients, width, field, first, own, grad_ref, feat_ref, out_ref, feat_rows, grad_rows, stage, held, done
):
    chip, core = here()
    slot = core if own else 1 - core
    in_width = grad_rows.shape[0]
    copies = [
        pltpu.make_async_copy(
            feat_ref.at[:, pl.ds(field * width, width), pl.ds(half * WIDE, WIDE)],
            held.at[:, half],
            done.at[half],
        )
        for half in range(2)
    ]
    for copy in copies:
        copy.start()
    interleave(grad_ref, grad_rows, stage)
    grads = grad_rows[...].reshape(in_width * orients, WIDE).astype(jnp.bfloat16)
    for copy in copies:
        copy.wait()
    for g in range(orients):
        s = lax.rem(g + 2 * chip + slot, orients)
        feat_rows[:, g, :] = held[s // 2, lax.rem(s, 2)].astype(jnp.float32)
    feats = feat_rows[...].reshape(width * orients, WIDE).astype(jnp.bfloat16)
    for j in range(3):
        window = grads[(first - j) * orients : (first - j + width) * orients]
        product = lax.dot_general(
            feats,
            window,
            (((0,), (0,)), ((), ())),
            preferred_element_type=jnp.float32,
        )
        for i in range(3):
            total = None
            for row in range(ROWS):
                grad_row = row - i + 1
                if not 0 <= grad_row < ROWS:
                    continue
                piece = product[
                    row * CHAN : (row + 1) * CHAN, grad_row * CHAN : (grad_row + 1) * CHAN
                ]
                total = piece if total is None else total + piece
            out_ref[i, j] = total.astype(jnp.bfloat16)


def filter_terms(feats, field, width, grads, in_width, first):
    orients = 2 * feats.shape[0]

    def terms(own):
        return call(
            functools.partial(filter_kernel, orients, width, field, first, own),
            jax.ShapeDtypeStruct((3, 3, CHAN, CHAN), jnp.bfloat16),
            [
                pltpu.VMEM((width, orients, WIDE), jnp.float32),
                pltpu.VMEM((in_width, orients, WIDE), jnp.float32),
                pltpu.VMEM((orients // 2, in_width, 2 * ROWS, CHAN), jnp.float32),
                pltpu.VMEM((orients // 2, 2, width, WIDE), jnp.bfloat16),
                pltpu.SemaphoreType.DMA((2,)),
            ],
            6 * width * orients * WIDE * WIDE,
            grads,
            feats,
            space=(VMEM, HBM),
            room=52,
        )

    theirs = lax.ppermute(terms(False), CORE, SWAP)
    return terms(True), theirs


def point_kernel(parts_ref, pre_ref, out_ref, held, done):
    total = parts_ref[0].astype(jnp.float32)
    for n in range(1, parts_ref.shape[0]):
        total = total + parts_ref[n].astype(jnp.float32)
    held[...] = (total * slope(pre_ref[...].astype(jnp.float32))).astype(jnp.bfloat16)
    copy_all([(held, out_ref.at[n]) for n in range(out_ref.shape[0])], done)


def exchange(parts, axes):
    return lax.all_to_all(parts, axes, 0, 0, tiled=True)


def chunks(pair):
    count = lax.axis_size(AZ)
    return [bank.reshape(count, -1, CHAN) for bank in pair]


def after(array, first):
    return lax.optimization_barrier((array, first))[0]


def halves_kernel(mine, theirs, stay_ref, leave_ref, both_ref):
    half = stay_ref.shape[0]
    side = lax.axis_index(AZ) // half
    both_ref[...] = mine[...].astype(jnp.float32) + theirs[...].astype(jnp.float32)
    stay_ref[...] = both_ref[pl.ds(side * half, half)].astype(jnp.bfloat16)
    leave_ref[...] = both_ref[pl.ds((1 - side) * half, half)].astype(jnp.bfloat16)


def deal_kernel(stay, came, out_ref):
    both = stay[...].astype(jnp.float32) + came[...].astype(jnp.float32)
    lines = both.reshape(-1, CHAN)
    count, size, _ = out_ref.shape
    for n in range(count):
        out_ref[n] = lines[n * size : (n + 1) * size].astype(jnp.bfloat16)


def half_terms(pair):
    mine, theirs = chunks(pair)
    count, size, _ = mine.shape
    half = jax.ShapeDtypeStruct((count // 2, size, CHAN), jnp.bfloat16)
    both = pltpu.VMEM(mine.shape, jnp.float32)
    stay, leave = call(halves_kernel, (half, half), [both], mine.size, mine, theirs)
    came = lax.ppermute(leave, AZ, [(i, (i + count // 2) % count) for i in range(count)])
    shape = jax.ShapeDtypeStruct((count, size // 2, CHAN), jnp.bfloat16)
    return call(deal_kernel, shape, [], mine.size, stay, came)


def join_kernel(mine, theirs, also, out_ref, held, done):
    size = mine.shape[1]
    both = mine[...].astype(jnp.float32) + theirs[...].astype(jnp.float32)
    held[:, :size] = both.astype(jnp.bfloat16)
    held[:, size:] = also[...]
    copy_all([(held, out_ref)], done)


def joined_terms(pair, also):
    mine, theirs = chunks(pair)
    count, size, _ = mine.shape
    shape = jax.ShapeDtypeStruct((count, size + also.shape[1], CHAN), jnp.bfloat16)
    held = [pltpu.VMEM(shape.shape, jnp.bfloat16), pltpu.SemaphoreType.DMA((1,))]
    return call(join_kernel, shape, held, mine.size, mine, theirs, also, out_space=HBM)


def reduce_kernel(size, parts_ref, out_ref, held, done):
    count = parts_ref.shape[0]
    total = [parts_ref[n].astype(jnp.float32) for n in (0, count // 2)]
    for n in range(1, count // 2):
        total[0] = total[0] + parts_ref[n].astype(jnp.float32)
        total[1] = total[1] + parts_ref[count // 2 + n].astype(jnp.float32)
    whole = [total[0][:size] + total[1][:size], total[0][size:], total[1][size:]]
    held[...] = jnp.concatenate(whole).astype(jnp.bfloat16)
    copy_all([(held, out_ref.at[n]) for n in range(count)], done)


def finish_kernel(size, scale, whole_ref, one_ref, two_ref, held_one, held_two, done):
    count = whole_ref.shape[0]
    dealt = (whole_ref.shape[1] - size) // 2
    held_one[...] = whole_ref[:, :size].astype(jnp.float32) * scale
    first = pltpu.make_async_copy(held_one, one_ref, done.at[0])
    first.start()
    for side in range(2):
        for n in range(count):
            part = whole_ref[n, size:].astype(jnp.float32) * scale
            held_two[side, n * dealt : (n + 1) * dealt] = part[side * dealt : (side + 1) * dealt]
    second = pltpu.make_async_copy(held_two, two_ref, done.at[1])
    second.start()
    first.wait()
    second.wait()


def summed_over_az(joined, size, scale):
    count, both, _ = joined.shape
    dealt = both - size
    held = [pltpu.VMEM((size + 2 * dealt, CHAN), jnp.bfloat16), pltpu.SemaphoreType.DMA((count,))]
    shape = jax.ShapeDtypeStruct((count, size + 2 * dealt, CHAN), jnp.bfloat16)
    copies = call(
        functools.partial(reduce_kernel, size),
        shape,
        held,
        joined.size,
        exchange(joined, AZ),
        out_space=HBM,
    )
    one = (count, size, CHAN)
    two = (2, count * size // 2, CHAN)
    banks = call(
        functools.partial(finish_kernel, size, scale),
        (jax.ShapeDtypeStruct(one, jnp.float32), jax.ShapeDtypeStruct(two, jnp.float32)),
        [
            pltpu.VMEM(one, jnp.float32),
            pltpu.VMEM(two, jnp.float32),
            pltpu.SemaphoreType.DMA((2,)),
        ],
        joined.size,
        exchange(copies, AZ),
        out_space=HBM,
        room=52,
    )
    return tuple(bank.reshape(1, 3, 3, CHAN, CHAN) for bank in banks)


def stacked(act, given, grad, pre, side):
    half = act.shape[0] // 2
    zeros = jnp.zeros((8, CHAN), jnp.float32)
    if side == 0:
        grad = [zeros[:2], grad[: half + 2], zeros[:4]]
        pre = [zeros[:1], pre[: half + 1], zeros[:6]]
    else:
        grad = [grad[half - 2 :], zeros[:6]]
        pre = [pre[half - 1 :], zeros[:7]]
    own = slice(side * half, (side + 1) * half)
    return jnp.concatenate([act[own], given[own], *grad, *pre])


def lanes_kernel(*refs):
    given, (mine_ref, away_ref, same_ref, cross_ref) = refs[:4], refs[4:8]
    held, done = refs[8:12], refs[12]
    _, core = here()
    copy_all(zip(given, held), done)
    inputs_ref, pre_one_ref, pre_two_ref, cotangent_ref = held
    for row in range(ROWS):
        lanes = slice(row * CHAN, (row + 1) * CHAN)
        pre = pre_one_ref[0, row].astype(jnp.float32)
        grad = cotangent_ref[0, row].astype(jnp.float32) * slope(
            pre_two_ref[0, row].astype(jnp.float32)
        )
        act = pre / (1.0 + jnp.exp(-pre))
        fields = (act, inputs_ref[0, row].astype(jnp.float32), grad, pre)
        left, right = stacked(*fields, 0), stacked(*fields, 1)
        mine_ref[:, lanes] = jnp.where(core == 0, left, right).astype(jnp.bfloat16)
        away_ref[:, lanes] = jnp.where(core == 0, right, left).astype(jnp.bfloat16)
        pad = jnp.zeros((5, CHAN), jnp.float32)
        low = jnp.concatenate([grad[:2], pre[:1], pad])
        high = jnp.concatenate([grad[-2:], pre[-1:], pad])
        same_ref[:, lanes] = jnp.where(core == 0, high, low).astype(jnp.bfloat16)
        cross_ref[:, lanes] = jnp.where(core == 0, low, high).astype(jnp.bfloat16)


def rims_kernel(mine_ref, partner_ref, same_ref, cross_ref, out_ref, pre_ref, held, stage, done):
    _, core = here()
    rows = mine_ref.shape[0] - held.shape[0]
    ahead = held.shape[0] - rows
    used = rows - 8
    at = lax.broadcasted_iota(jnp.int32, (rows, WIDE), 0)
    grad_at = jnp.where(core == 0, 0, used + 2)
    pre_at = jnp.where(core == 0, 0, used + 1)
    filled = []
    for body_ref, edge_ref in ((mine_ref, same_ref), (partner_ref, cross_ref)):
        body = body_ref[...].astype(jnp.float32)
        edge = edge_ref[...].astype(jnp.float32)
        grad = body[ahead : ahead + rows]
        grad = jnp.where(at == grad_at, edge[0:1], grad)
        grad = jnp.where(at == grad_at + 1, edge[1:2], grad)
        pre = jnp.where(at == pre_at, edge[2:3], body[ahead + rows :])
        filled.append(jnp.concatenate([body[:ahead], grad, pre]).astype(jnp.bfloat16))
    first = jnp.where(core == 0, filled[0], filled[1])
    second = jnp.where(core == 0, filled[1], filled[0])
    for half, part in enumerate((first, second)):
        held[:, half * WIDE : (half + 1) * WIDE] = part[: ahead + rows]
        pre = part[ahead + rows :].astype(jnp.float32)[: stage.shape[0]]
        for row in range(ROWS):
            stage[:, half * ROWS + row, :] = pre[:, lanes_of(row)]
    pre_ref[...] = stage[...].reshape(pre_ref.shape).astype(jnp.bfloat16)
    copy_all([(held, out_ref.at[n]) for n in range(out_ref.shape[0])], done)


def shards(inputs, pre_one, pre_two, cotangent, filt_one, filt_two):
    columns = inputs.shape[2]
    half = columns // 2
    core = lax.axis_index(CORE)
    az_count = lax.axis_size(AZ)
    rot_count = lax.axis_size(ROT)
    chips = lax.axis_size(CHIPS)
    cell_count = rot_count * inputs.shape[1] * columns * az_count
    scale = cell_count ** (-0.5)
    padded = half + 8
    lined = half + 2

    def narrow(*shape):
        return jax.ShapeDtypeStruct(shape, jnp.bfloat16)

    rows = columns + 2 * padded
    mine, away, same, cross = call(
        lanes_kernel,
        (narrow(rows, WIDE), narrow(rows, WIDE), narrow(8, WIDE), narrow(8, WIDE)),
        [pltpu.VMEM(inputs.shape, jnp.bfloat16)] * 4 + [pltpu.SemaphoreType.DMA((4,))],
        inputs.size * 20,
        inputs,
        pre_one,
        pre_two,
        cotangent,
        space=HBM,
        room=60,
    )
    after_me = [(i, (i + 1) % az_count) for i in range(az_count)]
    before_me = [(i, (i - 1) % az_count) for i in range(az_count)]
    place = lambda c, pairs, d: [(c * az_count + i, d * az_count + j) for i, j in pairs]
    same = lax.ppermute(same, (CORE, AZ), place(0, after_me, 0) + place(1, before_me, 1))
    cross = lax.ppermute(cross, (CORE, AZ), place(1, after_me, 0) + place(0, before_me, 1))
    partner = lax.ppermute(away, CORE, SWAP)
    mine = mine + lax.shift_right_logical(core, 1).astype(mine.dtype)
    sent, pre_pair = call(
        rims_kernel,
        (narrow(chips, columns + padded, 2 * WIDE), narrow(lined * 2 * ROWS, CHAN)),
        [
            pltpu.VMEM((columns + padded, 2 * WIDE), jnp.bfloat16),
            pltpu.VMEM((lined, 2 * ROWS, CHAN), jnp.float32),
            pltpu.SemaphoreType.DMA((chips,)),
        ],
        inputs.size * 20,
        mine,
        partner,
        same,
        cross,
        out_space=(HBM, VMEM),
    )
    other_two = lax.ppermute(filt_two[0], CORE, SWAP)
    first_blocks = exchange(after(sent, other_two), CHIPS)

    shares = conv(
        conv_two_kernel,
        first_blocks,
        padded,
        lined,
        filt_two[0],
        other_two,
        lined,
        lined,
        (chips, lined * 2 * ROWS, CHAN),
        [
            pltpu.VMEM((chips, lined * 2 * ROWS, CHAN), jnp.bfloat16),
            pltpu.SemaphoreType.DMA((chips,)),
        ],
        HBM,
        52,
    )
    late_blocks = after(first_blocks, shares)
    pair_two = filter_terms(late_blocks, 0, half, late_blocks, padded, 3)
    terms_two = half_terms(pair_two)
    arrived = after(exchange(shares, CHIPS), pair_two[0])
    copies = call(
        point_kernel,
        narrow(chips, *pre_pair.shape),
        [pltpu.VMEM(pre_pair.shape, jnp.bfloat16), pltpu.SemaphoreType.DMA((chips,))],
        arrived.size,
        arrived,
        pre_pair,
        out_space=HBM,
    )
    all_grad_one = after(exchange(copies, CHIPS), terms_two)
    joined = joined_terms(filter_terms(first_blocks, 1, half, all_grad_one, lined, 2), terms_two)
    filt_grad_one, filt_grad_two = summed_over_az(joined, filt_one.size // CHAN // az_count, scale)

    along_x = lax.axis_size(CHIPS[0])

    other_one = lax.ppermute(after(filt_one[0], joined), CORE, SWAP)

    shares = conv(
        conv_one_kernel,
        after(all_grad_one, joined),
        lined,
        lined,
        filt_one[0],
        other_one,
        half,
        half,
        (2, along_x, half, 2 * WIDE),
    )
    arrived_y = lax.ppermute(shares[1], CHIPS[1], SWAP)
    partial = (shares[0].astype(jnp.float32) + arrived_y.astype(jnp.float32)).astype(jnp.bfloat16)
    total = partial[0].astype(jnp.float32)
    for step in range(1, along_x):
        came = lax.ppermute(
            partial[step], CHIPS[0], [(i, (i + step) % along_x) for i in range(along_x)]
        )
        total = total + came.astype(jnp.float32)
    total = total.astype(jnp.bfloat16)
    left, right = total[:, :WIDE], total[:, WIDE:]
    mine = jnp.where(core == 0, left, right)
    theirs = lax.ppermute(jnp.where(core == 0, right, left), CORE, SWAP)
    whole = jnp.where(core == 0, jnp.concatenate([mine, theirs]), jnp.concatenate([theirs, mine]))
    input_grad = jnp.moveaxis(whole.reshape(columns, ROWS, CHAN), 1, 0)[None]
    return input_grad, filt_grad_one, filt_grad_two


def solution(mesh):
    finer = Mesh(mesh.devices.reshape(4, 2, 2, mesh.shape["az"]), (*ROT, AZ))
    field = P(ROT, None, AZ, None)
    bank = P(ROT, None, None, None, None)
    return jax.shard_map(
        shards,
        mesh=finer,
        in_specs=(field, field, field, field, bank, bank),
        out_specs=(field, bank, bank),
        check_vma=False,
    )
```

```python
import functools

import jax
import jax.numpy as jnp
from jax import lax
from jax.experimental import pallas as pl
from jax.experimental.pallas import tpu as pltpu
from jax.sharding import Mesh
from jax.sharding import PartitionSpec as P

CHIPS = ("rot_x", "rot_y")
CORE = "rot_c"
ROT = (*CHIPS, CORE)
AZ = "az"

ROWS = 4
CHAN = 128
WIDE = ROWS * CHAN
SWAP = [(0, 1), (1, 0)]
VMEM = pl.BlockSpec(memory_space=pltpu.VMEM)
HBM = pl.BlockSpec(memory_space=pltpu.HBM)


def slope(pre):
    logistic = 1.0 / (1.0 + jnp.exp(-pre))
    return logistic * (1.0 + pre * (1.0 - logistic))


def params(mebibytes):
    return pltpu.CompilerParams(vmem_limit_bytes=mebibytes * 1024 * 1024)


def here():
    return lax.axis_index(CHIPS[0]) * 2 + lax.axis_index(CHIPS[1]), lax.axis_index(CORE)


def call(kernel, out_shape, scratch, flops, *operands, space=VMEM, out_space=VMEM, room=40):
    n_bytes = sum(a.size * a.dtype.itemsize for a in operands)
    in_specs = list(space) if isinstance(space, tuple) else [space] * len(operands)
    out_specs = out_space
    if not isinstance(out_space, tuple):
        out_specs = jax.tree.map(lambda _: out_space, out_shape)
    return pl.pallas_call(
        kernel,
        out_shape=out_shape,
        in_specs=in_specs,
        out_specs=out_specs,
        scratch_shapes=scratch,
        compiler_params=params(room),
        cost_estimate=pl.CostEstimate(flops=flops, bytes_accessed=2 * n_bytes, transcendentals=0),
    )(*operands)


def copy_all(pairs, done):
    copies = [pltpu.make_async_copy(a, b, done.at[n]) for n, (a, b) in enumerate(pairs)]
    for copy in copies:
        copy.start()
    for copy in copies:
        copy.wait()


def lanes_of(row):
    return slice(row * CHAN, (row + 1) * CHAN)


def interleave(blocks_ref, rows_ref, stage):
    in_width, orients, _ = rows_ref.shape
    lines = blocks_ref.shape[2] == CHAN
    for n in range(orients // 2):
        if lines:
            stage[n] = blocks_ref[n].astype(jnp.float32).reshape(stage.shape[1:])
        for half in range(2):
            g = 2 * n + half
            if not lines:
                lanes = slice(half * WIDE, (half + 1) * WIDE)
                first = blocks_ref.shape[1] - in_width
                rows_ref[:, g, :] = blocks_ref[n, first:, lanes].astype(jnp.float32)
                continue
            for row in range(ROWS):
                rows_ref[:, g, lanes_of(row)] = stage[n, :, half * ROWS + row, :]


def band_weights(filt_ref, band_ref, slot):
    zero = jnp.zeros((CHAN, CHAN), jnp.bfloat16)
    for j in range(3):
        for out_row in range(ROWS):
            for in_row in range(ROWS):
                i = out_row - in_row + 1
                piece = filt_ref[i, j] if 0 <= i < 3 else zero
                band_ref[
                    slot,
                    j,
                    out_row * CHAN : (out_row + 1) * CHAN,
                    in_row * CHAN : (in_row + 1) * CHAN,
                ] = piece


def rotation_sums(orients, width, blocks_ref, mine_ref, other_ref, rows_0, rows_1, band, stage):
    in_width = rows_0.shape[0]
    _, core = here()
    band_weights(mine_ref, band, core)
    band_weights(other_ref, band, 1 - core)
    interleave(blocks_ref, rows_0, stage)
    for g in range(orients):
        rows_1[:, g, :] = rows_0[:, (g - 1) % orients, :]
    total = None
    for slot, rows in ((0, rows_0), (1, rows_1)):
        flat = rows[...].reshape(in_width * orients, WIDE).astype(jnp.bfloat16)
        for j in range(3):
            window = flat[(2 - j) * orients : (2 - j + width) * orients]
            term = lax.dot_general(
                window,
                band[slot, j],
                (((1,), (1,)), ((), ())),
                preferred_element_type=jnp.float32,
            )
            total = term if total is None else total + term
    return total.reshape(width, orients, WIDE)


def conv_two_kernel(orients, width, blocks_ref, mine_ref, other_ref, out_ref, *scratch):
    *rows, stage, sums, held, done = scratch
    chip, _ = here()
    sums[...] = rotation_sums(orients, width, blocks_ref, mine_ref, other_ref, *rows, stage)
    chips = orients // 2
    copies = []
    for pair in range(chips):
        for half in range(2):
            for row in range(ROWS):
                stage[pair, :, half * ROWS + row, :] = sums[:, 2 * pair + half, lanes_of(row)]
        held[pair] = stage[pair].reshape(held.shape[1:]).astype(jnp.bfloat16)
        to = lax.rem(pair + chip, chips)
        copies.append(pltpu.make_async_copy(held.at[pair], out_ref.at[to], done.at[pair]))
        copies[-1].start()
    for copy in copies:
        copy.wait()


def conv_one_kernel(orients, width, blocks_ref, mine_ref, other_ref, out_ref, *scratch):
    *rows, stage, sums = scratch
    chip, _ = here()
    sums[...] = rotation_sums(orients, width, blocks_ref, mine_ref, other_ref, *rows, stage)
    chips = orients // 2
    across = out_ref.shape[1]
    for pair in range(chips):
        to = lax.rem(pair + chip, chips)
        other = lax.rem(to + chip, 2)
        step = lax.rem(to // 2 - chip // 2 + across, across)
        for half in range(2):
            out_ref[other, step, :, half * WIDE : (half + 1) * WIDE] = sums[
                :, 2 * pair + half, :
            ].astype(jnp.bfloat16)


def conv(kernel, blocks, in_width, lined, mine, other, width, padded, out_shape, staging=(), out_space=VMEM, room=40):
    orients = 2 * blocks.shape[0]
    return call(
        functools.partial(kernel, orients, width),
        jax.ShapeDtypeStruct(out_shape, jnp.bfloat16),
        [
            pltpu.VMEM((in_width, orients, WIDE), jnp.float32),
            pltpu.VMEM((in_width, orients, WIDE), jnp.float32),
            pltpu.VMEM((2, 3, WIDE, WIDE), jnp.bfloat16),
            pltpu.VMEM((orients // 2, lined, 2 * ROWS, CHAN), jnp.float32),
            pltpu.VMEM((padded, orients, WIDE), jnp.float32),
            *staging,
        ],
        2 * 6 * width * orients * WIDE * WIDE,
        blocks,
        mine,
        other,
        out_space=out_space,
        room=room,
    )


def filter_kernel(
    orients, width, field, first, own, grad_ref, feat_ref, *refs
):
    (out_ref, *rows_ref), (feat_rows, grad_rows, stage, held, done) = refs[:-5], refs[-5:]
    chip, core = here()
    slot = core if own else 1 - core
    in_width = grad_rows.shape[0]
    copies = [
        pltpu.make_async_copy(
            feat_ref.at[:, pl.ds(field * width, width), pl.ds(half * WIDE, WIDE)],
            held.at[:, half],
            done.at[half],
        )
        for half in range(2)
    ]
    for copy in copies:
        copy.start()
    if own:
        grads = grad_ref[...]
    else:
        interleave(grad_ref, grad_rows, stage)
        grads = grad_rows[...].reshape(in_width * orients, WIDE).astype(jnp.bfloat16)
        rows_ref[0][...] = grads
    for copy in copies:
        copy.wait()
    for g in range(orients):
        s = lax.rem(g + 2 * chip + slot, orients)
        feat_rows[:, g, :] = held[s // 2, lax.rem(s, 2)].astype(jnp.float32)
    feats = feat_rows[...].reshape(width * orients, WIDE).astype(jnp.bfloat16)
    for j in range(3):
        window = grads[(first - j) * orients : (first - j + width) * orients]
        product = lax.dot_general(
            feats,
            window,
            (((0,), (0,)), ((), ())),
            preferred_element_type=jnp.float32,
        )
        for i in range(3):
            total = None
            for row in range(ROWS):
                grad_row = row - i + 1
                if not 0 <= grad_row < ROWS:
                    continue
                piece = product[
                    row * CHAN : (row + 1) * CHAN, grad_row * CHAN : (grad_row + 1) * CHAN
                ]
                total = piece if total is None else total + piece
            out_ref[i, j] = total.astype(jnp.bfloat16)


def filter_terms(feats, field, width, grads, in_width, first):
    orients = 2 * feats.shape[0]

    def terms(own, grads):
        bank = jax.ShapeDtypeStruct((3, 3, CHAN, CHAN), jnp.bfloat16)
        rows = jax.ShapeDtypeStruct((in_width * orients, WIDE), jnp.bfloat16)
        return call(
            functools.partial(filter_kernel, orients, width, field, first, own),
            bank if own else (bank, rows),
            [
                pltpu.VMEM((width, orients, WIDE), jnp.float32),
                pltpu.VMEM((in_width, orients, WIDE), jnp.float32),
                pltpu.VMEM((orients // 2, in_width, 2 * ROWS, CHAN), jnp.float32),
                pltpu.VMEM((orients // 2, 2, width, WIDE), jnp.bfloat16),
                pltpu.SemaphoreType.DMA((2,)),
            ],
            6 * width * orients * WIDE * WIDE,
            grads,
            feats,
            space=(VMEM, HBM),
            room=52,
        )

    other, rows = terms(False, grads)
    return terms(True, rows), lax.ppermute(other, CORE, SWAP)


def point_kernel(parts_ref, pre_ref, out_ref, held, done):
    total = parts_ref[0].astype(jnp.float32)
    for n in range(1, parts_ref.shape[0]):
        total = total + parts_ref[n].astype(jnp.float32)
    held[...] = (total * slope(pre_ref[...].astype(jnp.float32))).astype(jnp.bfloat16)
    copy_all([(held, out_ref.at[n]) for n in range(out_ref.shape[0])], done)


def exchange(parts, axes):
    return lax.all_to_all(parts, axes, 0, 0, tiled=True)


def chunks(pair):
    count = lax.axis_size(AZ)
    return [bank.reshape(count, -1, CHAN) for bank in pair]


def after(array, first):
    return lax.optimization_barrier((array, first))[0]


def halves_kernel(mine, theirs, stay_ref, leave_ref, both_ref):
    half = stay_ref.shape[0]
    side = lax.axis_index(AZ) // half
    both_ref[...] = mine[...].astype(jnp.float32) + theirs[...].astype(jnp.float32)
    stay_ref[...] = both_ref[pl.ds(side * half, half)].astype(jnp.bfloat16)
    leave_ref[...] = both_ref[pl.ds((1 - side) * half, half)].astype(jnp.bfloat16)


def deal_kernel(stay, came, out_ref):
    both = stay[...].astype(jnp.float32) + came[...].astype(jnp.float32)
    lines = both.reshape(-1, CHAN)
    count, size, _ = out_ref.shape
    for n in range(count):
        out_ref[n] = lines[n * size : (n + 1) * size].astype(jnp.bfloat16)


def half_terms(pair):
    mine, theirs = chunks(pair)
    count, size, _ = mine.shape
    half = jax.ShapeDtypeStruct((count // 2, size, CHAN), jnp.bfloat16)
    both = pltpu.VMEM(mine.shape, jnp.float32)
    stay, leave = call(halves_kernel, (half, half), [both], mine.size, mine, theirs)
    came = lax.ppermute(leave, AZ, [(i, (i + count // 2) % count) for i in range(count)])
    shape = jax.ShapeDtypeStruct((count, size // 2, CHAN), jnp.bfloat16)
    return call(deal_kernel, shape, [], mine.size, stay, came)


def join_kernel(mine, theirs, also, out_ref, held, done):
    size = mine.shape[1]
    both = mine[...].astype(jnp.float32) + theirs[...].astype(jnp.float32)
    held[:, :size] = both.astype(jnp.bfloat16)
    held[:, size:] = also[...]
    copy_all([(held, out_ref)], done)


def joined_terms(pair, also):
    mine, theirs = chunks(pair)
    count, size, _ = mine.shape
    shape = jax.ShapeDtypeStruct((count, size + also.shape[1], CHAN), jnp.bfloat16)
    held = [pltpu.VMEM(shape.shape, jnp.bfloat16), pltpu.SemaphoreType.DMA((1,))]
    return call(join_kernel, shape, held, mine.size, mine, theirs, also, out_space=HBM)


def reduce_kernel(size, parts_ref, out_ref, held, done):
    count = parts_ref.shape[0]
    total = [parts_ref[n].astype(jnp.float32) for n in (0, count // 2)]
    for n in range(1, count // 2):
        total[0] = total[0] + parts_ref[n].astype(jnp.float32)
        total[1] = total[1] + parts_ref[count // 2 + n].astype(jnp.float32)
    whole = [total[0][:size] + total[1][:size], total[0][size:], total[1][size:]]
    held[...] = jnp.concatenate(whole).astype(jnp.bfloat16)
    copy_all([(held, out_ref.at[n]) for n in range(count)], done)


def finish_kernel(size, scale, whole_ref, one_ref, two_ref, held_one, held_two, done):
    count = whole_ref.shape[0]
    dealt = (whole_ref.shape[1] - size) // 2
    held_one[...] = whole_ref[:, :size].astype(jnp.float32) * scale
    first = pltpu.make_async_copy(held_one, one_ref, done.at[0])
    first.start()
    for side in range(2):
        for n in range(count):
            part = whole_ref[n, size:].astype(jnp.float32) * scale
            held_two[side, n * dealt : (n + 1) * dealt] = part[side * dealt : (side + 1) * dealt]
    second = pltpu.make_async_copy(held_two, two_ref, done.at[1])
    second.start()
    first.wait()
    second.wait()


def summed_over_az(joined, size, scale):
    count, both, _ = joined.shape
    dealt = both - size
    held = [pltpu.VMEM((size + 2 * dealt, CHAN), jnp.bfloat16), pltpu.SemaphoreType.DMA((count,))]
    shape = jax.ShapeDtypeStruct((count, size + 2 * dealt, CHAN), jnp.bfloat16)
    copies = call(
        functools.partial(reduce_kernel, size),
        shape,
        held,
        joined.size,
        exchange(joined, AZ),
        out_space=HBM,
    )
    one = (count, size, CHAN)
    two = (2, count * size // 2, CHAN)
    banks = call(
        functools.partial(finish_kernel, size, scale),
        (jax.ShapeDtypeStruct(one, jnp.float32), jax.ShapeDtypeStruct(two, jnp.float32)),
        [
            pltpu.VMEM(one, jnp.float32),
            pltpu.VMEM(two, jnp.float32),
            pltpu.SemaphoreType.DMA((2,)),
        ],
        joined.size,
        exchange(copies, AZ),
        out_space=HBM,
        room=52,
    )
    return tuple(bank.reshape(1, 3, 3, CHAN, CHAN) for bank in banks)


def stacked(act, given, grad, pre, side):
    half = act.shape[0] // 2
    zeros = jnp.zeros((8, CHAN), jnp.float32)
    if side == 0:
        grad = [zeros[:2], grad[: half + 2], zeros[:4]]
        pre = [zeros[:1], pre[: half + 1], zeros[:6]]
    else:
        grad = [grad[half - 2 :], zeros[:6]]
        pre = [pre[half - 1 :], zeros[:7]]
    own = slice(side * half, (side + 1) * half)
    return jnp.concatenate([act[own], given[own], *grad, *pre])


def lanes_kernel(*refs):
    given, (mine_ref, away_ref, same_ref, cross_ref) = refs[:4], refs[4:8]
    held, done = refs[8:12], refs[12]
    _, core = here()
    copy_all(zip(given, held), done)
    inputs_ref, pre_one_ref, pre_two_ref, cotangent_ref = held
    for row in range(ROWS):
        lanes = slice(row * CHAN, (row + 1) * CHAN)
        pre = pre_one_ref[0, row].astype(jnp.float32)
        grad = cotangent_ref[0, row].astype(jnp.float32) * slope(
            pre_two_ref[0, row].astype(jnp.float32)
        )
        act = pre / (1.0 + jnp.exp(-pre))
        fields = (act, inputs_ref[0, row].astype(jnp.float32), grad, pre)
        left, right = stacked(*fields, 0), stacked(*fields, 1)
        mine_ref[:, lanes] = jnp.where(core == 0, left, right).astype(jnp.bfloat16)
        away_ref[:, lanes] = jnp.where(core == 0, right, left).astype(jnp.bfloat16)
        pad = jnp.zeros((5, CHAN), jnp.float32)
        low = jnp.concatenate([grad[:2], pre[:1], pad])
        high = jnp.concatenate([grad[-2:], pre[-1:], pad])
        same_ref[:, lanes] = jnp.where(core == 0, high, low).astype(jnp.bfloat16)
        cross_ref[:, lanes] = jnp.where(core == 0, low, high).astype(jnp.bfloat16)


def rims_kernel(mine_ref, partner_ref, same_ref, cross_ref, out_ref, pre_ref, held, stage, done):
    _, core = here()
    rows = mine_ref.shape[0] - held.shape[0]
    ahead = held.shape[0] - rows
    used = rows - 8
    at = lax.broadcasted_iota(jnp.int32, (rows, WIDE), 0)
    grad_at = jnp.where(core == 0, 0, used + 2)
    pre_at = jnp.where(core == 0, 0, used + 1)
    filled = []
    for body_ref, edge_ref in ((mine_ref, same_ref), (partner_ref, cross_ref)):
        body = body_ref[...].astype(jnp.float32)
        edge = edge_ref[...].astype(jnp.float32)
        grad = body[ahead : ahead + rows]
        grad = jnp.where(at == grad_at, edge[0:1], grad)
        grad = jnp.where(at == grad_at + 1, edge[1:2], grad)
        pre = jnp.where(at == pre_at, edge[2:3], body[ahead + rows :])
        filled.append(jnp.concatenate([body[:ahead], grad, pre]).astype(jnp.bfloat16))
    first = jnp.where(core == 0, filled[0], filled[1])
    second = jnp.where(core == 0, filled[1], filled[0])
    for half, part in enumerate((first, second)):
        held[:, half * WIDE : (half + 1) * WIDE] = part[: ahead + rows]
        pre = part[ahead + rows :].astype(jnp.float32)[: stage.shape[0]]
        for row in range(ROWS):
            stage[:, half * ROWS + row, :] = pre[:, lanes_of(row)]
    pre_ref[...] = stage[...].reshape(pre_ref.shape).astype(jnp.bfloat16)
    copy_all([(held, out_ref.at[n]) for n in range(out_ref.shape[0])], done)


def shards(inputs, pre_one, pre_two, cotangent, filt_one, filt_two):
    columns = inputs.shape[2]
    half = columns // 2
    core = lax.axis_index(CORE)
    az_count = lax.axis_size(AZ)
    rot_count = lax.axis_size(ROT)
    chips = lax.axis_size(CHIPS)
    cell_count = rot_count * inputs.shape[1] * columns * az_count
    scale = cell_count ** (-0.5)
    padded = half + 8
    lined = half + 2

    def narrow(*shape):
        return jax.ShapeDtypeStruct(shape, jnp.bfloat16)

    rows = columns + 2 * padded
    mine, away, same, cross = call(
        lanes_kernel,
        (narrow(rows, WIDE), narrow(rows, WIDE), narrow(8, WIDE), narrow(8, WIDE)),
        [pltpu.VMEM(inputs.shape, jnp.bfloat16)] * 4 + [pltpu.SemaphoreType.DMA((4,))],
        inputs.size * 20,
        inputs,
        pre_one,
        pre_two,
        cotangent,
        space=HBM,
        room=60,
    )
    after_me = [(i, (i + 1) % az_count) for i in range(az_count)]
    before_me = [(i, (i - 1) % az_count) for i in range(az_count)]
    place = lambda c, pairs, d: [(c * az_count + i, d * az_count + j) for i, j in pairs]
    same = lax.ppermute(same, (CORE, AZ), place(0, after_me, 0) + place(1, before_me, 1))
    cross = lax.ppermute(cross, (CORE, AZ), place(1, after_me, 0) + place(0, before_me, 1))
    partner = lax.ppermute(away, CORE, SWAP)
    mine = mine + lax.shift_right_logical(core, 1).astype(mine.dtype)
    sent, pre_pair = call(
        rims_kernel,
        (narrow(chips, columns + padded, 2 * WIDE), narrow(lined * 2 * ROWS, CHAN)),
        [
            pltpu.VMEM((columns + padded, 2 * WIDE), jnp.bfloat16),
            pltpu.VMEM((lined, 2 * ROWS, CHAN), jnp.float32),
            pltpu.SemaphoreType.DMA((chips,)),
        ],
        inputs.size * 20,
        mine,
        partner,
        same,
        cross,
        out_space=(HBM, VMEM),
    )
    other_two = lax.ppermute(filt_two[0], CORE, SWAP)
    first_blocks = exchange(after(sent, other_two), CHIPS)

    shares = conv(
        conv_two_kernel,
        first_blocks,
        padded,
        lined,
        filt_two[0],
        other_two,
        lined,
        lined,
        (chips, lined * 2 * ROWS, CHAN),
        [
            pltpu.VMEM((chips, lined * 2 * ROWS, CHAN), jnp.bfloat16),
            pltpu.SemaphoreType.DMA((chips,)),
        ],
        HBM,
        52,
    )
    late_blocks = after(first_blocks, shares)
    pair_two = filter_terms(late_blocks, 0, half, late_blocks, padded, 3)
    terms_two = half_terms(pair_two)
    arrived = after(exchange(shares, CHIPS), pair_two[0])
    copies = call(
        point_kernel,
        narrow(chips, *pre_pair.shape),
        [pltpu.VMEM(pre_pair.shape, jnp.bfloat16), pltpu.SemaphoreType.DMA((chips,))],
        arrived.size,
        arrived,
        pre_pair,
        out_space=HBM,
    )
    all_grad_one = after(exchange(copies, CHIPS), terms_two)
    joined = joined_terms(filter_terms(first_blocks, 1, half, all_grad_one, lined, 2), terms_two)
    filt_grad_one, filt_grad_two = summed_over_az(joined, filt_one.size // CHAN // az_count, scale)

    along_x = lax.axis_size(CHIPS[0])

    other_one = lax.ppermute(after(filt_one[0], joined), CORE, SWAP)

    shares = conv(
        conv_one_kernel,
        after(all_grad_one, joined),
        lined,
        lined,
        filt_one[0],
        other_one,
        half,
        half,
        (2, along_x, half, 2 * WIDE),
    )
    arrived_y = lax.ppermute(shares[1], CHIPS[1], SWAP)
    partial = (shares[0].astype(jnp.float32) + arrived_y.astype(jnp.float32)).astype(jnp.bfloat16)
    total = partial[0].astype(jnp.float32)
    for step in range(1, along_x):
        came = lax.ppermute(
            partial[step], CHIPS[0], [(i, (i + step) % along_x) for i in range(along_x)]
        )
        total = total + came.astype(jnp.float32)
    total = total.astype(jnp.bfloat16)
    left, right = total[:, :WIDE], total[:, WIDE:]
    mine = jnp.where(core == 0, left, right)
    theirs = lax.ppermute(jnp.where(core == 0, right, left), CORE, SWAP)
    whole = jnp.where(core == 0, jnp.concatenate([mine, theirs]), jnp.concatenate([theirs, mine]))
    input_grad = jnp.moveaxis(whole.reshape(columns, ROWS, CHAN), 1, 0)[None]
    return input_grad, filt_grad_one, filt_grad_two


def solution(mesh):
    finer = Mesh(mesh.devices.reshape(4, 2, 2, mesh.shape["az"]), (*ROT, AZ))
    field = P(ROT, None, AZ, None)
    bank = P(ROT, None, None, None, None)
    return jax.shard_map(
        shards,
        mesh=finer,
        in_specs=(field, field, field, field, bank, bank),
        out_specs=(field, bank, bank),
        check_vma=False,
    )
```
